256 devices in a mesh: wide: 64 (over y, z, x_hi), narrow: 4 (over x_lo, core).
Axes of the slice: x: 4 (x_hi: 2, x_lo: 2; x = x_hi * 2 + x_lo), y: 4, z: 8, core: 2. Of those that a mesh axis runs over, the one named last changes fastest.
Arguments:
- prior_lt: float32 [4096, 49152], P('narrow', 'wide'), may hold values from -2 to 2
- prior_d: float32 [4096], P('narrow'), may hold values from -4 to 4
- prior_e: float32 [4096], P('narrow'), may hold values from -4 to 4
- prior_pairs: int32 [4096], P('narrow'), may hold values from 0 to 1, as said below
- pivots: int32 [2, 256], replicated, may hold values from 0 to 49151, as said below
- a_first: float32 [256, 49152], P('narrow', 'wide'), may hold values from -6 to 6
- a_second: float32 [256, 49152], P('narrow', 'wide'), may hold values from -6 to 6
- inv_d: float32 [2, 256], P(None, 'narrow'), may hold values from -4 to 4
- inv_e: float32 [2, 256], P(None, 'narrow'), may hold values from -4 to 4
- panel_pairs: int32 [2, 256], P(None, 'narrow'), may hold values from 0 to 1, as said below
Outputs:
- l_first: float32 [256, 49152], P('narrow', 'wide')
- l_second: float32 [256, 49152], P('narrow', 'wide')
The draws below stay inside these ranges and needn't reach their ends.
Inputs may be any that keep to these rules, and one draw needn't show every extreme that they name: `pivots`: all 512 pivot rows are distinct; at most 16 of them lie in one tile of 768 consecutive rows, and some tile holds exactly 16. `prior_pairs`: 1 only at even positions; a 1 at position k joins k and k + 1 into a 2 x 2 pivot block. `panel_pairs`: 1 only at even positions along the last dimension; a 1 at position k joins k and k + 1 into a 2 x 2 pivot block.
All inputs are finite; a program needn't handle non-finite values.
Results may differ from the reference program's by a relative error of at most 0.000098.
Values sent between devices are 32-bit elements; how exact they have to be, the bound alone decides.
No kernel may reach another device: no remote copies, remote signals or barrier semaphores. Data moves between devices by JAX's collectives and lax.ppermute only.
A program may use at most 64 MiB of HBM per device.

```python
import jax
import jax.numpy as jnp
from jax import lax

ROWS = 768
K = 4096
P_SIZE = 256
N = 49152
CAP = 16
N_WIDE = 64


def draw_pivots(key, part):
    key_order = jax.random.fold_in(key, 11)
    key_full = jax.random.fold_in(key, 12)
    key_rows = jax.random.fold_in(key, 13)
    key_mix = jax.random.fold_in(key, 14)
    total_slots = N_WIDE * CAP
    order = jax.random.permutation(key_order, total_slots)
    full_tile = jax.random.randint(key_full, (), 0, N_WIDE)
    owner = order // CAP
    score = jnp.where(owner == full_tile, 0, total_slots) + jnp.arange(total_slots)
    picked = order[jnp.argsort(score)[:2 * P_SIZE]]
    tile = picked // CAP
    within = picked % CAP
    row_order = jax.random.permutation(key_rows, ROWS)
    offset = (row_order[within] + tile * 7) % ROWS
    rows_all = tile * ROWS + offset
    rows_all = jax.random.permutation(key_mix, rows_all)
    return rows_all.reshape(2, P_SIZE).astype(jnp.int32)


def draw_prior_pairs(key, part):
    bits = jax.random.randint(jax.random.fold_in(key, 21), (K // 2,), 0, 2)
    return jnp.stack([bits, jnp.zeros_like(bits)], 1).reshape(K).astype(jnp.int32)


def draw_panel_pairs(key, part):
    bits = jax.random.randint(jax.random.fold_in(key, 31), (2, P_SIZE // 2), 0, 2)
    return jnp.stack([bits, jnp.zeros_like(bits)], 2).reshape(2, P_SIZE).astype(jnp.int32)


def shard_levels(rng, extent, cuts, smallest, high):
    factor_of = 1.0
    for dim, shards_of in cuts:
        heights = jax.random.uniform(jax.random.fold_in(jax.random.fold_in(rng, 6), dim), (shards_of,), jnp.float32, smallest / len(cuts), high / len(cuts))
        factor_of = factor_of * jnp.repeat(jnp.exp(heights), extent[dim] // shards_of).reshape((-1,) + (1,) * (len(extent) - 1 - dim))
    return factor_of


def noise(rng, extent, deviation, most, split=(), kind=jnp.bfloat16):
    entries = jax.random.normal(rng, extent, jnp.float32) * deviation
    if len(split) > 0:
        entries = shard_levels(rng, extent, split, -0.22, 0.18) * entries
    return jnp.clip(entries, min=-most, max=most).astype(kind)


def setup_inputs(seed: int = 0) -> dict:
    arg_keys = jax.random.split(jax.random.key(seed), 11)
    return {
        "prior_lt": noise(arg_keys[0], (K, N), (1.0 / K ** 0.25), 2.0, ((0, 4), (1, 64)), jnp.float32),
        "prior_d": noise(arg_keys[1], (K,), 1.0, 4.0, ((0, 4),), jnp.float32),
        "prior_e": noise(arg_keys[2], (K,), 0.5, 4.0, ((0, 4),), jnp.float32),
        "prior_pairs": draw_prior_pairs(jax.random.fold_in(arg_keys[10], 71), 0),
        "pivots": draw_pivots(jax.random.fold_in(arg_keys[10], 71), 0),
        "a_first": noise(arg_keys[5], (P_SIZE, N), 1.0, 6.0, ((0, 4), (1, 64)), jnp.float32),
        "a_second": noise(arg_keys[6], (P_SIZE, N), 1.0, 6.0, ((0, 4), (1, 64)), jnp.float32),
        "inv_d": noise(arg_keys[7], (2, P_SIZE), 0.3, 4.0, ((1, 4),), jnp.float32),
        "inv_e": noise(arg_keys[8], (2, P_SIZE), 0.3, 4.0, ((1, 4),), jnp.float32),
        "panel_pairs": draw_panel_pairs(jax.random.fold_in(arg_keys[10], 71), 0),
    }


def couple(block, diag, off, pairs):
    joined = off * pairs.astype(jnp.float32)
    zero_row = jnp.zeros_like(block[:1])
    after = jnp.concatenate([block[1:], zero_row], 0)
    before = jnp.concatenate([zero_row, block[:-1]], 0)
    lower = jnp.concatenate([jnp.zeros_like(joined[:1]), joined[:-1]], 0)
    return diag[:, None] * block + joined[:, None] * after + lower[:, None] * before


def reference(prior_lt, prior_d, prior_e, prior_pairs, pivots, a_first, a_second, inv_d, inv_e, panel_pairs):
    flat = pivots.reshape(-1)
    chosen = jnp.take(prior_lt, flat, axis=1)
    coupled = couple(chosen, prior_d, prior_e, prior_pairs)
    update = lax.dot_general(coupled, prior_lt, (((0,), (0,)), ((), ())), precision=lax.Precision.HIGHEST)
    width = a_first.shape[0]
    w_first = a_first - update[:width]
    l_first = couple(w_first, inv_d[0], inv_e[0], panel_pairs[0])
    crossed = jnp.take(l_first, pivots[1], axis=1)
    correction = lax.dot_general(crossed, w_first, (((0,), (0,)), ((), ())), precision=lax.Precision.HIGHEST)
    w_second = a_second - update[width:] - correction
    l_second = couple(w_second, inv_d[1], inv_e[1], panel_pairs[1])
    return l_first, l_second
```

```python
import jax
import jax.numpy as jnp
from jax import lax
from jax.sharding import PartitionSpec as P

P_SIZE = 256
CAP = 16
NY, NZ, NH = 4, 8, 2
CORE = [(0, 1), (1, 0), (2, 3), (3, 2)]
CHIP = [(0, 2), (1, 3), (2, 0), (3, 1)]
HIGH = lax.Precision.HIGH
EXACT = lax.Precision.HIGHEST


def couple(block, diag, off, pairs):
    joined = off * pairs.astype(jnp.float32)
    zero_row = jnp.zeros_like(block[:1])
    after = jnp.concatenate([block[1:], zero_row], 0)
    before = jnp.concatenate([zero_row, block[:-1]], 0)
    lower = jnp.concatenate([jnp.zeros_like(joined[:1]), joined[:-1]], 0)
    return diag[:, None] * block + joined[:, None] * after + lower[:, None] * before


def couple_lanes(block, diag, off, pairs):
    joined = off * pairs.astype(jnp.float32)
    zero = jnp.zeros_like(block[:, :1])
    after = jnp.concatenate([block[:, 1:], zero], 1)
    before = jnp.concatenate([zero, block[:, :-1]], 1)
    lower = jnp.concatenate([jnp.zeros_like(joined[:1]), joined[:-1]], 0)
    return diag[None, :] * block + joined[None, :] * after + lower[None, :] * before


def shift(dy, dz, dh):
    pairs = []
    for y in range(NY):
        for z in range(NZ):
            for h in range(NH):
                to = ((y + dy) % NY * NZ + (z + dz) % NZ) * NH + (h + dh) % NH
                pairs.append(((y * NZ + z) * NH + h, to))
    return pairs


def moved(block, offsets, step):
    got = lax.ppermute(block, "wide", shift(*step))
    return got, [
        ((y - step[0]) % NY, (z - step[1]) % NZ, (h - step[2]) % NH) for y, z, h in offsets
    ]


def gather_tiles(block):
    held, at = block, [(0, 0, 0)]
    for step in ((0, 0, 1), (0, 4, 0)):
        got, its = moved(held, at, step)
        held, at = jnp.concatenate([held, got], 0), at + its
    parts = [moved(held, at, step) for step in ((2, 1, 0), (2, -1, 0), (0, 2, 0))]
    held = jnp.concatenate([held] + [p[0] for p in parts], 0)
    at = at + parts[0][1] + parts[1][1] + parts[2][1]
    half = len(at) // 2
    cut = half * block.shape[0]
    last = [moved(held, at, step) for step in ((1, 0, 0), (-1, 0, 0))]
    up, up_at = moved(held[:cut], at[:half], (0, 1, 0))
    have = set(at) | {o for p in last for o in p[1]} | set(up_at)
    low = [(y, (z + 1) % NZ, h) for y, z, h in at]
    keep = [i for i, o in enumerate(low) if o not in have]
    if keep == list(range(half)):
        down, down_at = moved(held[:cut], at[:half], (0, -1, 0))
    else:
        down, down_at = moved(held[cut:], at[half:], (0, -1, 0))
    arrays = [held] + [p[0] for p in last] + [up, down]
    offsets = at + last[0][1] + last[1][1] + up_at + down_at
    return arrays, offsets


def scatter_sum(block):
    me = lax.axis_index("narrow")
    core, chip = me % 2, me // 2
    rows = block.shape[0] // 4
    block = block.reshape(2, 2, rows, block.shape[1])
    mine = jnp.where(core == 0, block[:, 0], block[:, 1])
    other = jnp.where(core == 0, block[:, 1], block[:, 0])
    block = mine + lax.ppermute(other, "narrow", CORE)
    mine = jnp.where(chip == 0, block[0], block[1])
    other = jnp.where(chip == 0, block[1], block[0])
    return mine + lax.ppermute(other, "narrow", CHIP)


def shards(
    prior_lt, prior_d, prior_e, prior_pairs, pivots, a_first, a_second, inv_d, inv_e, panel_pairs
):
    k_local, tile_rows = prior_lt.shape
    blocks = a_first.shape[0]
    here = lax.axis_index("wide")
    flat = pivots.reshape(-1)
    tile = flat // tile_rows
    within = flat % tile_rows
    count = flat.shape[0]
    order = jnp.arange(count)
    rank = jnp.sum((tile[:, None] == tile[None, :]) & (order[None, :] < order[:, None]), 1)
    slot_hit = (rank[None, :] == jnp.arange(CAP)[:, None]) & (tile == here)[None, :]
    column = jnp.sum(jnp.where(slot_hit, within[None, :] + 1, 0), 1) - 1
    pick = (column[:, None] == jnp.arange(tile_rows)[None, :]).astype(jnp.float32)
    dims = (((1,), (1,)), ((), ()))
    slots_l = lax.dot_general(pick, prior_lt, dims, precision=EXACT)
    slots_a = lax.dot_general(pick, a_first, dims, precision=EXACT)
    block = jnp.concatenate([slots_l, jnp.pad(slots_a, ((0, 0), (0, 64)))], 1)
    arrays, offsets = gather_tiles(block)
    ty, tz, th = tile // (NZ * NH), tile // NH % NZ, tile % NH
    hy, hz, hh = here // (NZ * NH), here // NH % NZ, here % NH
    rel = ((ty - hy) % NY * NZ + (tz - hz) % NZ) * NH + (th - hh) % NH
    place_of = [0] * (NY * NZ * NH)
    for i, (y, z, h) in enumerate(offsets):
        place_of[(y * NZ + z) * NH + h] = i
    place = jnp.sum(
        jnp.where(rel[:, None] == jnp.arange(NY * NZ * NH)[None, :], jnp.array(place_of)[None, :], 0), 1
    )
    chosen = jnp.take(jnp.concatenate(arrays, 0), place * CAP + rank, axis=0, mode="clip")
    coupled_lt = couple(prior_lt, prior_d, prior_e, prior_pairs)
    first, second = chosen[:P_SIZE, :k_local], chosen[P_SIZE:, :k_local]
    plain = (((1,), (0,)), ((), ()))
    update_first = lax.dot_general(first, coupled_lt, plain, precision=HIGH)
    update_second = lax.dot_general(second, coupled_lt, plain, precision=HIGH)
    coupled_second = couple_lanes(second, prior_d, prior_e, prior_pairs)
    inner = lax.dot_general(first, coupled_second, dims, precision=HIGH)
    summed = scatter_sum(jnp.concatenate([update_first, inner], 1))
    a_crossed = chosen[P_SIZE:, k_local : k_local + blocks].T
    w_first = a_first - summed[:, :tile_rows]
    l_first = couple(w_first, inv_d[0], inv_e[0], panel_pairs[0])
    crossed = couple(a_crossed - summed[:, tile_rows:], inv_d[0], inv_e[0], panel_pairs[0])
    correction = lax.dot_general(crossed, w_first, (((0,), (0,)), ((), ())), precision=HIGH)
    w_second = a_second - scatter_sum(update_second + correction)
    l_second = couple(w_second, inv_d[1], inv_e[1], panel_pairs[1])
    return (l_first, l_second)


def solution(mesh):
    in_specs = (
        P("narrow", "wide"),
        P("narrow"),
        P("narrow"),
        P("narrow"),
        P(),
        P("narrow", "wide"),
        P("narrow", "wide"),
        P(None, "narrow"),
        P(None, "narrow"),
        P(None, "narrow"),
    )
    out_specs = (P("narrow", "wide"), P("narrow", "wide"))
    return jax.shard_map(shards, mesh=mesh, in_specs=in_specs, out_specs=out_specs, check_vma=False)
```

```python
import functools

import jax
import jax.numpy as jnp
from jax import lax
from jax.experimental import pallas as pl
from jax.experimental.pallas import tpu as pltpu
from jax.sharding import PartitionSpec as P

P_SIZE = 256
CAP = 16
NY, NZ, NH = 4, 8, 2
CORE = [(0, 1), (1, 0), (2, 3), (3, 2)]
CHIP = [(0, 2), (1, 3), (2, 0), (3, 1)]
HIGH = lax.Precision.HIGH
EXACT = lax.Precision.HIGHEST


def couple(block, diag, off, pairs):
    joined = off * pairs.astype(jnp.float32)
    zero_row = jnp.zeros_like(block[:1])
    after = jnp.concatenate([block[1:], zero_row], 0)
    before = jnp.concatenate([zero_row, block[:-1]], 0)
    lower = jnp.concatenate([jnp.zeros_like(joined[:1]), joined[:-1]], 0)
    return diag[:, None] * block + joined[:, None] * after + lower[:, None] * before


def couple_lanes(block, diag, off, pairs):
    joined = off * pairs.astype(jnp.float32)
    zero = jnp.zeros_like(block[:, :1])
    after = jnp.concatenate([block[:, 1:], zero], 1)
    before = jnp.concatenate([zero, block[:, :-1]], 1)
    lower = jnp.concatenate([jnp.zeros_like(joined[:1]), joined[:-1]], 0)
    return diag[None, :] * block + joined[None, :] * after + lower[None, :] * before


def shift(dy, dz, dh):
    pairs = []
    for y in range(NY):
        for z in range(NZ):
            for h in range(NH):
                to = ((y + dy) % NY * NZ + (z + dz) % NZ) * NH + (h + dh) % NH
                pairs.append(((y * NZ + z) * NH + h, to))
    return pairs


def moved(block, offsets, step):
    got = lax.ppermute(block, "wide", shift(*step))
    return got, [
        ((y - step[0]) % NY, (z - step[1]) % NZ, (h - step[2]) % NH) for y, z, h in offsets
    ]


def gather_tiles(block):
    rows = block.shape[0]
    held, at = block, [(0, 0, 0)]
    got, its = moved(held, at, (0, 4, 0))
    held, at = jnp.concatenate([held, got], 0), at + its
    parts = [moved(held, at, step) for step in ((2, 1, 0), (2, -1, 0), (0, 2, 0))]
    held = jnp.concatenate([held] + [p[0] for p in parts], 0)
    at = at + parts[0][1] + parts[1][1] + parts[2][1]
    half = len(at) // 2
    over = moved(held, at, (0, 0, 1))
    ahead = moved(held, at, (1, 0, 0))
    behind = moved(held, at, (-1, 0, 0))
    up = moved(held[: half * rows], at[:half], (0, 1, 0))
    down = moved(held[: half * rows], at[:half], (0, -1, 0))
    early = [(held, at), over, ahead, behind, up, down]
    cut, cut_at = over[0][: half * rows], over[1][:half]
    late = [
        moved(ahead[0], ahead[1], (0, 0, 1)),
        moved(over[0], over[1], (-1, 0, 0)),
        moved(cut, cut_at, (0, 1, 0)),
        moved(cut, cut_at, (0, -1, 0)),
    ]
    return early, late


def pick_kernel(index_ref, *refs, base, sizes, carried):
    out_ref = refs[-1]
    pieces = refs[: len(sizes)]
    width = out_ref.shape[1]
    step = 128
    for low in range(0, width, 2 * step):
        cols = slice(low, min(low + 2 * step, width))
        total = refs[len(sizes)][:, cols] if carried else None
        start = base
        for ref, size in zip(pieces, sizes):
            slot = start + lax.broadcasted_iota(jnp.int32, (index_ref.shape[0], size), 1)
            hit = jnp.where(index_ref[...] == slot, 1.0, 0.0).astype(jnp.bfloat16)
            value = ref[:, cols]
            big = value.astype(jnp.bfloat16)
            small = (value - big.astype(jnp.float32)).astype(jnp.bfloat16)
            part = jnp.dot(hit, big, preferred_element_type=jnp.float32)
            part = part + jnp.dot(hit, small, preferred_element_type=jnp.float32)
            total = part if total is None else total + part
            start += size
        out_ref[:, cols] = total


def pick_rows(index, pieces, base, carry):
    sizes = [p.shape[0] for p in pieces]
    width = pieces[0].shape[1]
    count = index.shape[0]
    args = [index.reshape(count, 1)] + list(pieces) + ([] if carry is None else [carry])
    return pl.pallas_call(
        functools.partial(pick_kernel, base=base, sizes=sizes, carried=carry is not None),
        out_shape=jax.ShapeDtypeStruct((count, width), jnp.float32),
        compiler_params=pltpu.CompilerParams(vmem_limit_bytes=48 * 2**20),
        cost_estimate=pl.CostEstimate(
            flops=4 * count * sum(sizes) * width,
            bytes_accessed=4 * width * (sum(sizes) + 2 * count),
            transcendentals=0,
        ),
    )(*args)


def quarter_order(me):
    core, chip = me % 2, me // 2
    return [(1 - chip) * 2 + 1 - core, chip * 2 + 1 - core, (1 - chip) * 2 + core, me]


def in_quarters(rows, quarters, blocks):
    return jnp.concatenate([lax.dynamic_slice_in_dim(rows, q * blocks, blocks) for q in quarters], 0)


def finish_sum(send, keep):
    half = keep.shape[0] // 2
    got = lax.ppermute(send, "narrow", CORE)
    away = lax.ppermute(keep[:half] + got[:half], "narrow", CHIP)
    return keep[half:] + got[half:] + away


def shards(
    prior_lt, prior_d, prior_e, prior_pairs, pivots, a_first, a_second, inv_d, inv_e, panel_pairs
):
    k_local, tile_rows = prior_lt.shape
    blocks = a_first.shape[0]
    here = lax.axis_index("wide")
    flat = pivots.reshape(-1)
    tile = flat // tile_rows
    within = flat % tile_rows
    count = flat.shape[0]
    order = jnp.arange(count)
    rank = jnp.sum((tile[:, None] == tile[None, :]) & (order[None, :] < order[:, None]), 1)
    slot_hit = (rank[None, :] == jnp.arange(CAP)[:, None]) & (tile == here)[None, :]
    column = jnp.sum(jnp.where(slot_hit, within[None, :] + 1, 0), 1) - 1
    pick = (column[:, None] == jnp.arange(tile_rows)[None, :]).astype(jnp.float32)
    dims = (((1,), (1,)), ((), ()))
    slots_l = lax.dot_general(pick, prior_lt, dims, precision=EXACT)
    slots_a = lax.dot_general(pick, a_first, dims, precision=EXACT)
    block = jnp.concatenate([slots_l, jnp.pad(slots_a, ((0, 0), (0, 64)))], 1)
    early, late = gather_tiles(block)
    offsets = [o for piece in early + late for o in piece[1]]
    ty, tz, th = tile // (NZ * NH), tile // NH % NZ, tile % NH
    hy, hz, hh = here // (NZ * NH), here // NH % NZ, here % NH
    rel = ((ty - hy) % NY * NZ + (tz - hz) % NZ) * NH + (th - hh) % NH
    place_of = [0] * (NY * NZ * NH)
    for i, (y, z, h) in enumerate(offsets):
        place_of[(y * NZ + z) * NH + h] = i
    place = jnp.sum(
        jnp.where(rel[:, None] == jnp.arange(NY * NZ * NH)[None, :], jnp.array(place_of)[None, :], 0), 1
    )
    where = place * CAP + rank
    quarters = quarter_order(lax.axis_index("narrow"))
    where = jnp.concatenate([in_quarters(where[:P_SIZE], quarters, blocks), where[P_SIZE:]])
    early_rows = CAP * sum(len(piece[1]) for piece in early)
    chosen = pick_rows(where, [p[0] for p in early], 0, None)
    chosen = pick_rows(where, [p[0] for p in late], early_rows, chosen)
    coupled_lt = couple(prior_lt, prior_d, prior_e, prior_pairs)
    plain = (((1,), (0,)), ((), ()))
    second = chosen[P_SIZE:, :k_local]
    coupled_second = couple_lanes(second, prior_d, prior_e, prior_pairs)
    halves = []
    for low in (0, P_SIZE // 2):
        part = chosen[low : low + P_SIZE // 2, :k_local]
        halves.append(
            jnp.concatenate(
                [
                    lax.dot_general(part, coupled_lt, plain, precision=HIGH),
                    lax.dot_general(part, coupled_second, dims, precision=HIGH),
                ],
                1,
            )
        )
    summed = finish_sum(*halves)
    w_first = a_first - summed[:, :tile_rows]
    l_first = couple(w_first, inv_d[0], inv_e[0], panel_pairs[0])
    w_crossed = chosen[P_SIZE:, k_local : k_local + blocks] - summed[:, tile_rows:].T
    crossed = couple_lanes(w_crossed, inv_d[0], inv_e[0], panel_pairs[0])
    halves = []
    for pair in (quarters[:2], quarters[2:]):
        halves.append(
            lax.dot_general(in_quarters(second, pair, blocks), coupled_lt, plain, precision=HIGH)
            + lax.dot_general(in_quarters(crossed, pair, blocks), w_first, plain, precision=HIGH)
        )
    w_second = a_second - finish_sum(*halves)
    l_second = couple(w_second, inv_d[1], inv_e[1], panel_pairs[1])
    return (l_first, l_second)


def solution(mesh):
    in_specs = (
        P("narrow", "wide"),
        P("narrow"),
        P("narrow"),
        P("narrow"),
        P(),
        P("narrow", "wide"),
        P("narrow", "wide"),
        P(None, "narrow"),
        P(None, "narrow"),
        P(None, "narrow"),
    )
    out_specs = (P("narrow", "wide"), P("narrow", "wide"))
    return jax.shard_map(shards, mesh=mesh, in_specs=in_specs, out_specs=out_specs, check_vma=False)
```

```python
import functools

import jax
import jax.numpy as jnp
from jax import lax
from jax.experimental import pallas as pl
from jax.experimental.pallas import tpu as pltpu
from jax.sharding import PartitionSpec as P

P_SIZE = 256
CAP = 16
NY, NZ, NH = 4, 8, 2
CORE = [(0, 1), (1, 0), (2, 3), (3, 2)]
CHIP = [(0, 2), (1, 3), (2, 0), (3, 1)]
HIGH = lax.Precision.HIGH


def couple(block, diag, off, pairs):
    joined = off * pairs.astype(jnp.float32)
    zero_row = jnp.zeros_like(block[:1])
    after = jnp.concatenate([block[1:], zero_row], 0)
    before = jnp.concatenate([zero_row, block[:-1]], 0)
    lower = jnp.concatenate([jnp.zeros_like(joined[:1]), joined[:-1]], 0)
    return diag[:, None] * block + joined[:, None] * after + lower[:, None] * before


def couple_lanes(block, diag, off, pairs):
    joined = off * pairs.astype(jnp.float32)
    zero = jnp.zeros_like(block[:, :1])
    after = jnp.concatenate([block[:, 1:], zero], 1)
    before = jnp.concatenate([zero, block[:, :-1]], 1)
    lower = jnp.concatenate([jnp.zeros_like(joined[:1]), joined[:-1]], 0)
    return diag[None, :] * block + joined[None, :] * after + lower[None, :] * before


def shift(dy, dz, dh):
    pairs = []
    for y in range(NY):
        for z in range(NZ):
            for h in range(NH):
                to = ((y + dy) % NY * NZ + (z + dz) % NZ) * NH + (h + dh) % NH
                pairs.append(((y * NZ + z) * NH + h, to))
    return pairs


def moved(block, offsets, step):
    got = lax.ppermute(block, "wide", shift(*step))
    return got, [
        ((y - step[0]) % NY, (z - step[1]) % NZ, (h - step[2]) % NH) for y, z, h in offsets
    ]


def gather_tiles(block):
    rows = block.shape[0]
    held, at = block, [(0, 0, 0)]
    for step in ((0, 4, 0), (0, 2, 0), (2, 1, 0)):
        got, its = moved(held, at, step)
        held, at = jnp.concatenate([held, got], 0), at + its
    half = len(at) // 2
    cut = half * rows
    ahead = moved(held, at, (1, 0, 0))
    behind = moved(held, at, (-1, 0, 0))
    over = moved(held, at, (0, 0, 1))
    up = moved(held[:cut], at[:half], (0, 1, 0))
    down = moved(held[cut:], at[half:], (0, -1, 0))
    early = [(held, at), ahead, behind, over, up, down]
    mixed = jnp.concatenate([ahead[0][cut:], behind[0][:cut]], 0)
    late = [
        moved(mixed, ahead[1][half:] + behind[1][:half], (0, 0, 1)),
        moved(over[0][:cut], over[1][:half], (1, 0, 0)),
        moved(over[0][cut:], over[1][half:], (-1, 0, 0)),
        moved(over[0][:cut], over[1][:half], (0, 1, 0)),
        moved(over[0][cut:], over[1][half:], (0, -1, 0)),
    ]
    return early, late


def split(value):
    big = value.astype(jnp.bfloat16)
    return big, (value - big.astype(jnp.float32)).astype(jnp.bfloat16)


def dot3(left, right, dims):
    def dot(x, y):
        return lax.dot_general(x, y, (dims, ((), ())), preferred_element_type=jnp.float32)

    return dot(left[0], right[0]) + (dot(left[0], right[1]) + dot(left[1], right[0]))


def slots_kernel(low_ref, row_ref, column_ref, lt_ref, a_ref, out_ref, pick_ref):
    step = pl.program_id(0)
    width = lt_ref.shape[1]
    depth = lt_ref.shape[0]
    count = row_ref.shape[1]

    def rows_of(value):
        total = None
        for _ in range(3):
            part = value.astype(jnp.bfloat16)
            value = value - part.astype(jnp.float32)
            got = lax.dot_general(
                part, pick_ref[...], (((1,), (1,)), ((), ())), preferred_element_type=jnp.float32
            )
            total = got if total is None else total + got
        return total

    @pl.when(step == 0)
    def _():
        low = low_ref[0]
        row = row_ref[...] - low
        mine = (row >= 0) & (row < width)
        before = lax.broadcasted_iota(jnp.int32, (count, count), 0) < lax.broadcasted_iota(
            jnp.int32, (count, count), 1
        )
        ones = jnp.broadcast_to(jnp.where(mine, 1.0, 0.0), (16, count)).astype(jnp.bfloat16)
        rank = jnp.dot(ones, before.astype(jnp.float32).astype(jnp.bfloat16), preferred_element_type=jnp.float32)
        slot = lax.broadcasted_iota(jnp.int32, (128, count), 0).astype(jnp.float32)
        hit = jnp.where((slot == rank[:1]) & mine, 1.0, 0.0).astype(jnp.bfloat16)
        column = column_ref[...] - low
        there = jnp.where(
            column == lax.broadcasted_iota(jnp.int32, (count, width), 1), 1.0, 0.0
        ).astype(jnp.bfloat16)
        pick_ref[...] = jnp.dot(hit, there, preferred_element_type=jnp.float32).astype(jnp.bfloat16)
        extra = rows_of(a_ref[...]).T
        total = pl.num_programs(0) * depth
        out_ref[:, total:] = jnp.concatenate([extra[:CAP], jnp.zeros_like(extra[:CAP])], 1)

    out_ref[:, pl.ds(pl.multiple_of(step * depth, 128), depth)] = rows_of(lt_ref[...]).T[:CAP]


def tile_slots(flat, low, prior_lt, a_first):
    k_local, width = prior_lt.shape
    blocks = a_first.shape[0]
    count = flat.shape[0]
    depth = k_local // 4
    return pl.pallas_call(
        slots_kernel,
        grid=(4,),
        in_specs=[
            pl.BlockSpec(memory_space=pltpu.SMEM),
            pl.BlockSpec((1, count), lambda i: (0, 0)),
            pl.BlockSpec((count, 1), lambda i: (0, 0)),
            pl.BlockSpec((depth, width), lambda i: (i, 0)),
            pl.BlockSpec((blocks, width), lambda i: (0, 0)),
        ],
        out_specs=pl.BlockSpec((CAP, k_local + 2 * blocks), lambda i: (0, 0)),
        out_shape=jax.ShapeDtypeStruct((CAP, k_local + 2 * blocks), jnp.float32),
        scratch_shapes=[pltpu.VMEM((128, width), jnp.bfloat16)],
        compiler_params=pltpu.CompilerParams(vmem_limit_bytes=32 * 2**20),
    )(low.reshape(1), flat.reshape(1, count), flat.reshape(count, 1), prior_lt, a_first)


def fill_parts(parts_ref, pieces):
    total = parts_ref.shape[0] // 2
    start = 0
    for ref in pieces:
        size = ref.shape[0]
        big, small = split(ref[...])
        parts_ref[start : start + size, :] = big
        parts_ref[total + start : total + start + size, :] = small
        start += size


def hits(index, base, total):
    slot = base + lax.broadcasted_iota(jnp.int32, (index.shape[0], total), 1)
    hit = jnp.where(index == slot, 1.0, 0.0).astype(jnp.bfloat16)
    return jnp.concatenate([hit, hit], 1)


def early_kernel(index_ref, *refs):
    *pieces, out_ref, parts_ref = refs
    fill_parts(parts_ref, pieces)
    total = parts_ref.shape[0] // 2
    hit = hits(index_ref[...], 0, total)
    for low in range(0, out_ref.shape[1], 384):
        out_ref[:, low : low + 384] = jnp.dot(
            hit, parts_ref[:, low : low + 384], preferred_element_type=jnp.float32
        )


def send_kernel(index_ref, weight_ref, carry_ref, lt_big_ref, lt_small_ref, *refs, base):
    *pieces, out_ref, second_ref, big_ref, small_ref, parts_ref = refs
    fill_parts(parts_ref, pieces)
    total = parts_ref.shape[0] // 2
    rows, k_local = out_ref.shape[0], lt_big_ref.shape[0]
    tile_rows = lt_big_ref.shape[1]
    hit = hits(index_ref[: rows + P_SIZE], base, total)
    taken = carry_ref[: rows + P_SIZE, :] + jnp.dot(
        hit, parts_ref[...], preferred_element_type=jnp.float32
    )
    second = taken[rows:]
    second_ref[...] = second
    second = second[:, :k_local]
    after = pltpu.roll(second, k_local - 1, 1)
    before = pltpu.roll(second, 1, 1)
    coupled = split(
        weight_ref[0:1, :] * second + weight_ref[1:2, :] * after + weight_ref[2:3, :] * before
    )
    big_ref[...] = coupled[0]
    small_ref[...] = coupled[1]
    first = split(taken[:rows, :k_local])
    out_ref[:, :tile_rows] = dot3(first, (lt_big_ref[...], lt_small_ref[...]), ((1,), (0,)))
    out_ref[:, tile_rows:] = dot3(first, coupled, ((1,), (1,)))


def keep_kernel(index_ref, carry_ref, lt_big_ref, lt_small_ref, parts_ref, big_ref, small_ref, out_ref, *, base):
    total = parts_ref.shape[0] // 2
    rows, k_local = out_ref.shape[0], lt_big_ref.shape[0]
    tile_rows = lt_big_ref.shape[1]
    hit = hits(index_ref[rows + P_SIZE :], base, total)
    taken = carry_ref[rows + P_SIZE :, :k_local] + jnp.dot(
        hit, parts_ref[:, :k_local], preferred_element_type=jnp.float32
    )
    first = split(taken)
    out_ref[:, :tile_rows] = dot3(first, (lt_big_ref[...], lt_small_ref[...]), ((1,), (0,)))
    out_ref[:, tile_rows:] = dot3(first, (big_ref[...], small_ref[...]), ((1,), (1,)))


def second_kernel(quarter_ref, second_ref, lt_big_ref, lt_small_ref, out_ref):
    k_local = lt_big_ref.shape[0]
    blocks = out_ref.shape[0] // 4
    for i in range(4):
        start = pl.multiple_of(quarter_ref[i] * blocks, blocks)
        rows = split(second_ref[pl.ds(start, blocks), :k_local])
        out_ref[i * blocks : (i + 1) * blocks, :] = dot3(
            rows, (lt_big_ref[...], lt_small_ref[...]), ((1,), (0,))
        )


def local_call(kernel, out_shape, flops, *args, scratch=(), smem=0):
    specs = [pl.BlockSpec(memory_space=pltpu.SMEM)] * smem
    specs += [pl.BlockSpec(memory_space=pltpu.VMEM)] * (len(args) - smem)
    return pl.pallas_call(
        kernel,
        in_specs=specs,
        out_shape=out_shape,
        scratch_shapes=list(scratch),
        compiler_params=pltpu.CompilerParams(vmem_limit_bytes=48 * 2**20),
        cost_estimate=pl.CostEstimate(
            flops=flops, bytes_accessed=4 * sum(x.size for x in args), transcendentals=0
        ),
    )(*args)


def quarter_order(me):
    core, chip = me % 2, me // 2
    return [(1 - chip) * 2 + 1 - core, chip * 2 + 1 - core, (1 - chip) * 2 + core, me]


def in_quarters(rows, quarters, blocks):
    return jnp.concatenate([lax.dynamic_slice_in_dim(rows, q * blocks, blocks) for q in quarters], 0)


def finish_sum(send, keep):
    half = keep.shape[0] // 2
    got = lax.ppermute(send, "narrow", CORE)
    away = lax.ppermute(keep[:half] + got[:half], "narrow", CHIP)
    return keep[half:] + got[half:] + away


def shards(
    prior_lt, prior_d, prior_e, prior_pairs, pivots, a_first, a_second, inv_d, inv_e, panel_pairs
):
    k_local, tile_rows = prior_lt.shape
    blocks = a_first.shape[0]
    here = lax.axis_index("wide")
    flat = pivots.reshape(-1)
    tile = flat // tile_rows
    count = flat.shape[0]
    order = jnp.arange(count)
    rank = jnp.sum((tile[:, None] == tile[None, :]) & (order[None, :] < order[:, None]), 1)
    block = tile_slots(flat, here * tile_rows, prior_lt, a_first)
    early, late = gather_tiles(block)
    offsets = [o for piece in early + late for o in piece[1]]
    ty, tz, th = tile // (NZ * NH), tile // NH % NZ, tile % NH
    hy, hz, hh = here // (NZ * NH), here // NH % NZ, here % NH
    rel = ((ty - hy) % NY * NZ + (tz - hz) % NZ) * NH + (th - hh) % NH
    place_of = [0] * (NY * NZ * NH)
    for i, (y, z, h) in enumerate(offsets):
        place_of[(y * NZ + z) * NH + h] = i
    place = jnp.sum(
        jnp.where(rel[:, None] == jnp.arange(NY * NZ * NH)[None, :], jnp.array(place_of)[None, :], 0), 1
    )
    where = place * CAP + rank
    quarters = quarter_order(lax.axis_index("narrow"))
    ordered = in_quarters(where[:P_SIZE], quarters, blocks)
    half = P_SIZE // 2
    where = jnp.concatenate([ordered[:half], where[P_SIZE:], ordered[half:]]).reshape(-1, 1)
    early_rows = CAP * sum(len(piece[1]) for piece in early)
    late_rows = CAP * sum(len(piece[1]) for piece in late)
    width = block.shape[1]
    wide = tile_rows + P_SIZE
    f32, b16 = jnp.float32, jnp.bfloat16
    shape = jax.ShapeDtypeStruct
    coupled_lt = couple(prior_lt, prior_d, prior_e, prior_pairs)
    rounded = lax.reduce_precision(coupled_lt, exponent_bits=8, mantissa_bits=7)
    lt_big, lt_small = rounded.astype(b16), (coupled_lt - rounded).astype(b16)
    joined = prior_e * prior_pairs.astype(f32)
    weights = jnp.stack([prior_d, joined, jnp.concatenate([jnp.zeros_like(joined[:1]), joined[:-1]])])
    carry = local_call(
        early_kernel,
        shape((2 * P_SIZE, width), f32),
        4 * 2 * P_SIZE * early_rows * width,
        where,
        *[piece[0] for piece in early],
        scratch=[pltpu.VMEM((2 * early_rows, width), b16)],
    )
    send, second, second_big, second_small, parts = local_call(
        functools.partial(send_kernel, base=early_rows),
        (
            shape((half, wide), f32),
            shape((P_SIZE, width), f32),
            shape((P_SIZE, k_local), b16),
            shape((P_SIZE, k_local), b16),
            shape((2 * late_rows, width), b16),
        ),
        4 * (half + P_SIZE) * late_rows * width + 6 * half * k_local * wide,
        where,
        weights,
        carry,
        lt_big,
        lt_small,
        *[piece[0] for piece in late],
    )
    keep = local_call(
        functools.partial(keep_kernel, base=early_rows),
        shape((half, wide), f32),
        4 * half * late_rows * width + 6 * half * k_local * wide,
        where,
        carry,
        lt_big,
        lt_small,
        parts,
        second_big,
        second_small,
    )
    summed = finish_sum(send, keep)
    update_second = local_call(
        second_kernel,
        shape((P_SIZE, tile_rows), f32),
        6 * P_SIZE * k_local * tile_rows,
        jnp.stack(quarters),
        second,
        lt_big,
        lt_small,
        smem=1,
    )
    w_first = a_first - summed[:, :tile_rows]
    l_first = couple(w_first, inv_d[0], inv_e[0], panel_pairs[0])
    w_crossed = second[:, k_local : k_local + blocks] - summed[:, tile_rows:].T
    crossed = couple_lanes(w_crossed, inv_d[0], inv_e[0], panel_pairs[0])
    plain = (((1,), (0,)), ((), ()))
    halves = []
    for low in (0, 2):
        rows = in_quarters(crossed, quarters[low : low + 2], blocks)
        part = update_second[low * blocks : (low + 2) * blocks]
        halves.append(part + lax.dot_general(rows, w_first, plain, precision=HIGH))
    w_second = a_second - finish_sum(*halves)
    l_second = couple(w_second, inv_d[1], inv_e[1], panel_pairs[1])
    return (l_first, l_second)


def solution(mesh):
    in_specs = (
        P("narrow", "wide"),
        P("narrow"),
        P("narrow"),
        P("narrow"),
        P(),
        P("narrow", "wide"),
        P("narrow", "wide"),
        P(None, "narrow"),
        P(None, "narrow"),
        P(None, "narrow"),
    )
    out_specs = (P("narrow", "wide"), P("narrow", "wide"))
    return jax.shard_map(shards, mesh=mesh, in_specs=in_specs, out_specs=out_specs, check_vma=False)
```

```python
import functools

import jax
import jax.numpy as jnp
from jax import lax
from jax.experimental import pallas as pl
from jax.experimental.pallas import tpu as pltpu
from jax.sharding import PartitionSpec as P

P_SIZE = 256
CAP = 16
NY, NZ, NH = 4, 8, 2
CORE = [(0, 1), (1, 0), (2, 3), (3, 2)]
CHIP = [(0, 2), (1, 3), (2, 0), (3, 1)]
HIGH = lax.Precision.HIGH


def couple(block, diag, off, pairs):
    joined = off * pairs.astype(jnp.float32)
    zero_row = jnp.zeros_like(block[:1])
    after = jnp.concatenate([block[1:], zero_row], 0)
    before = jnp.concatenate([zero_row, block[:-1]], 0)
    lower = jnp.concatenate([jnp.zeros_like(joined[:1]), joined[:-1]], 0)
    return diag[:, None] * block + joined[:, None] * after + lower[:, None] * before


def couple_lanes(block, diag, off, pairs):
    joined = off * pairs.astype(jnp.float32)
    zero = jnp.zeros_like(block[:, :1])
    after = jnp.concatenate([block[:, 1:], zero], 1)
    before = jnp.concatenate([zero, block[:, :-1]], 1)
    lower = jnp.concatenate([jnp.zeros_like(joined[:1]), joined[:-1]], 0)
    return diag[None, :] * block + joined[None, :] * after + lower[None, :] * before


def shift(dy, dz, dh):
    pairs = []
    for y in range(NY):
        for z in range(NZ):
            for h in range(NH):
                to = ((y + dy) % NY * NZ + (z + dz) % NZ) * NH + (h + dh) % NH
                pairs.append(((y * NZ + z) * NH + h, to))
    return pairs


def moved(block, offsets, step):
    got = lax.ppermute(block, "wide", shift(*step))
    return got, [
        ((y - step[0]) % NY, (z - step[1]) % NZ, (h - step[2]) % NH) for y, z, h in offsets
    ]


def gather_tiles(block):
    rows = block.shape[0]
    held, at = block, [(0, 0, 0)]
    got, its = moved(held, at, (0, 4, 0))
    held, at = jnp.concatenate([held, got], 0), at + its
    parts = [moved(held, at, step) for step in ((2, 1, 0), (2, -1, 0), (0, 2, 0))]
    held = jnp.concatenate([held] + [p[0] for p in parts], 0)
    at = at + parts[0][1] + parts[1][1] + parts[2][1]
    half = len(at) // 2
    cut = half * rows
    ahead = moved(held, at, (1, 0, 0))
    behind = moved(held, at, (-1, 0, 0))
    over = moved(held, at, (0, 0, 1))
    up = moved(held[:cut], at[:half], (0, 1, 0))
    down = moved(held[:cut], at[:half], (0, -1, 0))
    early = [(held, at), ahead, behind, over, up, down]
    mixed = jnp.concatenate([ahead[0][cut:], behind[0][:cut]], 0)
    late = [
        moved(mixed, ahead[1][half:] + behind[1][:half], (0, 0, 1)),
        moved(over[0][:cut], over[1][:half], (1, 0, 0)),
        moved(over[0][cut:], over[1][half:], (-1, 0, 0)),
        moved(over[0][:cut], over[1][:half], (0, 1, 0)),
        moved(over[0][:cut], over[1][:half], (0, -1, 0)),
    ]
    return early, late


def split(value):
    big = value.astype(jnp.bfloat16)
    return big, (value - big.astype(jnp.float32)).astype(jnp.bfloat16)


def dot3(left, right, dims):
    def dot(x, y):
        return lax.dot_general(x, y, (dims, ((), ())), preferred_element_type=jnp.float32)

    return dot(left[0], right[0]) + (dot(left[0], right[1]) + dot(left[1], right[0]))


def slots_kernel(low_ref, pivots_ref, a_ref, lt_ref, out_ref, lt_buf, sems):
    k_local, width = lt_ref.shape
    depth = k_local // sems.shape[0]
    copies = []
    for i in range(sems.shape[0]):
        rows = slice(i * depth, (i + 1) * depth)
        copies.append(pltpu.make_async_copy(lt_ref.at[rows], lt_buf.at[rows], sems.at[i]))
        copies[-1].start()
    row = jnp.concatenate([pivots_ref[0:1, :], pivots_ref[1:2, :]], 1) - low_ref[0]
    count = row.shape[1]
    mine = (row >= 0) & (row < width)
    before = lax.broadcasted_iota(jnp.int32, (count, count), 0) < lax.broadcasted_iota(
        jnp.int32, (count, count), 1
    )
    ones = jnp.broadcast_to(jnp.where(mine, 1.0, 0.0), (16, count)).astype(jnp.bfloat16)
    rank = jnp.dot(
        ones, jnp.where(before, 1.0, 0.0).astype(jnp.bfloat16), preferred_element_type=jnp.float32
    )
    slot = lax.broadcasted_iota(jnp.int32, (128, count), 0).astype(jnp.float32)
    hit = jnp.where((slot == rank[:1]) & mine, 1.0, 0.0).astype(jnp.bfloat16)
    there = jnp.where(row == lax.broadcasted_iota(jnp.int32, (width, count), 0), 1.0, 0.0)
    across = (((1,), (1,)), ((), ()))
    pick = lax.dot_general(
        hit, there.astype(jnp.bfloat16), across, preferred_element_type=jnp.float32
    ).astype(jnp.bfloat16)

    def rows_of(value):
        total = None
        for _ in range(3):
            part = value.astype(jnp.bfloat16)
            value = value - part.astype(jnp.float32)
            got = lax.dot_general(part, pick, across, preferred_element_type=jnp.float32)
            total = got if total is None else total + got
        return total.T[:CAP]

    extra = rows_of(a_ref[...])
    out_ref[:, k_local:] = jnp.concatenate([extra, jnp.zeros_like(extra)], 1)
    for i, copy in enumerate(copies):
        copy.wait()
        rows = slice(i * depth, (i + 1) * depth)
        out_ref[:, rows] = rows_of(lt_buf[rows, :])


def tile_slots(pivots, low, prior_lt, a_first):
    k_local, width = prior_lt.shape
    blocks = a_first.shape[0]
    vmem = pl.BlockSpec(memory_space=pltpu.VMEM)
    return pl.pallas_call(
        slots_kernel,
        in_specs=[
            pl.BlockSpec(memory_space=pltpu.SMEM),
            vmem,
            vmem,
            pl.BlockSpec(memory_space=pltpu.HBM),
        ],
        out_specs=vmem,
        out_shape=jax.ShapeDtypeStruct((CAP, k_local + 2 * blocks), jnp.float32),
        scratch_shapes=[pltpu.VMEM((k_local, width), jnp.float32), pltpu.SemaphoreType.DMA((4,))],
        compiler_params=pltpu.CompilerParams(vmem_limit_bytes=20 * 2**20),
    )(low.reshape(1), pivots, a_first, prior_lt)


def couple_kernel(weight_ref, lt_ref, after_ref, big_ref, small_ref):
    value = lt_ref[...]
    rows = value.shape[0]
    after = pltpu.roll(value, rows - 1, 0)
    before = pltpu.roll(value, 1, 0)
    mixed = weight_ref[:, 0:1] * value + weight_ref[:, 1:2] * after + weight_ref[:, 2:3] * before
    big_ref[...], small_ref[...] = split(mixed)


def coupled_parts(weights, prior_lt, following):
    k_local, width = prior_lt.shape
    depth = k_local // 4
    block = pl.BlockSpec((depth, width), lambda i: (i, 0))
    shape = jax.ShapeDtypeStruct((k_local, width), jnp.bfloat16)
    return pl.pallas_call(
        couple_kernel,
        grid=(4,),
        in_specs=[
            pl.BlockSpec((depth, 3), lambda i: (i, 0)),
            block,
            pl.BlockSpec(memory_space=pl.ANY),
        ],
        out_specs=(block, block),
        out_shape=(shape, shape),
        compiler_params=pltpu.CompilerParams(vmem_limit_bytes=20 * 2**20),
        cost_estimate=pl.CostEstimate(
            flops=8 * k_local * width, bytes_accessed=8 * k_local * width, transcendentals=0
        ),
    )(weights, prior_lt, following)


def fill_parts(parts_ref, pieces):
    total = parts_ref.shape[0] // 2
    start = 0
    for ref in pieces:
        size = ref.shape[0]
        big, small = split(ref[...])
        parts_ref[start : start + size, :] = big
        parts_ref[total + start : total + start + size, :] = small
        start += size


def hits(index, base, total):
    slot = base + lax.broadcasted_iota(jnp.int32, (index.shape[0], total), 1)
    hit = jnp.where(index == slot, 1.0, 0.0).astype(jnp.bfloat16)
    return jnp.concatenate([hit, hit], 1)


def early_kernel(index_ref, *refs):
    *pieces, out_ref, parts_ref = refs
    fill_parts(parts_ref, pieces)
    total = parts_ref.shape[0] // 2
    hit = hits(index_ref[...], 0, total)
    for low in range(0, out_ref.shape[1], 384):
        out_ref[:, low : low + 384] = jnp.dot(
            hit, parts_ref[:, low : low + 384], preferred_element_type=jnp.float32
        )


def send_kernel(index_ref, weight_ref, carry_ref, lt_big_ref, lt_small_ref, *refs, base):
    *pieces, out_ref, second_ref, entries_ref, big_ref, small_ref, keep_ref, parts_ref = refs
    fill_parts(parts_ref, pieces)
    total = parts_ref.shape[0] // 2
    rows, k_local = out_ref.shape[0], lt_big_ref.shape[0]
    tile_rows = lt_big_ref.shape[1]
    hit = hits(index_ref[...], base, total)
    taken = carry_ref[...] + jnp.dot(hit, parts_ref[...], preferred_element_type=jnp.float32)
    keep_ref[...] = taken[rows + P_SIZE :, :k_local]
    second = taken[rows : rows + P_SIZE]
    entries_ref[...] = second[:, k_local:]
    second = second[:, :k_local]
    second_ref[...] = second
    after = pltpu.roll(second, k_local - 1, 1)
    before = pltpu.roll(second, 1, 1)
    coupled = split(
        weight_ref[0:1, :] * second + weight_ref[1:2, :] * after + weight_ref[2:3, :] * before
    )
    big_ref[...] = coupled[0]
    small_ref[...] = coupled[1]
    first = split(taken[:rows, :k_local])
    out_ref[:, :tile_rows] = dot3(first, (lt_big_ref[...], lt_small_ref[...]), ((1,), (0,)))
    out_ref[:, tile_rows:] = dot3(first, coupled, ((1,), (1,)))


def keep_kernel(taken_ref, lt_big_ref, lt_small_ref, big_ref, small_ref, out_ref):
    tile_rows = lt_big_ref.shape[1]
    first = split(taken_ref[...])
    out_ref[:, :tile_rows] = dot3(first, (lt_big_ref[...], lt_small_ref[...]), ((1,), (0,)))
    out_ref[:, tile_rows:] = dot3(first, (big_ref[...], small_ref[...]), ((1,), (1,)))


def second_kernel(quarter_ref, second_ref, lt_big_ref, lt_small_ref, out_ref, whole_ref):
    blocks = out_ref.shape[0] // 4
    rows = split(second_ref[...])
    whole_ref[...] = dot3(rows, (lt_big_ref[...], lt_small_ref[...]), ((1,), (0,)))
    for i in range(4):
        start = pl.multiple_of(quarter_ref[i] * blocks, blocks)
        out_ref[i * blocks : (i + 1) * blocks, :] = whole_ref[pl.ds(start, blocks), :]


def local_call(kernel, out_shape, flops, *args, scratch=(), smem=0):
    vmem = pl.BlockSpec(memory_space=pltpu.VMEM)
    specs = [pl.BlockSpec(memory_space=pltpu.SMEM)] * smem + [vmem] * (len(args) - smem)
    return pl.pallas_call(
        kernel,
        in_specs=specs,
        out_specs=jax.tree.map(lambda _: vmem, out_shape),
        out_shape=out_shape,
        scratch_shapes=list(scratch),
        compiler_params=pltpu.CompilerParams(vmem_limit_bytes=20 * 2**20),
        cost_estimate=pl.CostEstimate(
            flops=flops, bytes_accessed=4 * sum(x.size for x in args), transcendentals=0
        ),
    )(*args)


def quarter_order(me):
    core, chip = me % 2, me // 2
    return [(1 - chip) * 2 + 1 - core, chip * 2 + 1 - core, (1 - chip) * 2 + core, me]


def in_quarters(rows, quarters, blocks):
    return jnp.concatenate([lax.dynamic_slice_in_dim(rows, q * blocks, blocks) for q in quarters], 0)


def finish_sum(send, keep):
    half = keep.shape[0] // 2
    got = lax.ppermute(send, "narrow", CORE)
    away = lax.ppermute(keep[:half] + got[:half], "narrow", CHIP)
    return keep[half:] + got[half:] + away


def shards(
    prior_lt, prior_d, prior_e, prior_pairs, pivots, a_first, a_second, inv_d, inv_e, panel_pairs
):
    k_local, tile_rows = prior_lt.shape
    blocks = a_first.shape[0]
    here = lax.axis_index("wide")
    flat = pivots.reshape(-1)
    tile = flat // tile_rows
    count = flat.shape[0]
    order = jnp.arange(count)
    rank = jnp.sum((tile[:, None] == tile[None, :]) & (order[None, :] < order[:, None]), 1)
    block = tile_slots(pivots, here * tile_rows, prior_lt, a_first)
    early, late = gather_tiles(block)
    offsets = [o for piece in early + late for o in piece[1]]
    ty, tz, th = tile // (NZ * NH), tile // NH % NZ, tile % NH
    hy, hz, hh = here // (NZ * NH), here // NH % NZ, here % NH
    rel = ((ty - hy) % NY * NZ + (tz - hz) % NZ) * NH + (th - hh) % NH
    place_of = [0] * (NY * NZ * NH)
    for i, (y, z, h) in enumerate(offsets):
        place_of[(y * NZ + z) * NH + h] = i
    place = jnp.sum(
        jnp.where(rel[:, None] == jnp.arange(NY * NZ * NH)[None, :], jnp.array(place_of)[None, :], 0), 1
    )
    where = place * CAP + rank
    quarters = quarter_order(lax.axis_index("narrow"))
    ordered = in_quarters(where[:P_SIZE], quarters, blocks)
    half = P_SIZE // 2
    where = jnp.concatenate([ordered[:half], where[P_SIZE:], ordered[half:]]).reshape(-1, 1)
    early_rows = CAP * sum(len(piece[1]) for piece in early)
    late_rows = CAP * sum(len(piece[1]) for piece in late)
    width = block.shape[1]
    wide = tile_rows + P_SIZE
    f32, b16 = jnp.float32, jnp.bfloat16
    shape = jax.ShapeDtypeStruct
    joined = prior_e * prior_pairs.astype(f32)
    weights = jnp.stack([prior_d, joined, jnp.concatenate([jnp.zeros_like(joined[:1]), joined[:-1]])])
    lt_big, lt_small = coupled_parts(weights.T, prior_lt, early[0][0])
    carry = local_call(
        early_kernel,
        shape((2 * P_SIZE, width), f32),
        4 * 2 * P_SIZE * early_rows * width,
        where,
        *[piece[0] for piece in early],
        scratch=[pltpu.VMEM((2 * early_rows, width), b16)],
    )
    send, second, entries, second_big, second_small, taken = local_call(
        functools.partial(send_kernel, base=early_rows),
        (
            shape((half, wide), f32),
            shape((P_SIZE, k_local), f32),
            shape((P_SIZE, width - k_local), f32),
            shape((P_SIZE, k_local), b16),
            shape((P_SIZE, k_local), b16),
            shape((half, k_local), f32),
        ),
        8 * P_SIZE * late_rows * width + 6 * half * k_local * wide,
        where,
        weights,
        carry,
        lt_big,
        lt_small,
        *[piece[0] for piece in late],
        scratch=[pltpu.VMEM((2 * late_rows, width), b16)],
    )
    keep = local_call(
        keep_kernel,
        shape((half, wide), f32),
        6 * half * k_local * wide,
        taken,
        lt_big,
        lt_small,
        second_big,
        second_small,
    )
    summed = finish_sum(send, keep)
    update_second = local_call(
        second_kernel,
        shape((P_SIZE, tile_rows), f32),
        6 * P_SIZE * k_local * tile_rows,
        jnp.stack(quarters),
        second,
        lt_big,
        lt_small,
        scratch=[pltpu.VMEM((P_SIZE, tile_rows), f32)],
        smem=1,
    )
    w_first = a_first - summed[:, :tile_rows]
    l_first = couple(w_first, inv_d[0], inv_e[0], panel_pairs[0])
    w_crossed = entries[:, :blocks] - summed[:, tile_rows:].T
    crossed = couple_lanes(w_crossed, inv_d[0], inv_e[0], panel_pairs[0])
    plain = (((1,), (0,)), ((), ()))
    halves = []
    for low in (0, 2):
        rows = in_quarters(crossed, quarters[low : low + 2], blocks)
        part = update_second[low * blocks : (low + 2) * blocks]
        halves.append(part + lax.dot_general(rows, w_first, plain, precision=HIGH))
    w_second = a_second - finish_sum(*halves)
    l_second = couple(w_second, inv_d[1], inv_e[1], panel_pairs[1])
    return (l_first, l_second)


def solution(mesh):
    in_specs = (
        P("narrow", "wide"),
        P("narrow"),
        P("narrow"),
        P("narrow"),
        P(),
        P("narrow", "wide"),
        P("narrow", "wide"),
        P(None, "narrow"),
        P(None, "narrow"),
        P(None, "narrow"),
    )
    out_specs = (P("narrow", "wide"), P("narrow", "wide"))
    return jax.shard_map(shards, mesh=mesh, in_specs=in_specs, out_specs=out_specs, check_vma=False)
```

```python
import functools

import jax
import jax.numpy as jnp
from jax import lax
from jax.experimental import pallas as pl
from jax.experimental.pallas import tpu as pltpu
from jax.sharding import PartitionSpec as P

P_SIZE = 256
CAP = 16
NY, NZ, NH = 4, 8, 2
CORE = [(0, 1), (1, 0), (2, 3), (3, 2)]
CHIP = [(0, 2), (1, 3), (2, 0), (3, 1)]
HIGH = lax.Precision.HIGH


def couple(block, diag, off, pairs):
    joined = off * pairs.astype(jnp.float32)
    zero_row = jnp.zeros_like(block[:1])
    after = jnp.concatenate([block[1:], zero_row], 0)
    before = jnp.concatenate([zero_row, block[:-1]], 0)
    lower = jnp.concatenate([jnp.zeros_like(joined[:1]), joined[:-1]], 0)
    return diag[:, None] * block + joined[:, None] * after + lower[:, None] * before


def couple_lanes(block, diag, off, pairs):
    joined = off * pairs.astype(jnp.float32)
    zero = jnp.zeros_like(block[:, :1])
    after = jnp.concatenate([block[:, 1:], zero], 1)
    before = jnp.concatenate([zero, block[:, :-1]], 1)
    lower = jnp.concatenate([jnp.zeros_like(joined[:1]), joined[:-1]], 0)
    return diag[None, :] * block + joined[None, :] * after + lower[None, :] * before


def shift(dy, dz, dh):
    pairs = []
    for y in range(NY):
        for z in range(NZ):
            for h in range(NH):
                to = ((y + dy) % NY * NZ + (z + dz) % NZ) * NH + (h + dh) % NH
                pairs.append(((y * NZ + z) * NH + h, to))
    return pairs


def moved(block, offsets, step):
    got = lax.ppermute(block, "wide", shift(*step))
    return got, [
        ((y - step[0]) % NY, (z - step[1]) % NZ, (h - step[2]) % NH) for y, z, h in offsets
    ]


def gather_tiles(block, made):
    rows = block.shape[0]
    held, at = block, [(0, 0, 0)]
    got, its = moved(held, at, (0, 4, 0))
    held, at = jnp.concatenate([held, got], 0), at + its
    parts = [moved(held, at, step) for step in ((2, 1, 0), (2, -1, 0), (0, 2, 0))]
    held = jnp.concatenate([held] + [p[0] for p in parts], 0)
    at = at + parts[0][1] + parts[1][1] + parts[2][1]
    half = len(at) // 2
    cut = half * rows
    over = moved(held, at, (0, 0, 1))
    ahead = moved(held, at, (1, 0, 0))
    behind = moved(held, at, (-1, 0, 0))
    up = moved(held[:cut], at[:half], (0, 1, 0))
    down = moved(held[:cut], at[:half], (0, -1, 0))
    early = [(held, at), ahead, behind, over, up, down]
    few = half // 2
    edge = few * rows
    ready = made(held)
    mixed = cuts([(ahead[0], held.shape[0] - edge, edge, 0, 0), (behind[0], 0, edge, 0, edge)], [2 * edge])
    low, high, middle = cuts(
        [(over[0], 0, 3 * edge, 0, 0), (over[0], edge, 3 * edge, 1, 0), (over[0], 0, cut, 2, 0)],
        [3 * edge, 3 * edge, cut],
        ready[0],
    )
    late = [
        moved(mixed[0], ahead[1][-few:] + behind[1][:few], (0, 0, 1)),
        moved(low, over[1][:-few], (1, 0, 0)),
        moved(high, over[1][few:], (-1, 0, 0)),
        moved(middle, over[1][:half], (0, 1, 0)),
        moved(middle, over[1][:half], (0, -1, 0)),
    ]
    return early, late, ready


def in_hbm(value):
    return pltpu.with_memory_space_constraint(value, pltpu.HBM)


def cuts_kernel(*refs, parts, inputs):
    sems = refs[-1]
    outs = refs[inputs:-1]
    copies = []
    for i, (start, size, out, to) in enumerate(parts):
        copies.append(
            pltpu.make_async_copy(
                refs[i].at[pl.ds(start, size)], outs[out].at[pl.ds(to, size)], sems.at[i]
            )
        )
        copies[-1].start()
    for copy in copies:
        copy.wait()


def cuts(parts, sizes, following=None):
    args = [in_hbm(part[0]) for part in parts] + ([] if following is None else [following])
    width = parts[0][0].shape[1]
    return pl.pallas_call(
        functools.partial(cuts_kernel, parts=[part[1:] for part in parts], inputs=len(args)),
        in_specs=[pl.BlockSpec(memory_space=pl.ANY)] * len(args),
        out_specs=[pl.BlockSpec(memory_space=pltpu.VMEM)] * len(sizes),
        out_shape=[jax.ShapeDtypeStruct((size, width), jnp.float32) for size in sizes],
        scratch_shapes=[pltpu.SemaphoreType.DMA((len(parts),))],
        compiler_params=pltpu.CompilerParams(vmem_limit_bytes=20 * 2**20),
    )(*args)


def split(value):
    big = value.astype(jnp.bfloat16)
    return big, (value - big.astype(jnp.float32)).astype(jnp.bfloat16)


def dot3(left, right, dims):
    def dot(x, y):
        return lax.dot_general(x, y, (dims, ((), ())), preferred_element_type=jnp.float32)

    return dot(left[0], right[0]) + (dot(left[0], right[1]) + dot(left[1], right[0]))


def slots_kernel(low_ref, pivots_hbm, a_hbm, lt_ref, out_ref, lt_buf, pivots_ref, a_ref, sems, more):
    k_local, width = lt_ref.shape
    depth = k_local // sems.shape[0]
    copies = []
    small = [
        pltpu.make_async_copy(pivots_hbm, pivots_ref, more.at[0]),
        pltpu.make_async_copy(a_hbm, a_ref, more.at[1]),
    ]
    for copy in small:
        copy.start()
    for i in range(sems.shape[0]):
        rows = slice(i * depth, (i + 1) * depth)
        copies.append(pltpu.make_async_copy(lt_ref.at[rows], lt_buf.at[rows], sems.at[i]))
        copies[-1].start()
    small[0].wait()
    row = jnp.concatenate([pivots_ref[0:1, :], pivots_ref[1:2, :]], 1) - low_ref[0]
    count = row.shape[1]
    mine = (row >= 0) & (row < width)
    before = lax.broadcasted_iota(jnp.int32, (count, count), 0) < lax.broadcasted_iota(
        jnp.int32, (count, count), 1
    )
    ones = jnp.broadcast_to(jnp.where(mine, 1.0, 0.0), (16, count)).astype(jnp.bfloat16)
    rank = jnp.dot(
        ones, jnp.where(before, 1.0, 0.0).astype(jnp.bfloat16), preferred_element_type=jnp.float32
    )
    slot = lax.broadcasted_iota(jnp.int32, (128, count), 0).astype(jnp.float32)
    hit = (slot == rank[:1]) & mine
    offset = jnp.sum(jnp.where(hit, row + 1, 0).astype(jnp.float32), 1, keepdims=True) - 1.0
    column = lax.broadcasted_iota(jnp.int32, (128, width), 1).astype(jnp.float32)
    pick = jnp.where(column == offset, 1.0, 0.0).astype(jnp.bfloat16)
    across = (((1,), (1,)), ((), ()))

    def rows_of(value):
        total = None
        for _ in range(3):
            part = value.astype(jnp.bfloat16)
            value = value - part.astype(jnp.float32)
            got = lax.dot_general(part, pick, across, preferred_element_type=jnp.float32)
            total = got if total is None else total + got
        return total.T[:CAP]

    small[1].wait()
    extra = rows_of(a_ref[...])
    out_ref[:, k_local:] = jnp.concatenate([extra, jnp.zeros_like(extra)], 1)
    for i, copy in enumerate(copies):
        copy.wait()
        rows = slice(i * depth, (i + 1) * depth)
        out_ref[:, rows] = rows_of(lt_buf[rows, :])


def tile_slots(pivots, low, prior_lt, a_first):
    k_local, width = prior_lt.shape
    blocks = a_first.shape[0]
    vmem = pl.BlockSpec(memory_space=pltpu.VMEM)
    return pl.pallas_call(
        slots_kernel,
        in_specs=[
            pl.BlockSpec(memory_space=pltpu.SMEM),
            pl.BlockSpec(memory_space=pl.ANY),
            pl.BlockSpec(memory_space=pl.ANY),
            pl.BlockSpec(memory_space=pl.ANY),
        ],
        out_specs=vmem,
        out_shape=jax.ShapeDtypeStruct((CAP, k_local + 2 * blocks), jnp.float32),
        scratch_shapes=[
            pltpu.VMEM((k_local, width), jnp.float32),
            pltpu.VMEM(pivots.shape, jnp.int32),
            pltpu.VMEM((blocks, width), jnp.float32),
            pltpu.SemaphoreType.DMA((4,)),
            pltpu.SemaphoreType.DMA((2,)),
        ],
        compiler_params=pltpu.CompilerParams(vmem_limit_bytes=20 * 2**20),
    )(low.reshape(1), in_hbm(pivots), in_hbm(a_first), in_hbm(prior_lt))


def couple_kernel(weight_ref, lt_ref, after_ref, big_ref, small_ref):
    value = lt_ref[...]
    rows = value.shape[0]
    after = pltpu.roll(value, rows - 1, 0)
    before = pltpu.roll(value, 1, 0)
    weight = weight_ref[...].T
    mixed = weight[:, 0:1] * value + weight[:, 1:2] * after + weight[:, 2:3] * before
    big_ref[...], small_ref[...] = split(mixed)


def coupled_parts(weights, prior_lt, following):
    k_local, width = prior_lt.shape
    depth = k_local // 4
    block = pl.BlockSpec((depth, width), lambda i: (i, 0))
    shape = jax.ShapeDtypeStruct((k_local, width), jnp.bfloat16)
    return pl.pallas_call(
        couple_kernel,
        grid=(4,),
        in_specs=[
            pl.BlockSpec((8, depth), lambda i: (0, i)),
            block,
            pl.BlockSpec(memory_space=pl.ANY),
        ],
        out_specs=(block, block),
        out_shape=(shape, shape),
        compiler_params=pltpu.CompilerParams(vmem_limit_bytes=20 * 2**20),
        cost_estimate=pl.CostEstimate(
            flops=8 * k_local * width, bytes_accessed=8 * k_local * width, transcendentals=0
        ),
    )(weights, in_hbm(prior_lt), following)


def fill_parts(parts_ref, pieces):
    total = parts_ref.shape[0] // 2
    start = 0
    for ref in pieces:
        size = ref.shape[0]
        big, small = split(ref[...])
        parts_ref[start : start + size, :] = big
        parts_ref[total + start : total + start + size, :] = small
        start += size


def hits(index, base, total):
    slot = base + lax.broadcasted_iota(jnp.int32, (index.shape[0], total), 1)
    hit = jnp.where(index == slot, 1.0, 0.0).astype(jnp.bfloat16)
    return jnp.concatenate([hit, hit], 1)


def early_kernel(index_ref, *refs):
    *pieces, out_ref, rows_ref, parts_ref, sems = refs
    total = rows_ref.shape[0]
    start, copies = 0, []
    for i, ref in enumerate(pieces):
        size = ref.shape[0]
        rows = slice(start, start + size)
        copies.append((rows, pltpu.make_async_copy(ref, rows_ref.at[rows], sems.at[i])))
        copies[-1][1].start()
        start += size
    hit = hits(index_ref[...], 0, total)
    for rows, copy in copies:
        copy.wait()
        big, small = split(rows_ref[rows, :])
        parts_ref[rows, :] = big
        parts_ref[total + rows.start : total + rows.stop, :] = small
    for low in range(0, out_ref.shape[1], 384):
        out_ref[:, low : low + 384] = jnp.dot(
            hit, parts_ref[:, low : low + 384], preferred_element_type=jnp.float32
        )


def send_kernel(index_ref, weight_ref, carry_ref, lt_big_ref, lt_small_ref, *refs, base):
    *pieces, out_ref, second_ref, entries_ref, big_ref, small_ref, keep_ref, parts_ref = refs
    fill_parts(parts_ref, pieces)
    total = parts_ref.shape[0] // 2
    rows, k_local = out_ref.shape[0], lt_big_ref.shape[0]
    tile_rows = lt_big_ref.shape[1]
    hit = hits(index_ref[...], base, total)
    taken = carry_ref[...] + jnp.dot(hit, parts_ref[...], preferred_element_type=jnp.float32)
    keep_ref[...] = taken[rows + P_SIZE :, :k_local]
    second = taken[rows : rows + P_SIZE]
    entries_ref[...] = second[:, k_local:]
    second = second[:, :k_local]
    second_ref[...] = second
    after = pltpu.roll(second, k_local - 1, 1)
    before = pltpu.roll(second, 1, 1)
    coupled = split(
        weight_ref[0:1, :] * second + weight_ref[1:2, :] * after + weight_ref[2:3, :] * before
    )
    big_ref[...] = coupled[0]
    small_ref[...] = coupled[1]
    first = split(taken[:rows, :k_local])
    out_ref[:, :tile_rows] = dot3(first, (lt_big_ref[...], lt_small_ref[...]), ((1,), (0,)))
    out_ref[:, tile_rows:] = dot3(first, coupled, ((1,), (1,)))


def keep_kernel(taken_ref, lt_big_ref, lt_small_ref, big_ref, small_ref, out_ref):
    tile_rows = lt_big_ref.shape[1]
    first = split(taken_ref[...])
    out_ref[:, :tile_rows] = dot3(first, (lt_big_ref[...], lt_small_ref[...]), ((1,), (0,)))
    out_ref[:, tile_rows:] = dot3(first, (big_ref[...], small_ref[...]), ((1,), (1,)))


def second_kernel(quarter_ref, second_ref, lt_big_ref, lt_small_ref, out_ref, whole_ref):
    blocks = out_ref.shape[0] // 4
    rows = split(second_ref[...])
    whole_ref[...] = dot3(rows, (lt_big_ref[...], lt_small_ref[...]), ((1,), (0,)))
    for i in range(4):
        start = pl.multiple_of(quarter_ref[i] * blocks, blocks)
        out_ref[i * blocks : (i + 1) * blocks, :] = whole_ref[pl.ds(start, blocks), :]


def local_call(kernel, out_shape, flops, *args, scratch=(), smem=0, hbm=0):
    vmem = pl.BlockSpec(memory_space=pltpu.VMEM)
    specs = [pl.BlockSpec(memory_space=pltpu.SMEM)] * smem + [vmem] * (len(args) - smem - hbm)
    specs += [pl.BlockSpec(memory_space=pl.ANY)] * hbm
    return pl.pallas_call(
        kernel,
        in_specs=specs,
        out_specs=jax.tree.map(lambda _: vmem, out_shape),
        out_shape=out_shape,
        scratch_shapes=list(scratch),
        compiler_params=pltpu.CompilerParams(vmem_limit_bytes=20 * 2**20),
        cost_estimate=pl.CostEstimate(
            flops=flops, bytes_accessed=4 * sum(x.size for x in args), transcendentals=0
        ),
    )(*args)


def quarter_order(me):
    core, chip = me % 2, me // 2
    return [(1 - chip) * 2 + 1 - core, chip * 2 + 1 - core, (1 - chip) * 2 + core, me]


def in_quarters(rows, quarters, blocks):
    return jnp.concatenate([lax.dynamic_slice_in_dim(rows, q * blocks, blocks) for q in quarters], 0)


def finish_sum(send, keep):
    half = keep.shape[0] // 2
    got = lax.ppermute(send, "narrow", CORE)
    away = lax.ppermute(keep[:half] + got[:half], "narrow", CHIP)
    return keep[half:] + got[half:] + away


def shards(
    prior_lt, prior_d, prior_e, prior_pairs, pivots, a_first, a_second, inv_d, inv_e, panel_pairs
):
    k_local, tile_rows = prior_lt.shape
    blocks = a_first.shape[0]
    here = lax.axis_index("wide")
    flat = pivots.reshape(-1)
    tile = flat // tile_rows
    count = flat.shape[0]
    order = jnp.arange(count)
    rank = jnp.sum((tile[:, None] == tile[None, :]) & (order[None, :] < order[:, None]), 1)
    block = tile_slots(pivots, here * tile_rows, prior_lt, a_first)
    joined = prior_e * prior_pairs.astype(jnp.float32)
    lower = jnp.concatenate([jnp.zeros_like(joined[:1]), joined[:-1]])
    weights = jnp.pad(jnp.stack([prior_d, joined, lower]), ((0, 5), (0, 0)))
    early, late, (lt_big, lt_small) = gather_tiles(
        block, lambda held: coupled_parts(weights, prior_lt, held)
    )
    offsets = [o for piece in early + late for o in piece[1]]
    ty, tz, th = tile // (NZ * NH), tile // NH % NZ, tile % NH
    hy, hz, hh = here // (NZ * NH), here // NH % NZ, here % NH
    rel = ((ty - hy) % NY * NZ + (tz - hz) % NZ) * NH + (th - hh) % NH
    place_of = [0] * (NY * NZ * NH)
    for i, (y, z, h) in enumerate(offsets):
        place_of[(y * NZ + z) * NH + h] = i
    place = jnp.sum(
        jnp.where(rel[:, None] == jnp.arange(NY * NZ * NH)[None, :], jnp.array(place_of)[None, :], 0), 1
    )
    where = place * CAP + rank
    quarters = quarter_order(lax.axis_index("narrow"))
    ordered = in_quarters(where[:P_SIZE], quarters, blocks)
    half = P_SIZE // 2
    where = jnp.concatenate([ordered[:half], where[P_SIZE:], ordered[half:]]).reshape(-1, 1)
    early_rows = CAP * sum(len(piece[1]) for piece in early)
    late_rows = CAP * sum(len(piece[1]) for piece in late)
    width = block.shape[1]
    wide = tile_rows + P_SIZE
    f32, b16 = jnp.float32, jnp.bfloat16
    shape = jax.ShapeDtypeStruct
    carry = local_call(
        early_kernel,
        shape((2 * P_SIZE, width), f32),
        4 * 2 * P_SIZE * early_rows * width,
        where,
        *[in_hbm(piece[0]) for piece in early],
        scratch=[
            pltpu.VMEM((early_rows, width), f32),
            pltpu.VMEM((2 * early_rows, width), b16),
            pltpu.SemaphoreType.DMA((len(early),)),
        ],
        hbm=len(early),
    )
    send, second, entries, second_big, second_small, taken = local_call(
        functools.partial(send_kernel, base=early_rows),
        (
            shape((half, wide), f32),
            shape((P_SIZE, k_local), f32),
            shape((P_SIZE, width - k_local), f32),
            shape((P_SIZE, k_local), b16),
            shape((P_SIZE, k_local), b16),
            shape((half, k_local), f32),
        ),
        8 * P_SIZE * late_rows * width + 6 * half * k_local * wide,
        where,
        weights,
        carry,
        lt_big,
        lt_small,
        *[piece[0] for piece in late],
        scratch=[pltpu.VMEM((2 * late_rows, width), b16)],
    )
    keep = local_call(
        keep_kernel,
        shape((half, wide), f32),
        6 * half * k_local * wide,
        taken,
        lt_big,
        lt_small,
        second_big,
        second_small,
    )
    summed = finish_sum(send, keep)
    update_second = local_call(
        second_kernel,
        shape((P_SIZE, tile_rows), f32),
        6 * P_SIZE * k_local * tile_rows,
        jnp.stack(quarters),
        second,
        lt_big,
        lt_small,
        scratch=[pltpu.VMEM((P_SIZE, tile_rows), f32)],
        smem=1,
    )
    w_first = a_first - summed[:, :tile_rows]
    l_first = couple(w_first, inv_d[0], inv_e[0], panel_pairs[0])
    w_crossed = entries[:, :blocks] - summed[:, tile_rows:].T
    crossed = couple_lanes(w_crossed, inv_d[0], inv_e[0], panel_pairs[0])
    plain = (((1,), (0,)), ((), ()))
    halves = []
    for low in (0, 2):
        rows = in_quarters(crossed, quarters[low : low + 2], blocks)
        part = update_second[low * blocks : (low + 2) * blocks]
        halves.append(part + lax.dot_general(rows, w_first, plain, precision=HIGH))
    w_second = a_second - finish_sum(*halves)
    l_second = couple(w_second, inv_d[1], inv_e[1], panel_pairs[1])
    return (l_first, l_second)


def solution(mesh):
    in_specs = (
        P("narrow", "wide"),
        P("narrow"),
        P("narrow"),
        P("narrow"),
        P(),
        P("narrow", "wide"),
        P("narrow", "wide"),
        P(None, "narrow"),
        P(None, "narrow"),
        P(None, "narrow"),
    )
    out_specs = (P("narrow", "wide"), P("narrow", "wide"))
    return jax.shard_map(shards, mesh=mesh, in_specs=in_specs, out_specs=out_specs, check_vma=False)
```

```python
import functools

import jax
import jax.numpy as jnp
from jax import lax
from jax.experimental import pallas as pl
from jax.experimental.pallas import tpu as pltpu
from jax.sharding import PartitionSpec as P

P_SIZE = 256
CAP = 16
NY, NZ, NH = 4, 8, 2
CORE = [(0, 1), (1, 0), (2, 3), (3, 2)]
CHIP = [(0, 2), (1, 3), (2, 0), (3, 1)]
HIGH = lax.Precision.HIGH


def couple(block, diag, off, pairs):
    joined = off * pairs.astype(jnp.float32)
    zero_row = jnp.zeros_like(block[:1])
    after = jnp.concatenate([block[1:], zero_row], 0)
    before = jnp.concatenate([zero_row, block[:-1]], 0)
    lower = jnp.concatenate([jnp.zeros_like(joined[:1]), joined[:-1]], 0)
    return diag[:, None] * block + joined[:, None] * after + lower[:, None] * before


def couple_lanes(block, diag, off, pairs):
    joined = off * pairs.astype(jnp.float32)
    zero = jnp.zeros_like(block[:, :1])
    after = jnp.concatenate([block[:, 1:], zero], 1)
    before = jnp.concatenate([zero, block[:, :-1]], 1)
    lower = jnp.concatenate([jnp.zeros_like(joined[:1]), joined[:-1]], 0)
    return diag[None, :] * block + joined[None, :] * after + lower[None, :] * before


def shift(dy, dz, dh):
    pairs = []
    for y in range(NY):
        for z in range(NZ):
            for h in range(NH):
                to = ((y + dy) % NY * NZ + (z + dz) % NZ) * NH + (h + dh) % NH
                pairs.append(((y * NZ + z) * NH + h, to))
    return pairs


def moved(block, offsets, step):
    got = lax.ppermute(block, "wide", shift(*step))
    return got, [
        ((y - step[0]) % NY, (z - step[1]) % NZ, (h - step[2]) % NH) for y, z, h in offsets
    ]


def gather_tiles(block, made):
    rows = block.shape[0]
    held, at = block, [(0, 0, 0)]
    got, its = moved(held, at, (0, 4, 0))
    held, at = jnp.concatenate([held, got], 0), at + its
    parts = [moved(held, at, step) for step in ((2, 1, 0), (2, -1, 0), (0, 2, 0))]
    held = jnp.concatenate([held] + [p[0] for p in parts], 0)
    at = at + parts[0][1] + parts[1][1] + parts[2][1]
    half = len(at) // 2
    cut = half * rows
    over = moved(held, at, (0, 0, 1))
    ahead = moved(held, at, (1, 0, 0))
    behind = moved(held, at, (-1, 0, 0))
    up = moved(held[:cut], at[:half], (0, 1, 0))
    down = moved(held[:cut], at[:half], (0, -1, 0))
    early = [(held, at), ahead, behind, over, up, down]
    ready = made(held)
    middle, *_ = cuts([(over[0], 0, cut, 0, 0)], [cut], ready[0])
    late = [
        moved(over[0], over[1], (1, 0, 0)),
        moved(over[0], over[1], (-1, 0, 0)),
        moved(middle, over[1][:half], (0, 1, 0)),
        moved(middle, over[1][:half], (0, -1, 0)),
    ]
    return early, late, ready


def in_hbm(value):
    return pltpu.with_memory_space_constraint(value, pltpu.HBM)


def cuts_kernel(*refs, parts, inputs):
    sems = refs[-1]
    outs = refs[inputs:-1]
    copies = []
    for i, (start, size, out, to) in enumerate(parts):
        copies.append(
            pltpu.make_async_copy(
                refs[i].at[pl.ds(start, size)], outs[out].at[pl.ds(to, size)], sems.at[i]
            )
        )
        copies[-1].start()
    for copy in copies:
        copy.wait()


def cuts(parts, sizes, following=None):
    args = [in_hbm(part[0]) for part in parts] + ([] if following is None else [following])
    width = parts[0][0].shape[1]
    return pl.pallas_call(
        functools.partial(cuts_kernel, parts=[part[1:] for part in parts], inputs=len(args)),
        in_specs=[pl.BlockSpec(memory_space=pl.ANY)] * len(args),
        out_specs=[pl.BlockSpec(memory_space=pltpu.VMEM)] * len(sizes),
        out_shape=[jax.ShapeDtypeStruct((size, width), jnp.float32) for size in sizes],
        scratch_shapes=[pltpu.SemaphoreType.DMA((len(parts),))],
        compiler_params=pltpu.CompilerParams(vmem_limit_bytes=20 * 2**20),
    )(*args)


def split(value):
    big = value.astype(jnp.bfloat16)
    return big, (value - big.astype(jnp.float32)).astype(jnp.bfloat16)


def dot3(left, right, dims):
    def dot(x, y):
        return lax.dot_general(x, y, (dims, ((), ())), preferred_element_type=jnp.float32)

    return dot(left[0], right[0]) + (dot(left[0], right[1]) + dot(left[1], right[0]))


def slots_kernel(low_ref, pivots_hbm, a_hbm, lt_ref, out_ref, lt_buf, pivots_ref, a_ref, sems, more):
    k_local, width = lt_ref.shape
    depth = k_local // sems.shape[0]
    copies = []
    small = [
        pltpu.make_async_copy(pivots_hbm, pivots_ref, more.at[0]),
        pltpu.make_async_copy(a_hbm, a_ref, more.at[1]),
    ]
    for copy in small:
        copy.start()
    for i in range(sems.shape[0]):
        rows = slice(i * depth, (i + 1) * depth)
        copies.append(pltpu.make_async_copy(lt_ref.at[rows], lt_buf.at[rows], sems.at[i]))
        copies[-1].start()
    small[0].wait()
    row = jnp.concatenate([pivots_ref[0:1, :], pivots_ref[1:2, :]], 1) - low_ref[0]
    count = row.shape[1]
    mine = (row >= 0) & (row < width)
    before = lax.broadcasted_iota(jnp.int32, (count, count), 0) < lax.broadcasted_iota(
        jnp.int32, (count, count), 1
    )
    ones = jnp.broadcast_to(jnp.where(mine, 1.0, 0.0), (16, count)).astype(jnp.bfloat16)
    rank = jnp.dot(
        ones, jnp.where(before, 1.0, 0.0).astype(jnp.bfloat16), preferred_element_type=jnp.float32
    )
    slot = lax.broadcasted_iota(jnp.int32, (128, count), 0).astype(jnp.float32)
    hit = (slot == rank[:1]) & mine
    offset = jnp.sum(jnp.where(hit, row + 1, 0).astype(jnp.float32), 1, keepdims=True) - 1.0
    column = lax.broadcasted_iota(jnp.int32, (128, width), 1).astype(jnp.float32)
    pick = jnp.where(column == offset, 1.0, 0.0).astype(jnp.bfloat16)
    across = (((1,), (1,)), ((), ()))

    def rows_of(value):
        total = None
        for _ in range(2):
            part = value.astype(jnp.bfloat16)
            value = value - part.astype(jnp.float32)
            got = lax.dot_general(part, pick, across, preferred_element_type=jnp.float32)
            total = got if total is None else total + got
        return total.T[:CAP]

    small[1].wait()
    extra = rows_of(a_ref[...])
    out_ref[:, k_local:] = jnp.concatenate([extra, jnp.zeros_like(extra)], 1)
    for i, copy in enumerate(copies):
        copy.wait()
        rows = slice(i * depth, (i + 1) * depth)
        out_ref[:, rows] = rows_of(lt_buf[rows, :])


def tile_slots(pivots, low, prior_lt, a_first):
    k_local, width = prior_lt.shape
    blocks = a_first.shape[0]
    vmem = pl.BlockSpec(memory_space=pltpu.VMEM)
    return pl.pallas_call(
        slots_kernel,
        in_specs=[
            pl.BlockSpec(memory_space=pltpu.SMEM),
            pl.BlockSpec(memory_space=pl.ANY),
            pl.BlockSpec(memory_space=pl.ANY),
            pl.BlockSpec(memory_space=pl.ANY),
        ],
        out_specs=vmem,
        out_shape=jax.ShapeDtypeStruct((CAP, k_local + 2 * blocks), jnp.float32),
        scratch_shapes=[
            pltpu.VMEM((k_local, width), jnp.float32),
            pltpu.VMEM(pivots.shape, jnp.int32),
            pltpu.VMEM((blocks, width), jnp.float32),
            pltpu.SemaphoreType.DMA((4,)),
            pltpu.SemaphoreType.DMA((2,)),
        ],
        compiler_params=pltpu.CompilerParams(vmem_limit_bytes=20 * 2**20),
    )(low.reshape(1), in_hbm(pivots), in_hbm(a_first), in_hbm(prior_lt))


def couple_kernel(weight_ref, lt_ref, after_ref, big_ref, small_ref):
    value = lt_ref[...]
    rows = value.shape[0]
    after = pltpu.roll(value, rows - 1, 0)
    before = pltpu.roll(value, 1, 0)
    weight = weight_ref[...].T
    mixed = weight[:, 0:1] * value + weight[:, 1:2] * after + weight[:, 2:3] * before
    big_ref[...], small_ref[...] = split(mixed)


def coupled_parts(weights, prior_lt, following):
    k_local, width = prior_lt.shape
    depth = k_local // 4
    block = pl.BlockSpec((depth, width), lambda i: (i, 0))
    shape = jax.ShapeDtypeStruct((k_local, width), jnp.bfloat16)
    return pl.pallas_call(
        couple_kernel,
        grid=(4,),
        in_specs=[
            pl.BlockSpec((8, depth), lambda i: (0, i)),
            block,
            pl.BlockSpec(memory_space=pl.ANY),
        ],
        out_specs=(block, block),
        out_shape=(shape, shape),
        compiler_params=pltpu.CompilerParams(vmem_limit_bytes=20 * 2**20),
        cost_estimate=pl.CostEstimate(
            flops=8 * k_local * width, bytes_accessed=8 * k_local * width, transcendentals=0
        ),
    )(weights, in_hbm(prior_lt), following)


def fill_parts(parts_ref, pieces):
    total = parts_ref.shape[0] // 2
    start = 0
    for ref in pieces:
        size = ref.shape[0]
        big, small = split(ref[...])
        parts_ref[start : start + size, :] = big
        parts_ref[total + start : total + start + size, :] = small
        start += size


def hits(index, base, total):
    slot = base + lax.broadcasted_iota(jnp.int32, (index.shape[0], total), 1)
    hit = jnp.where(index == slot, 1.0, 0.0).astype(jnp.bfloat16)
    return jnp.concatenate([hit, hit], 1)


def early_kernel(index_ref, *refs):
    *pieces, out_ref, rows_ref, parts_ref, sems = refs
    total = rows_ref.shape[0]
    start, copies = 0, []
    for i, ref in enumerate(pieces):
        size = ref.shape[0]
        rows = slice(start, start + size)
        copies.append((rows, pltpu.make_async_copy(ref, rows_ref.at[rows], sems.at[i])))
        copies[-1][1].start()
        start += size
    hit = hits(index_ref[...], 0, total)
    for rows, copy in copies:
        copy.wait()
        big, small = split(rows_ref[rows, :])
        parts_ref[rows, :] = big
        parts_ref[total + rows.start : total + rows.stop, :] = small
    for low in range(0, out_ref.shape[1], 384):
        out_ref[:, low : low + 384] = jnp.dot(
            hit, parts_ref[:, low : low + 384], preferred_element_type=jnp.float32
        )


def send_kernel(index_ref, weight_ref, carry_ref, lt_big_ref, lt_small_ref, *refs, base):
    *pieces, out_ref, second_ref, entries_ref, big_ref, small_ref, keep_ref, parts_ref = refs
    fill_parts(parts_ref, pieces)
    total = parts_ref.shape[0] // 2
    rows, k_local = out_ref.shape[0], lt_big_ref.shape[0]
    tile_rows = lt_big_ref.shape[1]
    hit = hits(index_ref[...], base, total)
    taken = carry_ref[...] + jnp.dot(hit, parts_ref[...], preferred_element_type=jnp.float32)
    keep_ref[...] = taken[rows + P_SIZE :, :k_local]
    second = taken[rows : rows + P_SIZE]
    entries_ref[...] = second[:, k_local:]
    second = second[:, :k_local]
    second_ref[...] = second
    after = pltpu.roll(second, k_local - 1, 1)
    before = pltpu.roll(second, 1, 1)
    coupled = split(
        weight_ref[0:1, :] * second + weight_ref[1:2, :] * after + weight_ref[2:3, :] * before
    )
    big_ref[...] = coupled[0]
    small_ref[...] = coupled[1]
    first = split(taken[:rows, :k_local])
    out_ref[:, :tile_rows] = dot3(first, (lt_big_ref[...], lt_small_ref[...]), ((1,), (0,)))
    out_ref[:, tile_rows:] = dot3(first, coupled, ((1,), (1,)))


def keep_kernel(taken_ref, lt_big_ref, lt_small_ref, big_ref, small_ref, out_ref):
    tile_rows = lt_big_ref.shape[1]
    first = split(taken_ref[...])
    out_ref[:, :tile_rows] = dot3(first, (lt_big_ref[...], lt_small_ref[...]), ((1,), (0,)))
    out_ref[:, tile_rows:] = dot3(first, (big_ref[...], small_ref[...]), ((1,), (1,)))


def second_kernel(quarter_ref, second_ref, lt_big_ref, lt_small_ref, out_ref, whole_ref):
    blocks = out_ref.shape[0] // 4
    rows = split(second_ref[...])
    whole_ref[...] = dot3(rows, (lt_big_ref[...], lt_small_ref[...]), ((1,), (0,)))
    for i in range(4):
        start = pl.multiple_of(quarter_ref[i] * blocks, blocks)
        out_ref[i * blocks : (i + 1) * blocks, :] = whole_ref[pl.ds(start, blocks), :]


def local_call(kernel, out_shape, flops, *args, scratch=(), smem=0, hbm=0):
    vmem = pl.BlockSpec(memory_space=pltpu.VMEM)
    specs = [pl.BlockSpec(memory_space=pltpu.SMEM)] * smem + [vmem] * (len(args) - smem - hbm)
    specs += [pl.BlockSpec(memory_space=pl.ANY)] * hbm
    return pl.pallas_call(
        kernel,
        in_specs=specs,
        out_specs=jax.tree.map(lambda _: vmem, out_shape),
        out_shape=out_shape,
        scratch_shapes=list(scratch),
        compiler_params=pltpu.CompilerParams(vmem_limit_bytes=20 * 2**20),
        cost_estimate=pl.CostEstimate(
            flops=flops, bytes_accessed=4 * sum(x.size for x in args), transcendentals=0
        ),
    )(*args)


def quarter_order(me):
    core, chip = me % 2, me // 2
    return [(1 - chip) * 2 + 1 - core, chip * 2 + 1 - core, (1 - chip) * 2 + core, me]


def in_quarters(rows, quarters, blocks):
    return jnp.concatenate([lax.dynamic_slice_in_dim(rows, q * blocks, blocks) for q in quarters], 0)


def finish_sum(send, keep):
    half = keep.shape[0] // 2
    got = lax.ppermute(send, "narrow", CORE)
    away = lax.ppermute(keep[:half] + got[:half], "narrow", CHIP)
    return keep[half:] + got[half:] + away


def shards(
    prior_lt, prior_d, prior_e, prior_pairs, pivots, a_first, a_second, inv_d, inv_e, panel_pairs
):
    k_local, tile_rows = prior_lt.shape
    blocks = a_first.shape[0]
    here = lax.axis_index("wide")
    flat = pivots.reshape(-1)
    tile = flat // tile_rows
    count = flat.shape[0]
    order = jnp.arange(count)
    rank = jnp.sum((tile[:, None] == tile[None, :]) & (order[None, :] < order[:, None]), 1)
    block = tile_slots(pivots, here * tile_rows, prior_lt, a_first)
    joined = prior_e * prior_pairs.astype(jnp.float32)
    lower = jnp.concatenate([jnp.zeros_like(joined[:1]), joined[:-1]])
    weights = jnp.pad(jnp.stack([prior_d, joined, lower]), ((0, 5), (0, 0)))
    early, late, (lt_big, lt_small) = gather_tiles(
        block, lambda held: coupled_parts(weights, prior_lt, held)
    )
    offsets = [o for piece in early + late for o in piece[1]]
    ty, tz, th = tile // (NZ * NH), tile // NH % NZ, tile % NH
    hy, hz, hh = here // (NZ * NH), here // NH % NZ, here % NH
    rel = ((ty - hy) % NY * NZ + (tz - hz) % NZ) * NH + (th - hh) % NH
    place_of = [0] * (NY * NZ * NH)
    for i, (y, z, h) in enumerate(offsets):
        place_of[(y * NZ + z) * NH + h] = i
    place = jnp.sum(
        jnp.where(rel[:, None] == jnp.arange(NY * NZ * NH)[None, :], jnp.array(place_of)[None, :], 0), 1
    )
    where = place * CAP + rank
    quarters = quarter_order(lax.axis_index("narrow"))
    ordered = in_quarters(where[:P_SIZE], quarters, blocks)
    half = P_SIZE // 2
    where = jnp.concatenate([ordered[:half], where[P_SIZE:], ordered[half:]]).reshape(-1, 1)
    early_rows = CAP * sum(len(piece[1]) for piece in early)
    late_rows = CAP * sum(len(piece[1]) for piece in late)
    width = block.shape[1]
    wide = tile_rows + P_SIZE
    f32, b16 = jnp.float32, jnp.bfloat16
    shape = jax.ShapeDtypeStruct
    carry = local_call(
        early_kernel,
        shape((2 * P_SIZE, width), f32),
        4 * 2 * P_SIZE * early_rows * width,
        where,
        *[in_hbm(piece[0]) for piece in early],
        scratch=[
            pltpu.VMEM((early_rows, width), f32),
            pltpu.VMEM((2 * early_rows, width), b16),
            pltpu.SemaphoreType.DMA((len(early),)),
        ],
        hbm=len(early),
    )
    send, second, entries, second_big, second_small, taken = local_call(
        functools.partial(send_kernel, base=early_rows),
        (
            shape((half, wide), f32),
            shape((P_SIZE, k_local), f32),
            shape((P_SIZE, width - k_local), f32),
            shape((P_SIZE, k_local), b16),
            shape((P_SIZE, k_local), b16),
            shape((half, k_local), f32),
        ),
        8 * P_SIZE * late_rows * width + 6 * half * k_local * wide,
        where,
        weights,
        carry,
        lt_big,
        lt_small,
        *[pltpu.with_memory_space_constraint(piece[0], pltpu.VMEM) for piece in late],
        scratch=[pltpu.VMEM((2 * late_rows, width), b16)],
    )
    keep = local_call(
        keep_kernel,
        shape((half, wide), f32),
        6 * half * k_local * wide,
        taken,
        lt_big,
        lt_small,
        second_big,
        second_small,
    )
    summed = finish_sum(send, keep)
    update_second = local_call(
        second_kernel,
        shape((P_SIZE, tile_rows), f32),
        6 * P_SIZE * k_local * tile_rows,
        jnp.stack(quarters),
        second,
        lt_big,
        lt_small,
        scratch=[pltpu.VMEM((P_SIZE, tile_rows), f32)],
        smem=1,
    )
    w_first = a_first - summed[:, :tile_rows]
    l_first = couple(w_first, inv_d[0], inv_e[0], panel_pairs[0])
    w_crossed = entries[:, :blocks] - summed[:, tile_rows:].T
    crossed = couple_lanes(w_crossed, inv_d[0], inv_e[0], panel_pairs[0])
    plain = (((1,), (0,)), ((), ()))
    halves = []
    for low in (0, 2):
        rows = in_quarters(crossed, quarters[low : low + 2], blocks)
        part = update_second[low * blocks : (low + 2) * blocks]
        halves.append(part + lax.dot_general(rows, w_first, plain, precision=HIGH))
    w_second = a_second - finish_sum(*halves)
    l_second = couple(w_second, inv_d[1], inv_e[1], panel_pairs[1])
    return (l_first, l_second)


def solution(mesh):
    in_specs = (
        P("narrow", "wide"),
        P("narrow"),
        P("narrow"),
        P("narrow"),
        P(),
        P("narrow", "wide"),
        P("narrow", "wide"),
        P(None, "narrow"),
        P(None, "narrow"),
        P(None, "narrow"),
    )
    out_specs = (P("narrow", "wide"), P("narrow", "wide"))
    return jax.shard_map(shards, mesh=mesh, in_specs=in_specs, out_specs=out_specs, check_vma=False)
```

```python
import functools

import jax
import jax.numpy as jnp
from jax import lax
from jax.experimental import pallas as pl
from jax.experimental.pallas import tpu as pltpu
from jax.sharding import PartitionSpec as P

P_SIZE = 256
CAP = 16
NY, NZ, NH = 4, 8, 2
CORE = [(0, 1), (1, 0), (2, 3), (3, 2)]
CHIP = [(0, 2), (1, 3), (2, 0), (3, 1)]


def shift(dy, dz, dh):
    pairs = []
    for y in range(NY):
        for z in range(NZ):
            for h in range(NH):
                to = ((y + dy) % NY * NZ + (z + dz) % NZ) * NH + (h + dh) % NH
                pairs.append(((y * NZ + z) * NH + h, to))
    return pairs


def moved(block, offsets, step):
    got = lax.ppermute(block, "wide", shift(*step))
    return got, [
        ((y - step[0]) % NY, (z - step[1]) % NZ, (h - step[2]) % NH) for y, z, h in offsets
    ]


def gather_tiles(block, made):
    rows = block.shape[0]
    held, at = block, [(0, 0, 0)]
    got, its = moved(held, at, (0, 4, 0))
    held, at = jnp.concatenate([held, got], 0), at + its
    ready = made(got)
    parts = [moved(held, at, step) for step in ((2, 1, 0), (2, -1, 0), (0, 2, 0))]
    pair = 2 * rows
    blocks = [held] + [p[0] for p in parts]
    places = [(piece, 0, pair, 0, pair * i) for i, piece in enumerate(blocks)]
    places += [(blocks[i], 0, pair, 1, pair * i) for i in range(2)]
    held, low = cuts(places, [4 * pair, 2 * pair], ready[0])
    at = at + parts[0][1] + parts[1][1] + parts[2][1]
    half = len(at) // 2
    cut = half * rows
    over = moved(held, at, (0, 0, 1))
    ahead = moved(held, at, (1, 0, 0))
    behind = moved(held, at, (-1, 0, 0))
    up = moved(low, at[:half], (0, 1, 0))
    down = moved(low, at[:half], (0, -1, 0))
    early = [(held, at), ahead, behind, over, up, down]
    (middle,) = cuts([(over[0], 0, cut, 0, 0)], [cut])
    late = [
        moved(over[0], over[1], (1, 0, 0)),
        moved(over[0], over[1], (-1, 0, 0)),
        moved(middle, over[1][:half], (0, 1, 0)),
        moved(middle, over[1][:half], (0, -1, 0)),
    ]
    return early, late, ready


def in_hbm(value):
    return pltpu.with_memory_space_constraint(value, pltpu.HBM)


def cuts_kernel(*refs, parts, inputs):
    sems = refs[-1]
    outs = refs[inputs:-1]
    copies = []
    for i, (start, size, out, to) in enumerate(parts):
        copies.append(
            pltpu.make_async_copy(
                refs[i].at[pl.ds(start, size)], outs[out].at[pl.ds(to, size)], sems.at[i]
            )
        )
        copies[-1].start()
    for copy in copies:
        copy.wait()


def cuts(parts, sizes, following=None):
    args = [in_hbm(part[0]) for part in parts] + ([] if following is None else [following])
    width = parts[0][0].shape[1]
    return pl.pallas_call(
        functools.partial(cuts_kernel, parts=[part[1:] for part in parts], inputs=len(args)),
        in_specs=[pl.BlockSpec(memory_space=pl.ANY)] * len(args),
        out_specs=[pl.BlockSpec(memory_space=pltpu.VMEM)] * len(sizes),
        out_shape=[jax.ShapeDtypeStruct((size, width), jnp.float32) for size in sizes],
        scratch_shapes=[pltpu.SemaphoreType.DMA((len(parts),))],
        compiler_params=pltpu.CompilerParams(vmem_limit_bytes=20 * 2**20),
    )(*args)


def split(value):
    big = value.astype(jnp.bfloat16)
    return big, (value - big.astype(jnp.float32)).astype(jnp.bfloat16)


def dot3(left, right, dims):
    def dot(x, y):
        return lax.dot_general(x, y, (dims, ((), ())), preferred_element_type=jnp.float32)

    return dot(left[0], right[0]) + (dot(left[0], right[1]) + dot(left[1], right[0]))


def slots_kernel(low_ref, pivots_hbm, a_hbm, lt_ref, out_ref, lt_buf, pivots_ref, a_ref, sems, more):
    k_local, width = lt_ref.shape
    depth = k_local // sems.shape[0]
    copies = []
    small = [
        pltpu.make_async_copy(pivots_hbm, pivots_ref, more.at[0]),
        pltpu.make_async_copy(a_hbm, a_ref, more.at[1]),
    ]
    for copy in small:
        copy.start()
    for i in range(sems.shape[0]):
        rows = slice(i * depth, (i + 1) * depth)
        copies.append(pltpu.make_async_copy(lt_ref.at[rows], lt_buf.at[rows], sems.at[i]))
        copies[-1].start()
    small[0].wait()
    row = jnp.concatenate([pivots_ref[0:1, :], pivots_ref[1:2, :]], 1) - low_ref[0]
    count = row.shape[1]
    mine = (row >= 0) & (row < width)
    before = lax.broadcasted_iota(jnp.int32, (count, count), 0) < lax.broadcasted_iota(
        jnp.int32, (count, count), 1
    )
    ones = jnp.broadcast_to(jnp.where(mine, 1.0, 0.0), (16, count)).astype(jnp.bfloat16)
    rank = jnp.dot(
        ones, jnp.where(before, 1.0, 0.0).astype(jnp.bfloat16), preferred_element_type=jnp.float32
    )
    slot = lax.broadcasted_iota(jnp.int32, (128, count), 0).astype(jnp.float32)
    hit = (slot == rank[:1]) & mine
    offset = jnp.sum(jnp.where(hit, row + 1, 0).astype(jnp.float32), 1, keepdims=True) - 1.0
    column = lax.broadcasted_iota(jnp.int32, (128, width), 1).astype(jnp.float32)
    pick = jnp.where(column == offset, 1.0, 0.0).astype(jnp.bfloat16)
    across = (((1,), (1,)), ((), ()))

    def rows_of(value):
        total = None
        for _ in range(2):
            part = value.astype(jnp.bfloat16)
            value = value - part.astype(jnp.float32)
            got = lax.dot_general(part, pick, across, preferred_element_type=jnp.float32)
            total = got if total is None else total + got
        return total.T[:CAP]

    small[1].wait()
    extra = rows_of(a_ref[...])
    out_ref[:, k_local:] = jnp.concatenate([extra, jnp.zeros_like(extra)], 1)
    for i, copy in enumerate(copies):
        copy.wait()
        rows = slice(i * depth, (i + 1) * depth)
        out_ref[:, rows] = rows_of(lt_buf[rows, :])


def tile_slots(pivots, low, prior_lt, a_first):
    k_local, width = prior_lt.shape
    blocks = a_first.shape[0]
    vmem = pl.BlockSpec(memory_space=pltpu.VMEM)
    return pl.pallas_call(
        slots_kernel,
        in_specs=[
            pl.BlockSpec(memory_space=pltpu.SMEM),
            pl.BlockSpec(memory_space=pl.ANY),
            pl.BlockSpec(memory_space=pl.ANY),
            pl.BlockSpec(memory_space=pl.ANY),
        ],
        out_specs=vmem,
        out_shape=jax.ShapeDtypeStruct((CAP, k_local + 2 * blocks), jnp.float32),
        scratch_shapes=[
            pltpu.VMEM((k_local, width), jnp.float32),
            pltpu.VMEM(pivots.shape, jnp.int32),
            pltpu.VMEM((blocks, width), jnp.float32),
            pltpu.SemaphoreType.DMA((4,)),
            pltpu.SemaphoreType.DMA((2,)),
        ],
        compiler_params=pltpu.CompilerParams(vmem_limit_bytes=20 * 2**20),
    )(low.reshape(1), in_hbm(pivots), in_hbm(a_first), in_hbm(prior_lt))


def couple_kernel(weight_ref, lt_ref, after_ref, big_ref, small_ref):
    big_ref[...], small_ref[...] = split(couple_rows(lt_ref[...], weight_ref[...].T))


def coupled_parts(weights, prior_lt, following):
    k_local, width = prior_lt.shape
    depth = k_local // 4
    block = pl.BlockSpec((depth, width), lambda i: (i, 0))
    shape = jax.ShapeDtypeStruct((k_local, width), jnp.bfloat16)
    return pl.pallas_call(
        couple_kernel,
        grid=(4,),
        in_specs=[
            pl.BlockSpec((8, depth), lambda i: (0, i)),
            block,
            pl.BlockSpec(memory_space=pl.ANY),
        ],
        out_specs=(block, block),
        out_shape=(shape, shape),
        compiler_params=pltpu.CompilerParams(vmem_limit_bytes=20 * 2**20),
        cost_estimate=pl.CostEstimate(
            flops=8 * k_local * width, bytes_accessed=8 * k_local * width, transcendentals=0
        ),
    )(weights, in_hbm(prior_lt), following)


def fill_parts(parts_ref, pieces, rows_ref, sems):
    total = rows_ref.shape[0]
    start, copies = 0, []
    for i, ref in enumerate(pieces):
        rows = slice(start, start + ref.shape[0])
        copies.append((rows, pltpu.make_async_copy(ref, rows_ref.at[rows], sems.at[i])))
        copies[-1][1].start()
        start += ref.shape[0]
    for rows, copy in copies:
        copy.wait()
        big, small = split(rows_ref[rows, :])
        parts_ref[rows, :] = big
        parts_ref[total + rows.start : total + rows.stop, :] = small


def piece_scratch(rows, width, pieces):
    return [
        pltpu.VMEM((2 * rows, width), jnp.bfloat16),
        pltpu.VMEM((rows, width), jnp.float32),
        pltpu.SemaphoreType.DMA((len(pieces),)),
    ]


def hits(index, base, total):
    slot = base + lax.broadcasted_iota(jnp.int32, (index.shape[0], total), 1)
    hit = jnp.where(index == slot, 1.0, 0.0).astype(jnp.bfloat16)
    return jnp.concatenate([hit, hit], 1)


def early_kernel(index_ref, *refs):
    *pieces, out_ref, parts_ref, rows_ref, sems = refs
    hit = hits(index_ref[...], 0, rows_ref.shape[0])
    fill_parts(parts_ref, pieces, rows_ref, sems)
    for low in range(0, out_ref.shape[1], 384):
        out_ref[:, low : low + 384] = jnp.dot(
            hit, parts_ref[:, low : low + 384], preferred_element_type=jnp.float32
        )


def send_kernel(index_ref, weight_ref, carry_ref, lt_big_ref, lt_small_ref, *refs, base):
    *pieces, out_ref, second_ref, entries_ref, big_ref, small_ref, keep_ref, parts_ref, rows_ref, sems = refs
    fill_parts(parts_ref, pieces, rows_ref, sems)
    total = rows_ref.shape[0]
    rows, k_local = out_ref.shape[0], lt_big_ref.shape[0]
    tile_rows = lt_big_ref.shape[1]
    hit = hits(index_ref[...], base, total)
    taken = carry_ref[...] + jnp.dot(hit, parts_ref[...], preferred_element_type=jnp.float32)
    keep_ref[...] = taken[rows + P_SIZE :, :k_local]
    second = taken[rows : rows + P_SIZE]
    entries_ref[...] = second[:, k_local:]
    second = second[:, :k_local]
    second_ref[...] = second
    after = pltpu.roll(second, k_local - 1, 1)
    before = pltpu.roll(second, 1, 1)
    coupled = split(
        weight_ref[0:1, :] * second + weight_ref[1:2, :] * after + weight_ref[2:3, :] * before
    )
    big_ref[...] = coupled[0]
    small_ref[...] = coupled[1]
    first = split(taken[:rows, :k_local])
    out_ref[:, :tile_rows] = dot3(first, (lt_big_ref[...], lt_small_ref[...]), ((1,), (0,)))
    out_ref[:, tile_rows:] = dot3(first, coupled, ((1,), (1,)))


def keep_kernel(taken_ref, lt_big_ref, lt_small_ref, big_ref, small_ref, out_ref):
    tile_rows = lt_big_ref.shape[1]
    first = split(taken_ref[...])
    out_ref[:, :tile_rows] = dot3(first, (lt_big_ref[...], lt_small_ref[...]), ((1,), (0,)))
    out_ref[:, tile_rows:] = dot3(first, (big_ref[...], small_ref[...]), ((1,), (1,)))


def second_kernel(quarter_ref, second_ref, lt_big_ref, lt_small_ref, out_ref, whole_ref):
    blocks = out_ref.shape[0] // 4
    rows = split(second_ref[...])
    whole_ref[...] = dot3(rows, (lt_big_ref[...], lt_small_ref[...]), ((1,), (0,)))
    for i in range(4):
        start = pl.multiple_of(quarter_ref[i] * blocks, blocks)
        out_ref[i * blocks : (i + 1) * blocks, :] = whole_ref[pl.ds(start, blocks), :]


def local_call(kernel, out_shape, flops, *args, scratch=(), smem=0, hbm=0):
    vmem = pl.BlockSpec(memory_space=pltpu.VMEM)
    specs = [pl.BlockSpec(memory_space=pltpu.SMEM)] * smem + [vmem] * (len(args) - smem - hbm)
    specs += [pl.BlockSpec(memory_space=pl.ANY)] * hbm
    return pl.pallas_call(
        kernel,
        in_specs=specs,
        out_specs=jax.tree.map(lambda _: vmem, out_shape),
        out_shape=out_shape,
        scratch_shapes=list(scratch),
        compiler_params=pltpu.CompilerParams(vmem_limit_bytes=20 * 2**20),
        cost_estimate=pl.CostEstimate(
            flops=flops, bytes_accessed=4 * sum(x.size for x in args), transcendentals=0
        ),
    )(*args)


def quarter_order(me):
    core, chip = me % 2, me // 2
    return [(1 - chip) * 2 + 1 - core, chip * 2 + 1 - core, (1 - chip) * 2 + core, me]


def in_quarters(rows, quarters, blocks):
    return jnp.concatenate([lax.dynamic_slice_in_dim(rows, q * blocks, blocks) for q in quarters], 0)


def in_vmem(value):
    return pltpu.with_memory_space_constraint(value, pltpu.VMEM)


def add_kernel(keep_ref, got_ref, away_ref, rest_ref):
    half = away_ref.shape[0]
    away_ref[...] = keep_ref[:half, :] + got_ref[:half, :]
    rest_ref[...] = keep_ref[half:, :] + got_ref[half:, :]


def hop_sum(send, keep):
    got = lax.ppermute(send, "narrow", CORE)
    part = jax.ShapeDtypeStruct((keep.shape[0] // 2, keep.shape[1]), keep.dtype)
    away, rest = local_call(add_kernel, (part, part), keep.size, in_vmem(keep), in_vmem(got))
    return rest, lax.ppermute(away, "narrow", CHIP)


def couple_rows(value, weight):
    rows = value.shape[0]
    after = pltpu.roll(value, rows - 1, 0)
    before = pltpu.roll(value, 1, 0)
    return weight[:, 0:1] * value + weight[:, 1:2] * after + weight[:, 2:3] * before


def middle_kernel(
    quarter_ref, weight_ref, a_ref, entries_ref, update_ref, rest_ref, away_ref,
    out_ref, send_ref, keep_ref, turned_ref,
):
    blocks, tile_rows = a_ref.shape
    half = send_ref.shape[0]
    summed = rest_ref[...] + away_ref[...]
    weight = weight_ref[...].T[:blocks]
    w_first = a_ref[...] - summed[:, :tile_rows]
    out_ref[...] = couple_rows(w_first, weight)
    crossed = couple_rows(entries_ref[...].T[:blocks] - summed[:, tile_rows:], weight)
    turned_ref[:, :blocks] = crossed.T
    right = split(w_first)
    for i, ref in enumerate((send_ref, keep_ref)):
        left = [
            turned_ref[pl.ds(pl.multiple_of(quarter_ref[2 * i + j] * blocks, blocks), blocks), :blocks]
            for j in range(2)
        ]
        left = split(jnp.concatenate(left, 0))
        ref[...] = update_ref[i * half : (i + 1) * half, :] + dot3(left, right, ((1,), (0,)))


def last_kernel(weight_ref, a_ref, rest_ref, away_ref, out_ref):
    weight = weight_ref[...].T[: a_ref.shape[0]]
    out_ref[...] = couple_rows(a_ref[...] - (rest_ref[...] + away_ref[...]), weight)


def operator_rows(diag, off, pairs):
    joined = off * pairs.astype(jnp.float32)
    lower = jnp.concatenate([jnp.zeros_like(joined[:1]), joined[:-1]])
    rows = jnp.stack([diag, joined, lower])
    return jnp.pad(rows, ((0, 5), (0, -diag.shape[0] % 128)))


def shards(
    prior_lt, prior_d, prior_e, prior_pairs, pivots, a_first, a_second, inv_d, inv_e, panel_pairs
):
    k_local, tile_rows = prior_lt.shape
    blocks = a_first.shape[0]
    here = lax.axis_index("wide")
    flat = pivots.reshape(-1)
    tile = flat // tile_rows
    count = flat.shape[0]
    order = jnp.arange(count)
    rank = jnp.sum((tile[:, None] == tile[None, :]) & (order[None, :] < order[:, None]), 1)
    block = tile_slots(pivots, here * tile_rows, prior_lt, a_first)
    weights = operator_rows(prior_d, prior_e, prior_pairs)
    early, late, (lt_big, lt_small) = gather_tiles(
        block, lambda held: coupled_parts(weights, prior_lt, held)
    )
    offsets = [o for piece in early + late for o in piece[1]]
    ty, tz, th = tile // (NZ * NH), tile // NH % NZ, tile % NH
    hy, hz, hh = here // (NZ * NH), here // NH % NZ, here % NH
    rel = ((ty - hy) % NY * NZ + (tz - hz) % NZ) * NH + (th - hh) % NH
    place_of = [0] * (NY * NZ * NH)
    for i, (y, z, h) in enumerate(offsets):
        place_of[(y * NZ + z) * NH + h] = i
    place = jnp.sum(
        jnp.where(rel[:, None] == jnp.arange(NY * NZ * NH)[None, :], jnp.array(place_of)[None, :], 0), 1
    )
    where = place * CAP + rank
    quarters = quarter_order(lax.axis_index("narrow"))
    ordered = in_quarters(where[:P_SIZE], quarters, blocks)
    half = P_SIZE // 2
    where = jnp.concatenate([ordered[:half], where[P_SIZE:], ordered[half:]]).reshape(-1, 1)
    early_rows = CAP * sum(len(piece[1]) for piece in early)
    late_rows = CAP * sum(len(piece[1]) for piece in late)
    width = block.shape[1]
    wide = tile_rows + P_SIZE
    f32, b16 = jnp.float32, jnp.bfloat16
    shape = jax.ShapeDtypeStruct
    carry = local_call(
        early_kernel,
        shape((2 * P_SIZE, width), f32),
        4 * 2 * P_SIZE * early_rows * width,
        where,
        *[in_hbm(piece[0]) for piece in early],
        scratch=piece_scratch(early_rows, width, early),
        hbm=len(early),
    )
    send, second, entries, second_big, second_small, taken = local_call(
        functools.partial(send_kernel, base=early_rows),
        (
            shape((half, wide), f32),
            shape((P_SIZE, k_local), f32),
            shape((P_SIZE, width - k_local), f32),
            shape((P_SIZE, k_local), b16),
            shape((P_SIZE, k_local), b16),
            shape((half, k_local), f32),
        ),
        8 * P_SIZE * late_rows * width + 6 * half * k_local * wide,
        where,
        weights,
        carry,
        lt_big,
        lt_small,
        *[in_hbm(piece[0]) for piece in late],
        scratch=piece_scratch(late_rows, width, late),
        hbm=len(late),
    )
    keep = local_call(
        keep_kernel,
        shape((half, wide), f32),
        6 * half * k_local * wide,
        taken,
        lt_big,
        lt_small,
        second_big,
        second_small,
    )
    rest, away = hop_sum(send, keep)
    update_second = local_call(
        second_kernel,
        shape((P_SIZE, tile_rows), f32),
        6 * P_SIZE * k_local * tile_rows,
        jnp.stack(quarters),
        second,
        lt_big,
        lt_small,
        scratch=[pltpu.VMEM((P_SIZE, tile_rows), f32)],
        smem=1,
    )
    l_first, send, keep = local_call(
        middle_kernel,
        (shape((blocks, tile_rows), f32), shape((half, tile_rows), f32), shape((half, tile_rows), f32)),
        6 * P_SIZE * blocks * tile_rows,
        jnp.stack(quarters),
        operator_rows(inv_d[0], inv_e[0], panel_pairs[0]),
        a_first,
        entries,
        update_second,
        in_vmem(rest),
        in_vmem(away),
        scratch=[pltpu.VMEM((P_SIZE, 128), f32)],
        smem=1,
    )
    rest, away = hop_sum(send, keep)
    l_second = local_call(
        last_kernel,
        shape((blocks, tile_rows), f32),
        8 * blocks * tile_rows,
        operator_rows(inv_d[1], inv_e[1], panel_pairs[1]),
        a_second,
        in_vmem(rest),
        in_vmem(away),
    )
    return (l_first, l_second)


def solution(mesh):
    in_specs = (
        P("narrow", "wide"),
        P("narrow"),
        P("narrow"),
        P("narrow"),
        P(),
        P("narrow", "wide"),
        P("narrow", "wide"),
        P(None, "narrow"),
        P(None, "narrow"),
        P(None, "narrow"),
    )
    out_specs = (P("narrow", "wide"), P("narrow", "wide"))
    return jax.shard_map(shards, mesh=mesh, in_specs=in_specs, out_specs=out_specs, check_vma=False)
```

```python
import functools

import jax
import jax.numpy as jnp
from jax import lax
from jax.experimental import pallas as pl
from jax.experimental.pallas import tpu as pltpu
from jax.sharding import PartitionSpec as P

P_SIZE = 256
CAP = 16
NY, NZ, NH = 4, 8, 2
CORE = [(0, 1), (1, 0), (2, 3), (3, 2)]
CHIP = [(0, 2), (1, 3), (2, 0), (3, 1)]


def shift(dy, dz, dh):
    pairs = []
    for y in range(NY):
        for z in range(NZ):
            for h in range(NH):
                to = ((y + dy) % NY * NZ + (z + dz) % NZ) * NH + (h + dh) % NH
                pairs.append(((y * NZ + z) * NH + h, to))
    return pairs


def moved(block, offsets, step):
    got = lax.ppermute(block, "wide", shift(*step))
    return got, [
        ((y - step[0]) % NY, (z - step[1]) % NZ, (h - step[2]) % NH) for y, z, h in offsets
    ]


def gather_tiles(block, made):
    rows = block.shape[0]
    held, at = block, [(0, 0, 0)]
    got, its = moved(held, at, (0, 4, 0))
    held, at = jnp.concatenate([held, got], 0), at + its
    parts = [moved(held, at, step) for step in ((2, 1, 0), (2, -1, 0), (0, 2, 0))]
    held = jnp.concatenate([held] + [p[0] for p in parts], 0)
    at = at + parts[0][1] + parts[1][1] + parts[2][1]
    half = len(at) // 2
    cut = half * rows
    over = moved(held, at, (0, 0, 1))
    ahead = moved(held, at, (1, 0, 0))
    behind = moved(held, at, (-1, 0, 0))
    up = moved(held[:cut], at[:half], (0, 1, 0))
    down = moved(held[:cut], at[:half], (0, -1, 0))
    early = [(held, at), ahead, behind, over, up, down]
    ready = made(held)
    (middle,) = cuts([(over[0], 0, cut, 0, 0)], [cut], ready[0])
    late = [
        moved(over[0], over[1], (1, 0, 0)),
        moved(over[0], over[1], (-1, 0, 0)),
        moved(middle, over[1][:half], (0, 1, 0)),
        moved(middle, over[1][:half], (0, -1, 0)),
    ]
    return early, late, ready


def in_hbm(value):
    return pltpu.with_memory_space_constraint(value, pltpu.HBM)


def cuts_kernel(*refs, parts, inputs):
    sems = refs[-1]
    outs = refs[inputs:-1]
    copies = []
    for i, (start, size, out, to) in enumerate(parts):
        copies.append(
            pltpu.make_async_copy(
                refs[i].at[pl.ds(start, size)], outs[out].at[pl.ds(to, size)], sems.at[i]
            )
        )
        copies[-1].start()
    for copy in copies:
        copy.wait()


def cuts(parts, sizes, following=None):
    args = [in_vmem(part[0]) for part in parts] + ([] if following is None else [following])
    width = parts[0][0].shape[1]
    return pl.pallas_call(
        functools.partial(cuts_kernel, parts=[part[1:] for part in parts], inputs=len(args)),
        in_specs=[pl.BlockSpec(memory_space=pl.ANY)] * len(args),
        out_specs=[pl.BlockSpec(memory_space=pltpu.VMEM)] * len(sizes),
        out_shape=[jax.ShapeDtypeStruct((size, width), jnp.float32) for size in sizes],
        scratch_shapes=[pltpu.SemaphoreType.DMA((len(parts),))],
        compiler_params=pltpu.CompilerParams(vmem_limit_bytes=20 * 2**20),
    )(*args)


def split(value):
    big = value.astype(jnp.bfloat16)
    return big, (value - big.astype(jnp.float32)).astype(jnp.bfloat16)


def dot3(left, right, dims):
    def dot(x, y):
        return lax.dot_general(x, y, (dims, ((), ())), preferred_element_type=jnp.float32)

    return dot(left[0], right[0]) + (dot(left[0], right[1]) + dot(left[1], right[0]))


def slots_kernel(low_ref, pivots_hbm, a_hbm, lt_ref, out_ref, lt_buf, pivots_ref, a_ref, sems, more):
    k_local, width = lt_ref.shape
    depth = k_local // sems.shape[0]
    copies = []
    small = [
        pltpu.make_async_copy(pivots_hbm, pivots_ref, more.at[0]),
        pltpu.make_async_copy(a_hbm, a_ref, more.at[1]),
    ]
    for copy in small:
        copy.start()
    for i in range(sems.shape[0]):
        rows = slice(i * depth, (i + 1) * depth)
        copies.append(pltpu.make_async_copy(lt_ref.at[rows], lt_buf.at[rows], sems.at[i]))
        copies[-1].start()
    small[0].wait()
    row = jnp.concatenate([pivots_ref[0:1, :], pivots_ref[1:2, :]], 1) - low_ref[0]
    count = row.shape[1]
    mine = (row >= 0) & (row < width)
    before = lax.broadcasted_iota(jnp.int32, (count, count), 0) < lax.broadcasted_iota(
        jnp.int32, (count, count), 1
    )
    ones = jnp.broadcast_to(jnp.where(mine, 1.0, 0.0), (16, count)).astype(jnp.bfloat16)
    rank = jnp.dot(
        ones, jnp.where(before, 1.0, 0.0).astype(jnp.bfloat16), preferred_element_type=jnp.float32
    )
    slot = lax.broadcasted_iota(jnp.int32, (128, count), 0).astype(jnp.float32)
    hit = (slot == rank[:1]) & mine
    offset = jnp.sum(jnp.where(hit, row + 1, 0).astype(jnp.float32), 1, keepdims=True) - 1.0
    column = lax.broadcasted_iota(jnp.int32, (128, width), 1).astype(jnp.float32)
    pick = jnp.where(column == offset, 1.0, 0.0).astype(jnp.bfloat16)
    across = (((1,), (1,)), ((), ()))

    def rows_of(value):
        total = None
        for _ in range(2):
            part = value.astype(jnp.bfloat16)
            value = value - part.astype(jnp.float32)
            got = lax.dot_general(part, pick, across, preferred_element_type=jnp.float32)
            total = got if total is None else total + got
        return total.T[:CAP]

    small[1].wait()
    extra = rows_of(a_ref[...])
    out_ref[:, k_local:] = jnp.concatenate([extra, jnp.zeros_like(extra)], 1)
    for i, copy in enumerate(copies):
        copy.wait()
        rows = slice(i * depth, (i + 1) * depth)
        out_ref[:, rows] = rows_of(lt_buf[rows, :])


def tile_slots(pivots, low, prior_lt, a_first):
    k_local, width = prior_lt.shape
    blocks = a_first.shape[0]
    vmem = pl.BlockSpec(memory_space=pltpu.VMEM)
    return pl.pallas_call(
        slots_kernel,
        in_specs=[
            pl.BlockSpec(memory_space=pltpu.SMEM),
            pl.BlockSpec(memory_space=pl.ANY),
            pl.BlockSpec(memory_space=pl.ANY),
            pl.BlockSpec(memory_space=pl.ANY),
        ],
        out_specs=vmem,
        out_shape=jax.ShapeDtypeStruct((CAP, k_local + 2 * blocks), jnp.float32),
        scratch_shapes=[
            pltpu.VMEM((k_local, width), jnp.float32),
            pltpu.VMEM(pivots.shape, jnp.int32),
            pltpu.VMEM((blocks, width), jnp.float32),
            pltpu.SemaphoreType.DMA((4,)),
            pltpu.SemaphoreType.DMA((2,)),
        ],
        compiler_params=pltpu.CompilerParams(vmem_limit_bytes=20 * 2**20),
    )(low.reshape(1), in_hbm(pivots), in_hbm(a_first), in_hbm(prior_lt))


def couple_kernel(weight_ref, lt_ref, after_ref, big_ref, small_ref):
    big_ref[...], small_ref[...] = split(couple_rows(lt_ref[...], weight_ref[...].T))


def coupled_parts(weights, prior_lt, following):
    k_local, width = prior_lt.shape
    depth = k_local // 4
    block = pl.BlockSpec((depth, width), lambda i: (i, 0))
    shape = jax.ShapeDtypeStruct((k_local, width), jnp.bfloat16)
    return pl.pallas_call(
        couple_kernel,
        grid=(4,),
        in_specs=[
            pl.BlockSpec((8, depth), lambda i: (0, i)),
            block,
            pl.BlockSpec(memory_space=pl.ANY),
        ],
        out_specs=(block, block),
        out_shape=(shape, shape),
        compiler_params=pltpu.CompilerParams(vmem_limit_bytes=20 * 2**20),
        cost_estimate=pl.CostEstimate(
            flops=8 * k_local * width, bytes_accessed=8 * k_local * width, transcendentals=0
        ),
    )(weights, in_hbm(prior_lt), following)


def fill_parts(parts_ref, pieces):
    start, total = 0, parts_ref.shape[0] // 2
    for ref in pieces:
        size = ref.shape[0]
        big, small = split(ref[...])
        parts_ref[start : start + size, :] = big
        parts_ref[total + start : total + start + size, :] = small
        start += size


def hits(index, base, total):
    slot = base + lax.broadcasted_iota(jnp.int32, (index.shape[0], total), 1)
    hit = jnp.where(index == slot, 1.0, 0.0).astype(jnp.bfloat16)
    return jnp.concatenate([hit, hit], 1)


def early_kernel(index_ref, *refs):
    *pieces, out_ref, parts_ref = refs
    fill_parts(parts_ref, pieces)
    hit = hits(index_ref[...], 0, parts_ref.shape[0] // 2)
    for low in range(0, out_ref.shape[1], 384):
        out_ref[:, low : low + 384] = jnp.dot(
            hit, parts_ref[:, low : low + 384], preferred_element_type=jnp.float32
        )


def send_kernel(index_ref, weight_ref, carry_ref, lt_big_ref, lt_small_ref, *refs, base):
    *pieces, out_ref, second_ref, entries_ref, big_ref, small_ref, keep_ref, parts_ref = refs
    fill_parts(parts_ref, pieces)
    total = parts_ref.shape[0] // 2
    rows, k_local = out_ref.shape[0], lt_big_ref.shape[0]
    tile_rows = lt_big_ref.shape[1]
    hit = hits(index_ref[...], base, total)
    taken = carry_ref[...] + jnp.dot(hit, parts_ref[...], preferred_element_type=jnp.float32)
    keep_ref[...] = taken[rows + P_SIZE :, :k_local]
    second = taken[rows : rows + P_SIZE]
    entries_ref[...] = second[:, k_local:]
    second = second[:, :k_local]
    second_ref[...] = second
    after = pltpu.roll(second, k_local - 1, 1)
    before = pltpu.roll(second, 1, 1)
    coupled = split(
        weight_ref[0:1, :] * second + weight_ref[1:2, :] * after + weight_ref[2:3, :] * before
    )
    big_ref[...] = coupled[0]
    small_ref[...] = coupled[1]
    first = split(taken[:rows, :k_local])
    out_ref[:, :tile_rows] = dot3(first, (lt_big_ref[...], lt_small_ref[...]), ((1,), (0,)))
    out_ref[:, tile_rows:] = dot3(first, coupled, ((1,), (1,)))


def keep_kernel(taken_ref, lt_big_ref, lt_small_ref, big_ref, small_ref, out_ref):
    tile_rows = lt_big_ref.shape[1]
    first = split(taken_ref[...])
    out_ref[:, :tile_rows] = dot3(first, (lt_big_ref[...], lt_small_ref[...]), ((1,), (0,)))
    out_ref[:, tile_rows:] = dot3(first, (big_ref[...], small_ref[...]), ((1,), (1,)))


def second_kernel(quarter_ref, second_ref, lt_big_ref, lt_small_ref, out_ref, whole_ref):
    blocks = out_ref.shape[0] // 4
    rows = split(second_ref[...])
    whole_ref[...] = dot3(rows, (lt_big_ref[...], lt_small_ref[...]), ((1,), (0,)))
    for i in range(4):
        start = pl.multiple_of(quarter_ref[i] * blocks, blocks)
        out_ref[i * blocks : (i + 1) * blocks, :] = whole_ref[pl.ds(start, blocks), :]


def local_call(kernel, out_shape, flops, *args, scratch=(), smem=0):
    vmem = pl.BlockSpec(memory_space=pltpu.VMEM)
    specs = [pl.BlockSpec(memory_space=pltpu.SMEM)] * smem + [vmem] * (len(args) - smem)
    return pl.pallas_call(
        kernel,
        in_specs=specs,
        out_specs=jax.tree.map(lambda _: vmem, out_shape),
        out_shape=out_shape,
        scratch_shapes=list(scratch),
        compiler_params=pltpu.CompilerParams(vmem_limit_bytes=20 * 2**20),
        cost_estimate=pl.CostEstimate(
            flops=flops, bytes_accessed=4 * sum(x.size for x in args), transcendentals=0
        ),
    )(*args)


def quarter_order(me):
    core, chip = me % 2, me // 2
    return [(1 - chip) * 2 + 1 - core, chip * 2 + 1 - core, (1 - chip) * 2 + core, me]


def in_quarters(rows, quarters, blocks):
    return jnp.concatenate([lax.dynamic_slice_in_dim(rows, q * blocks, blocks) for q in quarters], 0)


def in_vmem(value):
    return pltpu.with_memory_space_constraint(value, pltpu.VMEM)


def add_kernel(keep_ref, got_ref, away_ref, rest_ref):
    half = away_ref.shape[0]
    away_ref[...] = keep_ref[:half, :] + got_ref[:half, :]
    rest_ref[...] = keep_ref[half:, :] + got_ref[half:, :]


def hop_sum(send, keep):
    got = lax.ppermute(send, "narrow", CORE)
    part = jax.ShapeDtypeStruct((keep.shape[0] // 2, keep.shape[1]), keep.dtype)
    away, rest = local_call(add_kernel, (part, part), keep.size, in_vmem(keep), in_vmem(got))
    return rest, lax.ppermute(away, "narrow", CHIP)


def couple_rows(value, weight):
    rows = value.shape[0]
    after = pltpu.roll(value, rows - 1, 0)
    before = pltpu.roll(value, 1, 0)
    return weight[:, 0:1] * value + weight[:, 1:2] * after + weight[:, 2:3] * before


def middle_kernel(
    quarter_ref, weight_ref, a_ref, entries_ref, update_ref, rest_ref, away_ref,
    out_ref, send_ref, keep_ref, turned_ref,
):
    blocks, tile_rows = a_ref.shape
    half = send_ref.shape[0]
    summed = rest_ref[...] + away_ref[...]
    weight = weight_ref[...].T[:blocks]
    w_first = a_ref[...] - summed[:, :tile_rows]
    out_ref[...] = couple_rows(w_first, weight)
    crossed = couple_rows(entries_ref[...].T[:blocks] - summed[:, tile_rows:], weight)
    turned_ref[:, :blocks] = crossed.T
    right = split(w_first)
    for i, ref in enumerate((send_ref, keep_ref)):
        left = [
            turned_ref[pl.ds(pl.multiple_of(quarter_ref[2 * i + j] * blocks, blocks), blocks), :blocks]
            for j in range(2)
        ]
        left = split(jnp.concatenate(left, 0))
        ref[...] = update_ref[i * half : (i + 1) * half, :] + dot3(left, right, ((1,), (0,)))


def last_kernel(weight_ref, a_ref, rest_ref, away_ref, out_ref):
    weight = weight_ref[...].T[: a_ref.shape[0]]
    out_ref[...] = couple_rows(a_ref[...] - (rest_ref[...] + away_ref[...]), weight)


def operator_rows(diag, off, pairs):
    joined = off * pairs.astype(jnp.float32)
    lower = jnp.concatenate([jnp.zeros_like(joined[:1]), joined[:-1]])
    rows = jnp.stack([diag, joined, lower])
    return jnp.pad(rows, ((0, 5), (0, -diag.shape[0] % 128)))


def shards(
    prior_lt, prior_d, prior_e, prior_pairs, pivots, a_first, a_second, inv_d, inv_e, panel_pairs
):
    k_local, tile_rows = prior_lt.shape
    blocks = a_first.shape[0]
    here = lax.axis_index("wide")
    flat = pivots.reshape(-1)
    tile = flat // tile_rows
    count = flat.shape[0]
    order = jnp.arange(count)
    rank = jnp.sum((tile[:, None] == tile[None, :]) & (order[None, :] < order[:, None]), 1)
    block = tile_slots(pivots, here * tile_rows, prior_lt, a_first)
    weights = operator_rows(prior_d, prior_e, prior_pairs)
    early, late, (lt_big, lt_small) = gather_tiles(
        block, lambda held: coupled_parts(weights, prior_lt, held)
    )
    offsets = [o for piece in early + late for o in piece[1]]
    ty, tz, th = tile // (NZ * NH), tile // NH % NZ, tile % NH
    hy, hz, hh = here // (NZ * NH), here // NH % NZ, here % NH
    rel = ((ty - hy) % NY * NZ + (tz - hz) % NZ) * NH + (th - hh) % NH
    place_of = [0] * (NY * NZ * NH)
    for i, (y, z, h) in enumerate(offsets):
        place_of[(y * NZ + z) * NH + h] = i
    place = jnp.sum(
        jnp.where(rel[:, None] == jnp.arange(NY * NZ * NH)[None, :], jnp.array(place_of)[None, :], 0), 1
    )
    where = place * CAP + rank
    quarters = quarter_order(lax.axis_index("narrow"))
    ordered = in_quarters(where[:P_SIZE], quarters, blocks)
    half = P_SIZE // 2
    where = jnp.concatenate([ordered[:half], where[P_SIZE:], ordered[half:]]).reshape(-1, 1)
    early_rows = CAP * sum(len(piece[1]) for piece in early)
    late_rows = CAP * sum(len(piece[1]) for piece in late)
    width = block.shape[1]
    wide = tile_rows + P_SIZE
    f32, b16 = jnp.float32, jnp.bfloat16
    shape = jax.ShapeDtypeStruct
    carry = local_call(
        early_kernel,
        shape((2 * P_SIZE, width), f32),
        4 * 2 * P_SIZE * early_rows * width,
        where,
        *[in_vmem(piece[0]) for piece in early],
        scratch=[pltpu.VMEM((2 * early_rows, width), b16)],
    )
    send, second, entries, second_big, second_small, taken = local_call(
        functools.partial(send_kernel, base=early_rows),
        (
            shape((half, wide), f32),
            shape((P_SIZE, k_local), f32),
            shape((P_SIZE, width - k_local), f32),
            shape((P_SIZE, k_local), b16),
            shape((P_SIZE, k_local), b16),
            shape((half, k_local), f32),
        ),
        8 * P_SIZE * late_rows * width + 6 * half * k_local * wide,
        where,
        weights,
        carry,
        lt_big,
        lt_small,
        *[in_vmem(piece[0]) for piece in late],
        scratch=[pltpu.VMEM((2 * late_rows, width), b16)],
    )
    keep = local_call(
        keep_kernel,
        shape((half, wide), f32),
        6 * half * k_local * wide,
        taken,
        lt_big,
        lt_small,
        second_big,
        second_small,
    )
    rest, away = hop_sum(send, keep)
    update_second = local_call(
        second_kernel,
        shape((P_SIZE, tile_rows), f32),
        6 * P_SIZE * k_local * tile_rows,
        jnp.stack(quarters),
        second,
        lt_big,
        lt_small,
        scratch=[pltpu.VMEM((P_SIZE, tile_rows), f32)],
        smem=1,
    )
    l_first, send, keep = local_call(
        middle_kernel,
        (shape((blocks, tile_rows), f32), shape((half, tile_rows), f32), shape((half, tile_rows), f32)),
        6 * P_SIZE * blocks * tile_rows,
        jnp.stack(quarters),
        operator_rows(inv_d[0], inv_e[0], panel_pairs[0]),
        a_first,
        entries,
        update_second,
        in_vmem(rest),
        in_vmem(away),
        scratch=[pltpu.VMEM((P_SIZE, 128), f32)],
        smem=1,
    )
    rest, away = hop_sum(send, keep)
    l_second = local_call(
        last_kernel,
        shape((blocks, tile_rows), f32),
        8 * blocks * tile_rows,
        operator_rows(inv_d[1], inv_e[1], panel_pairs[1]),
        a_second,
        in_vmem(rest),
        in_vmem(away),
    )
    return (l_first, l_second)


def solution(mesh):
    in_specs = (
        P("narrow", "wide"),
        P("narrow"),
        P("narrow"),
        P("narrow"),
        P(),
        P("narrow", "wide"),
        P("narrow", "wide"),
        P(None, "narrow"),
        P(None, "narrow"),
        P(None, "narrow"),
    )
    out_specs = (P("narrow", "wide"), P("narrow", "wide"))
    return jax.shard_map(shards, mesh=mesh, in_specs=in_specs, out_specs=out_specs, check_vma=False)
```

```python
import functools

import jax
import jax.numpy as jnp
from jax import lax
from jax.experimental import pallas as pl
from jax.experimental.pallas import tpu as pltpu
from jax.sharding import PartitionSpec as P

P_SIZE = 256
CAP = 16
NY, NZ, NH = 4, 8, 2
CORE = [(0, 1), (1, 0), (2, 3), (3, 2)]
CHIP = [(0, 2), (1, 3), (2, 0), (3, 1)]


def shift(dy, dz, dh):
    pairs = []
    for y in range(NY):
        for z in range(NZ):
            for h in range(NH):
                to = ((y + dy) % NY * NZ + (z + dz) % NZ) * NH + (h + dh) % NH
                pairs.append(((y * NZ + z) * NH + h, to))
    return pairs


def moved(block, offsets, step):
    got = lax.ppermute(block, "wide", shift(*step))
    return got, [
        ((y - step[0]) % NY, (z - step[1]) % NZ, (h - step[2]) % NH) for y, z, h in offsets
    ]


def gather_tiles(block, made):
    rows = block.shape[0]
    held, at = block, [(0, 0, 0)]
    got, its = moved(held, at, (0, 4, 0))
    held, at = jnp.concatenate([held, got], 0), at + its
    ready = [in_hbm(part) for part in made(got)]
    parts = [moved(held, at, step) for step in ((2, 1, 0), (2, -1, 0), (0, 2, 0))]
    pair = 2 * rows
    pieces = [held] + [p[0] for p in parts]
    places = [(piece, 0, pair, 0, pair * i) for i, piece in enumerate(pieces)]
    places += [(pieces[i], 0, pair, 1, pair * i) for i in range(2)]
    held, low = cuts(places, [4 * pair, 2 * pair], ready[0])
    at = at + parts[0][1] + parts[1][1] + parts[2][1]
    half = len(at) // 2
    cut = half * rows
    over = moved(held, at, (0, 0, 1))
    ahead = moved(held, at, (1, 0, 0))
    behind = moved(held, at, (-1, 0, 0))
    up = moved(low, at[:half], (0, 1, 0))
    down = moved(low, at[:half], (0, -1, 0))
    early = [(held, at), ahead, behind, over, up, down]
    (middle,) = cuts([(over[0], 0, cut, 0, 0)], [cut])
    late = [
        moved(over[0], over[1], (1, 0, 0)),
        moved(over[0], over[1], (-1, 0, 0)),
        moved(middle, over[1][:half], (0, 1, 0)),
        moved(middle, over[1][:half], (0, -1, 0)),
    ]
    return early, late, ready


def in_hbm(value):
    return pltpu.with_memory_space_constraint(value, pltpu.HBM)


def cuts_kernel(*refs, parts, inputs):
    sems = refs[-1]
    outs = refs[inputs:-1]
    copies = []
    for i, (start, size, out, to) in enumerate(parts):
        copies.append(
            pltpu.make_async_copy(
                refs[i].at[pl.ds(start, size)], outs[out].at[pl.ds(to, size)], sems.at[i]
            )
        )
        copies[-1].start()
    for copy in copies:
        copy.wait()


def cuts(parts, sizes, following=None):
    args = [in_vmem(part[0]) for part in parts] + ([] if following is None else [following])
    width = parts[0][0].shape[1]
    return pl.pallas_call(
        functools.partial(cuts_kernel, parts=[part[1:] for part in parts], inputs=len(args)),
        in_specs=[pl.BlockSpec(memory_space=pl.ANY)] * len(args),
        out_specs=[pl.BlockSpec(memory_space=pltpu.VMEM)] * len(sizes),
        out_shape=[jax.ShapeDtypeStruct((size, width), jnp.float32) for size in sizes],
        scratch_shapes=[pltpu.SemaphoreType.DMA((len(parts),))],
        compiler_params=pltpu.CompilerParams(vmem_limit_bytes=20 * 2**20),
    )(*args)


def split(value):
    big = value.astype(jnp.bfloat16)
    return big, (value - big.astype(jnp.float32)).astype(jnp.bfloat16)


def dot3(left, right, dims):
    def dot(x, y):
        return lax.dot_general(x, y, (dims, ((), ())), preferred_element_type=jnp.float32)

    return dot(left[0], right[0]) + (dot(left[0], right[1]) + dot(left[1], right[0]))


def slots_kernel(low_ref, pivots_hbm, a_hbm, lt_ref, out_ref, lt_buf, pivots_ref, a_ref, sems, more):
    k_local, width = lt_ref.shape
    depth = k_local // sems.shape[0]
    copies = []
    small = [
        pltpu.make_async_copy(pivots_hbm, pivots_ref, more.at[0]),
        pltpu.make_async_copy(a_hbm, a_ref, more.at[1]),
    ]
    for copy in small:
        copy.start()
    for i in range(sems.shape[0]):
        rows = slice(i * depth, (i + 1) * depth)
        copies.append(pltpu.make_async_copy(lt_ref.at[rows], lt_buf.at[rows], sems.at[i]))
        copies[-1].start()
    small[0].wait()
    row = jnp.concatenate([pivots_ref[0:1, :], pivots_ref[1:2, :]], 1) - low_ref[0]
    count = row.shape[1]
    mine = (row >= 0) & (row < width)
    before = lax.broadcasted_iota(jnp.int32, (count, count), 0) < lax.broadcasted_iota(
        jnp.int32, (count, count), 1
    )
    ones = jnp.broadcast_to(jnp.where(mine, 1.0, 0.0), (16, count)).astype(jnp.bfloat16)
    rank = jnp.dot(
        ones, jnp.where(before, 1.0, 0.0).astype(jnp.bfloat16), preferred_element_type=jnp.float32
    )
    slot = lax.broadcasted_iota(jnp.int32, (128, count), 0).astype(jnp.float32)
    hit = (slot == rank[:1]) & mine
    offset = jnp.sum(jnp.where(hit, row + 1, 0).astype(jnp.float32), 1, keepdims=True) - 1.0
    column = lax.broadcasted_iota(jnp.int32, (128, width), 1).astype(jnp.float32)
    pick = jnp.where(column == offset, 1.0, 0.0).astype(jnp.bfloat16)
    across = (((1,), (1,)), ((), ()))

    def rows_of(value):
        total = None
        for _ in range(2):
            part = value.astype(jnp.bfloat16)
            value = value - part.astype(jnp.float32)
            got = lax.dot_general(part, pick, across, preferred_element_type=jnp.float32)
            total = got if total is None else total + got
        return total.T[:CAP]

    small[1].wait()
    extra = rows_of(a_ref[...])
    out_ref[:, k_local:] = jnp.concatenate([extra, jnp.zeros_like(extra)], 1)
    for i, copy in enumerate(copies):
        copy.wait()
        rows = slice(i * depth, (i + 1) * depth)
        out_ref[:, rows] = rows_of(lt_buf[rows, :])


def tile_slots(pivots, low, prior_lt, a_first):
    k_local, width = prior_lt.shape
    blocks = a_first.shape[0]
    vmem = pl.BlockSpec(memory_space=pltpu.VMEM)
    return pl.pallas_call(
        slots_kernel,
        in_specs=[
            pl.BlockSpec(memory_space=pltpu.SMEM),
            pl.BlockSpec(memory_space=pl.ANY),
            pl.BlockSpec(memory_space=pl.ANY),
            pl.BlockSpec(memory_space=pl.ANY),
        ],
        out_specs=vmem,
        out_shape=jax.ShapeDtypeStruct((CAP, k_local + 2 * blocks), jnp.float32),
        scratch_shapes=[
            pltpu.VMEM((k_local, width), jnp.float32),
            pltpu.VMEM(pivots.shape, jnp.int32),
            pltpu.VMEM((blocks, width), jnp.float32),
            pltpu.SemaphoreType.DMA((4,)),
            pltpu.SemaphoreType.DMA((2,)),
        ],
        compiler_params=pltpu.CompilerParams(vmem_limit_bytes=20 * 2**20),
    )(low.reshape(1), in_hbm(pivots), in_hbm(a_first), in_hbm(prior_lt))


def couple_kernel(weight_ref, lt_ref, after_ref, big_ref, small_ref):
    big_ref[...], small_ref[...] = split(couple_rows(lt_ref[...], weight_ref[...].T))


def coupled_parts(weights, prior_lt, following):
    k_local, width = prior_lt.shape
    depth = k_local // 4
    block = pl.BlockSpec((depth, width), lambda i: (i, 0))
    shape = jax.ShapeDtypeStruct((k_local, width), jnp.bfloat16)
    return pl.pallas_call(
        couple_kernel,
        grid=(4,),
        in_specs=[
            pl.BlockSpec((8, depth), lambda i: (0, i)),
            block,
            pl.BlockSpec(memory_space=pl.ANY),
        ],
        out_specs=(block, block),
        out_shape=(shape, shape),
        compiler_params=pltpu.CompilerParams(vmem_limit_bytes=20 * 2**20),
        cost_estimate=pl.CostEstimate(
            flops=8 * k_local * width, bytes_accessed=8 * k_local * width, transcendentals=0
        ),
    )(weights, in_hbm(prior_lt), following)


def fill_parts(parts_ref, pieces):
    start, total = 0, parts_ref.shape[0] // 2
    for ref in pieces:
        size = ref.shape[0]
        big, small = split(ref[...])
        parts_ref[start : start + size, :] = big
        parts_ref[total + start : total + start + size, :] = small
        start += size


def hits(index, base, total):
    slot = base + lax.broadcasted_iota(jnp.int32, (index.shape[0], total), 1)
    hit = jnp.where(index == slot, 1.0, 0.0).astype(jnp.bfloat16)
    return jnp.concatenate([hit, hit], 1)


def early_kernel(index_ref, *refs):
    *pieces, big_in, small_in, out_ref, big_out, small_out, parts_ref, sems = refs
    copies = [
        pltpu.make_async_copy(big_in, big_out, sems.at[0]),
        pltpu.make_async_copy(small_in, small_out, sems.at[1]),
    ]
    for copy in copies:
        copy.start()
    fill_parts(parts_ref, pieces)
    hit = hits(index_ref[...], 0, parts_ref.shape[0] // 2)
    for low in range(0, out_ref.shape[1], 384):
        out_ref[:, low : low + 384] = jnp.dot(
            hit, parts_ref[:, low : low + 384], preferred_element_type=jnp.float32
        )
    for copy in copies:
        copy.wait()


def send_kernel(index_ref, weight_ref, carry_ref, lt_big_ref, lt_small_ref, *refs, base):
    *pieces, out_ref, second_ref, entries_ref, big_ref, small_ref, keep_ref, parts_ref = refs
    fill_parts(parts_ref, pieces)
    total = parts_ref.shape[0] // 2
    rows, k_local = out_ref.shape[0], lt_big_ref.shape[0]
    tile_rows = lt_big_ref.shape[1]
    hit = hits(index_ref[...], base, total)
    taken = carry_ref[...] + jnp.dot(hit, parts_ref[...], preferred_element_type=jnp.float32)
    keep_ref[...] = taken[rows + P_SIZE :, :k_local]
    second = taken[rows : rows + P_SIZE]
    entries_ref[...] = second[:, k_local:]
    second = second[:, :k_local]
    second_ref[...] = second
    after = pltpu.roll(second, k_local - 1, 1)
    before = pltpu.roll(second, 1, 1)
    coupled = split(
        weight_ref[0:1, :] * second + weight_ref[1:2, :] * after + weight_ref[2:3, :] * before
    )
    big_ref[...] = coupled[0]
    small_ref[...] = coupled[1]
    first = split(taken[:rows, :k_local])
    out_ref[:, :tile_rows] = dot3(first, (lt_big_ref[...], lt_small_ref[...]), ((1,), (0,)))
    out_ref[:, tile_rows:] = dot3(first, coupled, ((1,), (1,)))


def keep_kernel(taken_ref, lt_big_ref, lt_small_ref, big_ref, small_ref, out_ref):
    tile_rows = lt_big_ref.shape[1]
    first = split(taken_ref[...])
    out_ref[:, :tile_rows] = dot3(first, (lt_big_ref[...], lt_small_ref[...]), ((1,), (0,)))
    out_ref[:, tile_rows:] = dot3(first, (big_ref[...], small_ref[...]), ((1,), (1,)))


def second_kernel(quarter_ref, second_ref, lt_big_ref, lt_small_ref, out_ref, whole_ref):
    blocks = out_ref.shape[0] // 4
    rows = split(second_ref[...])
    whole_ref[...] = dot3(rows, (lt_big_ref[...], lt_small_ref[...]), ((1,), (0,)))
    for i in range(4):
        start = pl.multiple_of(quarter_ref[i] * blocks, blocks)
        out_ref[i * blocks : (i + 1) * blocks, :] = whole_ref[pl.ds(start, blocks), :]


def local_call(kernel, out_shape, flops, *args, scratch=(), smem=0, hbm=0):
    vmem = pl.BlockSpec(memory_space=pltpu.VMEM)
    specs = [pl.BlockSpec(memory_space=pltpu.SMEM)] * smem + [vmem] * (len(args) - smem - hbm)
    specs += [pl.BlockSpec(memory_space=pl.ANY)] * hbm
    return pl.pallas_call(
        kernel,
        in_specs=specs,
        out_specs=jax.tree.map(lambda _: vmem, out_shape),
        out_shape=out_shape,
        scratch_shapes=list(scratch),
        compiler_params=pltpu.CompilerParams(vmem_limit_bytes=20 * 2**20),
        cost_estimate=pl.CostEstimate(
            flops=flops, bytes_accessed=4 * sum(x.size for x in args), transcendentals=0
        ),
    )(*args)


def quarter_order(me):
    core, chip = me % 2, me // 2
    return [(1 - chip) * 2 + 1 - core, chip * 2 + 1 - core, (1 - chip) * 2 + core, me]


def in_quarters(rows, quarters, blocks):
    return jnp.concatenate([lax.dynamic_slice_in_dim(rows, q * blocks, blocks) for q in quarters], 0)


def in_vmem(value):
    return pltpu.with_memory_space_constraint(value, pltpu.VMEM)


def add_kernel(keep_ref, got_ref, away_ref, rest_ref):
    half = away_ref.shape[0]
    away_ref[...] = keep_ref[:half, :] + got_ref[:half, :]
    rest_ref[...] = keep_ref[half:, :] + got_ref[half:, :]


def hop_sum(send, keep):
    got = lax.ppermute(send, "narrow", CORE)
    part = jax.ShapeDtypeStruct((keep.shape[0] // 2, keep.shape[1]), keep.dtype)
    away, rest = local_call(add_kernel, (part, part), keep.size, in_vmem(keep), in_vmem(got))
    return rest, lax.ppermute(away, "narrow", CHIP)


def couple_rows(value, weight):
    rows = value.shape[0]
    after = pltpu.roll(value, rows - 1, 0)
    before = pltpu.roll(value, 1, 0)
    return weight[:, 0:1] * value + weight[:, 1:2] * after + weight[:, 2:3] * before


def middle_kernel(
    quarter_ref, weight_ref, a_ref, entries_ref, update_ref, rest_ref, away_ref,
    out_ref, send_ref, keep_ref, turned_ref,
):
    blocks, tile_rows = a_ref.shape
    half = send_ref.shape[0]
    summed = rest_ref[...] + away_ref[...]
    weight = weight_ref[...].T[:blocks]
    w_first = a_ref[...] - summed[:, :tile_rows]
    out_ref[...] = couple_rows(w_first, weight)
    crossed = couple_rows(entries_ref[...].T[:blocks] - summed[:, tile_rows:], weight)
    turned_ref[:, :blocks] = crossed.T
    right = split(w_first)
    for i, ref in enumerate((send_ref, keep_ref)):
        left = [
            turned_ref[pl.ds(pl.multiple_of(quarter_ref[2 * i + j] * blocks, blocks), blocks), :blocks]
            for j in range(2)
        ]
        left = split(jnp.concatenate(left, 0))
        ref[...] = update_ref[i * half : (i + 1) * half, :] + dot3(left, right, ((1,), (0,)))


def last_kernel(weight_ref, a_ref, rest_ref, away_ref, out_ref):
    weight = weight_ref[...].T[: a_ref.shape[0]]
    out_ref[...] = couple_rows(a_ref[...] - (rest_ref[...] + away_ref[...]), weight)


def operator_rows(diag, off, pairs):
    joined = off * pairs.astype(jnp.float32)
    lower = jnp.concatenate([jnp.zeros_like(joined[:1]), joined[:-1]])
    rows = jnp.stack([diag, joined, lower])
    return jnp.pad(rows, ((0, 5), (0, -diag.shape[0] % 128)))


def shards(
    prior_lt, prior_d, prior_e, prior_pairs, pivots, a_first, a_second, inv_d, inv_e, panel_pairs
):
    k_local, tile_rows = prior_lt.shape
    blocks = a_first.shape[0]
    here = lax.axis_index("wide")
    flat = pivots.reshape(-1)
    tile = flat // tile_rows
    count = flat.shape[0]
    order = jnp.arange(count)
    rank = jnp.sum((tile[:, None] == tile[None, :]) & (order[None, :] < order[:, None]), 1)
    block = tile_slots(pivots, here * tile_rows, prior_lt, a_first)
    weights = operator_rows(prior_d, prior_e, prior_pairs)
    early, late, parts = gather_tiles(
        block, lambda held: coupled_parts(weights, prior_lt, held)
    )
    offsets = [o for piece in early + late for o in piece[1]]
    ty, tz, th = tile // (NZ * NH), tile // NH % NZ, tile % NH
    hy, hz, hh = here // (NZ * NH), here // NH % NZ, here % NH
    rel = ((ty - hy) % NY * NZ + (tz - hz) % NZ) * NH + (th - hh) % NH
    place_of = [0] * (NY * NZ * NH)
    for i, (y, z, h) in enumerate(offsets):
        place_of[(y * NZ + z) * NH + h] = i
    place = jnp.sum(
        jnp.where(rel[:, None] == jnp.arange(NY * NZ * NH)[None, :], jnp.array(place_of)[None, :], 0), 1
    )
    where = place * CAP + rank
    quarters = quarter_order(lax.axis_index("narrow"))
    ordered = in_quarters(where[:P_SIZE], quarters, blocks)
    half = P_SIZE // 2
    where = jnp.concatenate([ordered[:half], where[P_SIZE:], ordered[half:]]).reshape(-1, 1)
    early_rows = CAP * sum(len(piece[1]) for piece in early)
    late_rows = CAP * sum(len(piece[1]) for piece in late)
    width = block.shape[1]
    wide = tile_rows + P_SIZE
    f32, b16 = jnp.float32, jnp.bfloat16
    shape = jax.ShapeDtypeStruct
    part = shape((k_local, tile_rows), b16)
    carry, lt_big, lt_small = local_call(
        early_kernel,
        (shape((2 * P_SIZE, width), f32), part, part),
        4 * 2 * P_SIZE * early_rows * width,
        where,
        *[in_vmem(piece[0]) for piece in early],
        *parts,
        scratch=[pltpu.VMEM((2 * early_rows, width), b16), pltpu.SemaphoreType.DMA((2,))],
        hbm=2,
    )
    send, second, entries, second_big, second_small, taken = local_call(
        functools.partial(send_kernel, base=early_rows),
        (
            shape((half, wide), f32),
            shape((P_SIZE, k_local), f32),
            shape((P_SIZE, width - k_local), f32),
            shape((P_SIZE, k_local), b16),
            shape((P_SIZE, k_local), b16),
            shape((half, k_local), f32),
        ),
        8 * P_SIZE * late_rows * width + 6 * half * k_local * wide,
        where,
        weights,
        carry,
        lt_big,
        lt_small,
        *[in_vmem(piece[0]) for piece in late],
        scratch=[pltpu.VMEM((2 * late_rows, width), b16)],
    )
    keep = local_call(
        keep_kernel,
        shape((half, wide), f32),
        6 * half * k_local * wide,
        taken,
        lt_big,
        lt_small,
        second_big,
        second_small,
    )
    rest, away = hop_sum(send, keep)
    update_second = local_call(
        second_kernel,
        shape((P_SIZE, tile_rows), f32),
        6 * P_SIZE * k_local * tile_rows,
        jnp.stack(quarters),
        second,
        lt_big,
        lt_small,
        scratch=[pltpu.VMEM((P_SIZE, tile_rows), f32)],
        smem=1,
    )
    l_first, send, keep = local_call(
        middle_kernel,
        (shape((blocks, tile_rows), f32), shape((half, tile_rows), f32), shape((half, tile_rows), f32)),
        6 * P_SIZE * blocks * tile_rows,
        jnp.stack(quarters),
        operator_rows(inv_d[0], inv_e[0], panel_pairs[0]),
        a_first,
        entries,
        update_second,
        in_vmem(rest),
        in_vmem(away),
        scratch=[pltpu.VMEM((P_SIZE, 128), f32)],
        smem=1,
    )
    rest, away = hop_sum(send, keep)
    l_second = local_call(
        last_kernel,
        shape((blocks, tile_rows), f32),
        8 * blocks * tile_rows,
        operator_rows(inv_d[1], inv_e[1], panel_pairs[1]),
        a_second,
        in_vmem(rest),
        in_vmem(away),
    )
    return (l_first, l_second)


def solution(mesh):
    in_specs = (
        P("narrow", "wide"),
        P("narrow"),
        P("narrow"),
        P("narrow"),
        P(),
        P("narrow", "wide"),
        P("narrow", "wide"),
        P(None, "narrow"),
        P(None, "narrow"),
        P(None, "narrow"),
    )
    out_specs = (P("narrow", "wide"), P("narrow", "wide"))
    return jax.shard_map(shards, mesh=mesh, in_specs=in_specs, out_specs=out_specs, check_vma=False)
```

```python
import functools

import jax
import jax.numpy as jnp
from jax import lax
from jax.experimental import pallas as pl
from jax.experimental.pallas import tpu as pltpu
from jax.sharding import PartitionSpec as P

P_SIZE = 256
CAP = 16
NY, NZ, NH = 4, 8, 2
CORE = [(0, 1), (1, 0), (2, 3), (3, 2)]
CHIP = [(0, 2), (1, 3), (2, 0), (3, 1)]


def shift(dy, dz, dh):
    pairs = []
    for y in range(NY):
        for z in range(NZ):
            for h in range(NH):
                to = ((y + dy) % NY * NZ + (z + dz) % NZ) * NH + (h + dh) % NH
                pairs.append(((y * NZ + z) * NH + h, to))
    return pairs


def moved(block, offsets, step):
    got = lax.ppermute(block, "wide", shift(*step))
    return got, [
        ((y - step[0]) % NY, (z - step[1]) % NZ, (h - step[2]) % NH) for y, z, h in offsets
    ]


def gather_tiles(block, made):
    rows = block.shape[0]
    held, at = block, [(0, 0, 0)]
    got, its = moved(held, at, (0, 4, 0))
    held, at = jnp.concatenate([held, got], 0), at + its
    parts = [moved(held, at, step) for step in ((2, 1, 0), (2, -1, 0), (0, 2, 0))]
    held = jnp.concatenate([held] + [p[0] for p in parts], 0)
    at = at + parts[0][1] + parts[1][1] + parts[2][1]
    half = len(at) // 2
    cut = half * rows
    over = moved(held, at, (0, 0, 1))
    ahead = moved(held, at, (1, 0, 0))
    behind = moved(held, at, (-1, 0, 0))
    up = moved(held[:cut], at[:half], (0, 1, 0))
    down = moved(held[:cut], at[:half], (0, -1, 0))
    early = [(held, at), ahead, behind, over, up, down]
    ready = made(held)
    (middle,) = cuts([(over[0], 0, cut, 0, 0)], [cut])
    late = [
        moved(over[0], over[1], (1, 0, 0)),
        moved(over[0], over[1], (-1, 0, 0)),
        moved(middle, over[1][:half], (0, 1, 0)),
        moved(middle, over[1][:half], (0, -1, 0)),
    ]
    return early, late, ready


def in_hbm(value):
    return pltpu.with_memory_space_constraint(value, pltpu.HBM)


def cuts_kernel(*refs, parts, inputs):
    sems = refs[-1]
    outs = refs[inputs:-1]
    copies = []
    for i, (start, size, out, to) in enumerate(parts):
        copies.append(
            pltpu.make_async_copy(
                refs[i].at[pl.ds(start, size)], outs[out].at[pl.ds(to, size)], sems.at[i]
            )
        )
        copies[-1].start()
    for copy in copies:
        copy.wait()


def cuts(parts, sizes, following=None):
    args = [in_vmem(part[0]) for part in parts] + ([] if following is None else [following])
    width = parts[0][0].shape[1]
    return pl.pallas_call(
        functools.partial(cuts_kernel, parts=[part[1:] for part in parts], inputs=len(args)),
        in_specs=[pl.BlockSpec(memory_space=pl.ANY)] * len(args),
        out_specs=[pl.BlockSpec(memory_space=pltpu.VMEM)] * len(sizes),
        out_shape=[jax.ShapeDtypeStruct((size, width), jnp.float32) for size in sizes],
        scratch_shapes=[pltpu.SemaphoreType.DMA((len(parts),))],
        compiler_params=pltpu.CompilerParams(vmem_limit_bytes=20 * 2**20),
    )(*args)


def split(value):
    big = value.astype(jnp.bfloat16)
    return big, (value - big.astype(jnp.float32)).astype(jnp.bfloat16)


def dot3(left, right, dims):
    def dot(x, y):
        return lax.dot_general(x, y, (dims, ((), ())), preferred_element_type=jnp.float32)

    return dot(left[0], right[0]) + (dot(left[0], right[1]) + dot(left[1], right[0]))


def slots_kernel(low_ref, pivots_hbm, a_hbm, lt_ref, out_ref, lt_buf, pivots_ref, a_ref, sems, more):
    k_local, width = lt_ref.shape
    depth = k_local // sems.shape[0]
    copies = []
    small = [
        pltpu.make_async_copy(pivots_hbm, pivots_ref, more.at[0]),
        pltpu.make_async_copy(a_hbm, a_ref, more.at[1]),
    ]
    for copy in small:
        copy.start()
    for i in range(sems.shape[0]):
        rows = slice(i * depth, (i + 1) * depth)
        copies.append(pltpu.make_async_copy(lt_ref.at[rows], lt_buf.at[rows], sems.at[i]))
        copies[-1].start()
    small[0].wait()
    row = jnp.concatenate([pivots_ref[0:1, :], pivots_ref[1:2, :]], 1) - low_ref[0]
    count = row.shape[1]
    mine = (row >= 0) & (row < width)
    before = lax.broadcasted_iota(jnp.int32, (count, count), 0) < lax.broadcasted_iota(
        jnp.int32, (count, count), 1
    )
    ones = jnp.broadcast_to(jnp.where(mine, 1.0, 0.0), (16, count)).astype(jnp.bfloat16)
    rank = jnp.dot(
        ones, jnp.where(before, 1.0, 0.0).astype(jnp.bfloat16), preferred_element_type=jnp.float32
    )
    slot = lax.broadcasted_iota(jnp.int32, (128, count), 0).astype(jnp.float32)
    hit = (slot == rank[:1]) & mine
    offset = jnp.sum(jnp.where(hit, row + 1, 0).astype(jnp.float32), 1, keepdims=True) - 1.0
    column = lax.broadcasted_iota(jnp.int32, (128, width), 1).astype(jnp.float32)
    pick = jnp.where(column == offset, 1.0, 0.0).astype(jnp.bfloat16)
    across = (((1,), (1,)), ((), ()))

    def rows_of(value):
        total = None
        for _ in range(2):
            part = value.astype(jnp.bfloat16)
            value = value - part.astype(jnp.float32)
            got = lax.dot_general(part, pick, across, preferred_element_type=jnp.float32)
            total = got if total is None else total + got
        return total.T[:CAP]

    small[1].wait()
    extra = rows_of(a_ref[...])
    out_ref[:, k_local:] = jnp.concatenate([extra, jnp.zeros_like(extra)], 1)
    for i, copy in enumerate(copies):
        copy.wait()
        rows = slice(i * depth, (i + 1) * depth)
        out_ref[:, rows] = rows_of(lt_buf[rows, :])


def tile_slots(pivots, low, prior_lt, a_first):
    k_local, width = prior_lt.shape
    blocks = a_first.shape[0]
    vmem = pl.BlockSpec(memory_space=pltpu.VMEM)
    return pl.pallas_call(
        slots_kernel,
        in_specs=[
            pl.BlockSpec(memory_space=pltpu.SMEM),
            pl.BlockSpec(memory_space=pl.ANY),
            pl.BlockSpec(memory_space=pl.ANY),
            pl.BlockSpec(memory_space=pl.ANY),
        ],
        out_specs=vmem,
        out_shape=jax.ShapeDtypeStruct((CAP, k_local + 2 * blocks), jnp.float32),
        scratch_shapes=[
            pltpu.VMEM((k_local, width), jnp.float32),
            pltpu.VMEM(pivots.shape, jnp.int32),
            pltpu.VMEM((blocks, width), jnp.float32),
            pltpu.SemaphoreType.DMA((4,)),
            pltpu.SemaphoreType.DMA((2,)),
        ],
        compiler_params=pltpu.CompilerParams(vmem_limit_bytes=20 * 2**20),
    )(low.reshape(1), in_hbm(pivots), in_hbm(a_first), in_hbm(prior_lt))


def couple_kernel(weight_ref, lt_ref, after_ref, big_ref, small_ref):
    big_ref[...], small_ref[...] = split(couple_rows(lt_ref[...], weight_ref[...].T))


def coupled_parts(weights, prior_lt, following):
    k_local, width = prior_lt.shape
    depth = k_local // 4
    block = pl.BlockSpec((depth, width), lambda i: (i, 0))
    shape = jax.ShapeDtypeStruct((k_local, width), jnp.bfloat16)
    return pl.pallas_call(
        couple_kernel,
        grid=(4,),
        in_specs=[
            pl.BlockSpec((8, depth), lambda i: (0, i)),
            block,
            pl.BlockSpec(memory_space=pl.ANY),
        ],
        out_specs=(block, block),
        out_shape=(shape, shape),
        compiler_params=pltpu.CompilerParams(vmem_limit_bytes=20 * 2**20),
        cost_estimate=pl.CostEstimate(
            flops=8 * k_local * width, bytes_accessed=8 * k_local * width, transcendentals=0
        ),
    )(weights, in_hbm(prior_lt), following)


def fill_parts(parts_ref, pieces):
    start, total = 0, parts_ref.shape[0] // 2
    for ref in pieces:
        size = ref.shape[0]
        big, small = split(ref[...])
        parts_ref[start : start + size, :] = big
        parts_ref[total + start : total + start + size, :] = small
        start += size


def hits(index, base, total):
    slot = base + lax.broadcasted_iota(jnp.int32, (index.shape[0], total), 1)
    hit = jnp.where(index == slot, 1.0, 0.0).astype(jnp.bfloat16)
    return jnp.concatenate([hit, hit], 1)


def early_kernel(index_ref, *refs):
    *pieces, out_ref, parts_ref = refs
    fill_parts(parts_ref, pieces)
    hit = hits(index_ref[...], 0, parts_ref.shape[0] // 2)
    for low in range(0, out_ref.shape[1], 384):
        out_ref[:, low : low + 384] = jnp.dot(
            hit, parts_ref[:, low : low + 384], preferred_element_type=jnp.float32
        )


def send_kernel(index_ref, weight_ref, carry_ref, lt_big_ref, lt_small_ref, *refs, base):
    *pieces, out_ref, second_ref, entries_ref, big_ref, small_ref, keep_ref, parts_ref = refs
    fill_parts(parts_ref, pieces)
    total = parts_ref.shape[0] // 2
    rows, k_local = out_ref.shape[0], lt_big_ref.shape[0]
    tile_rows = lt_big_ref.shape[1]
    hit = hits(index_ref[...], base, total)
    taken = carry_ref[...] + jnp.dot(hit, parts_ref[...], preferred_element_type=jnp.float32)
    keep_ref[...] = taken[rows + P_SIZE :, :k_local]
    second = taken[rows : rows + P_SIZE]
    entries_ref[...] = second[:, k_local:]
    second = second[:, :k_local]
    second_ref[...] = second
    after = pltpu.roll(second, k_local - 1, 1)
    before = pltpu.roll(second, 1, 1)
    coupled = split(
        weight_ref[0:1, :] * second + weight_ref[1:2, :] * after + weight_ref[2:3, :] * before
    )
    big_ref[...] = coupled[0]
    small_ref[...] = coupled[1]
    first = split(taken[:rows, :k_local])
    out_ref[:, :tile_rows] = dot3(first, (lt_big_ref[...], lt_small_ref[...]), ((1,), (0,)))
    out_ref[:, tile_rows:] = dot3(first, coupled, ((1,), (1,)))


def keep_kernel(taken_ref, lt_big_ref, lt_small_ref, big_ref, small_ref, out_ref):
    tile_rows = lt_big_ref.shape[1]
    first = split(taken_ref[...])
    out_ref[:, :tile_rows] = dot3(first, (lt_big_ref[...], lt_small_ref[...]), ((1,), (0,)))
    out_ref[:, tile_rows:] = dot3(first, (big_ref[...], small_ref[...]), ((1,), (1,)))


def second_kernel(quarter_ref, second_ref, lt_big_ref, lt_small_ref, out_ref, whole_ref):
    blocks = out_ref.shape[0] // 4
    rows = split(second_ref[...])
    whole_ref[...] = dot3(rows, (lt_big_ref[...], lt_small_ref[...]), ((1,), (0,)))
    for i in range(4):
        start = pl.multiple_of(quarter_ref[i] * blocks, blocks)
        out_ref[i * blocks : (i + 1) * blocks, :] = whole_ref[pl.ds(start, blocks), :]


def local_call(kernel, out_shape, flops, *args, scratch=(), smem=0):
    vmem = pl.BlockSpec(memory_space=pltpu.VMEM)
    specs = [pl.BlockSpec(memory_space=pltpu.SMEM)] * smem + [vmem] * (len(args) - smem)
    return pl.pallas_call(
        kernel,
        in_specs=specs,
        out_specs=jax.tree.map(lambda _: vmem, out_shape),
        out_shape=out_shape,
        scratch_shapes=list(scratch),
        compiler_params=pltpu.CompilerParams(vmem_limit_bytes=20 * 2**20),
        cost_estimate=pl.CostEstimate(
            flops=flops, bytes_accessed=4 * sum(x.size for x in args), transcendentals=0
        ),
    )(*args)


def quarter_order(me):
    core, chip = me % 2, me // 2
    return [(1 - chip) * 2 + 1 - core, chip * 2 + 1 - core, (1 - chip) * 2 + core, me]


def in_quarters(rows, quarters, blocks):
    return jnp.concatenate([lax.dynamic_slice_in_dim(rows, q * blocks, blocks) for q in quarters], 0)


def in_vmem(value):
    return pltpu.with_memory_space_constraint(value, pltpu.VMEM)


def add_kernel(keep_ref, got_ref, away_ref, rest_ref):
    half = away_ref.shape[0]
    away_ref[...] = keep_ref[:half, :] + got_ref[:half, :]
    rest_ref[...] = keep_ref[half:, :] + got_ref[half:, :]


def hop_sum(send, keep):
    got = lax.ppermute(send, "narrow", CORE)
    part = jax.ShapeDtypeStruct((keep.shape[0] // 2, keep.shape[1]), keep.dtype)
    away, rest = local_call(add_kernel, (part, part), keep.size, in_vmem(keep), in_vmem(got))
    return rest, lax.ppermute(away, "narrow", CHIP)


def couple_rows(value, weight):
    rows = value.shape[0]
    after = pltpu.roll(value, rows - 1, 0)
    before = pltpu.roll(value, 1, 0)
    return weight[:, 0:1] * value + weight[:, 1:2] * after + weight[:, 2:3] * before


def middle_kernel(
    quarter_ref, weight_ref, a_ref, entries_ref, update_ref, rest_ref, away_ref,
    out_ref, send_ref, keep_ref, turned_ref,
):
    blocks, tile_rows = a_ref.shape
    half = send_ref.shape[0]
    summed = rest_ref[...] + away_ref[...]
    weight = weight_ref[...].T[:blocks]
    w_first = a_ref[...] - summed[:, :tile_rows]
    out_ref[...] = couple_rows(w_first, weight)
    crossed = couple_rows(entries_ref[...].T[:blocks] - summed[:, tile_rows:], weight)
    turned_ref[:, :blocks] = crossed.T
    right = split(w_first)
    for i, ref in enumerate((send_ref, keep_ref)):
        left = [
            turned_ref[pl.ds(pl.multiple_of(quarter_ref[2 * i + j] * blocks, blocks), blocks), :blocks]
            for j in range(2)
        ]
        left = split(jnp.concatenate(left, 0))
        ref[...] = update_ref[i * half : (i + 1) * half, :] + dot3(left, right, ((1,), (0,)))


def last_kernel(weight_ref, a_ref, rest_ref, away_ref, out_ref):
    weight = weight_ref[...].T[: a_ref.shape[0]]
    out_ref[...] = couple_rows(a_ref[...] - (rest_ref[...] + away_ref[...]), weight)


def operator_rows(diag, off, pairs):
    joined = off * pairs.astype(jnp.float32)
    lower = jnp.concatenate([jnp.zeros_like(joined[:1]), joined[:-1]])
    rows = jnp.stack([diag, joined, lower])
    return jnp.pad(rows, ((0, 5), (0, -diag.shape[0] % 128)))


def shards(
    prior_lt, prior_d, prior_e, prior_pairs, pivots, a_first, a_second, inv_d, inv_e, panel_pairs
):
    k_local, tile_rows = prior_lt.shape
    blocks = a_first.shape[0]
    here = lax.axis_index("wide")
    flat = pivots.reshape(-1)
    tile = flat // tile_rows
    count = flat.shape[0]
    order = jnp.arange(count)
    rank = jnp.sum((tile[:, None] == tile[None, :]) & (order[None, :] < order[:, None]), 1)
    block = tile_slots(pivots, here * tile_rows, prior_lt, a_first)
    weights = operator_rows(prior_d, prior_e, prior_pairs)
    early, late, (lt_big, lt_small) = gather_tiles(
        block, lambda held: coupled_parts(weights, prior_lt, held)
    )
    offsets = [o for piece in early + late for o in piece[1]]
    ty, tz, th = tile // (NZ * NH), tile // NH % NZ, tile % NH
    hy, hz, hh = here // (NZ * NH), here // NH % NZ, here % NH
    rel = ((ty - hy) % NY * NZ + (tz - hz) % NZ) * NH + (th - hh) % NH
    place_of = [0] * (NY * NZ * NH)
    for i, (y, z, h) in enumerate(offsets):
        place_of[(y * NZ + z) * NH + h] = i
    place = jnp.sum(
        jnp.where(rel[:, None] == jnp.arange(NY * NZ * NH)[None, :], jnp.array(place_of)[None, :], 0), 1
    )
    where = place * CAP + rank
    quarters = quarter_order(lax.axis_index("narrow"))
    ordered = in_quarters(where[:P_SIZE], quarters, blocks)
    half = P_SIZE // 2
    where = jnp.concatenate([ordered[:half], where[P_SIZE:], ordered[half:]]).reshape(-1, 1)
    early_rows = CAP * sum(len(piece[1]) for piece in early)
    late_rows = CAP * sum(len(piece[1]) for piece in late)
    width = block.shape[1]
    wide = tile_rows + P_SIZE
    f32, b16 = jnp.float32, jnp.bfloat16
    shape = jax.ShapeDtypeStruct
    carry = local_call(
        early_kernel,
        shape((2 * P_SIZE, width), f32),
        4 * 2 * P_SIZE * early_rows * width,
        where,
        *[in_vmem(piece[0]) for piece in early[:4]],
        *[in_hbm(piece[0]) for piece in early[4:]],
        scratch=[pltpu.VMEM((2 * early_rows, width), b16)],
    )
    send, second, entries, second_big, second_small, taken = local_call(
        functools.partial(send_kernel, base=early_rows),
        (
            shape((half, wide), f32),
            shape((P_SIZE, k_local), f32),
            shape((P_SIZE, width - k_local), f32),
            shape((P_SIZE, k_local), b16),
            shape((P_SIZE, k_local), b16),
            shape((half, k_local), f32),
        ),
        8 * P_SIZE * late_rows * width + 6 * half * k_local * wide,
        where,
        weights,
        carry,
        lt_big,
        lt_small,
        *[in_vmem(piece[0]) for piece in late],
        scratch=[pltpu.VMEM((2 * late_rows, width), b16)],
    )
    keep = local_call(
        keep_kernel,
        shape((half, wide), f32),
        6 * half * k_local * wide,
        taken,
        lt_big,
        lt_small,
        second_big,
        second_small,
    )
    rest, away = hop_sum(send, keep)
    update_second = local_call(
        second_kernel,
        shape((P_SIZE, tile_rows), f32),
        6 * P_SIZE * k_local * tile_rows,
        jnp.stack(quarters),
        second,
        lt_big,
        lt_small,
        scratch=[pltpu.VMEM((P_SIZE, tile_rows), f32)],
        smem=1,
    )
    l_first, send, keep = local_call(
        middle_kernel,
        (shape((blocks, tile_rows), f32), shape((half, tile_rows), f32), shape((half, tile_rows), f32)),
        6 * P_SIZE * blocks * tile_rows,
        jnp.stack(quarters),
        operator_rows(inv_d[0], inv_e[0], panel_pairs[0]),
        a_first,
        entries,
        update_second,
        in_vmem(rest),
        in_vmem(away),
        scratch=[pltpu.VMEM((P_SIZE, 128), f32)],
        smem=1,
    )
    rest, away = hop_sum(send, keep)
    l_second = local_call(
        last_kernel,
        shape((blocks, tile_rows), f32),
        8 * blocks * tile_rows,
        operator_rows(inv_d[1], inv_e[1], panel_pairs[1]),
        a_second,
        in_vmem(rest),
        in_vmem(away),
    )
    return (l_first, l_second)


def solution(mesh):
    in_specs = (
        P("narrow", "wide"),
        P("narrow"),
        P("narrow"),
        P("narrow"),
        P(),
        P("narrow", "wide"),
        P("narrow", "wide"),
        P(None, "narrow"),
        P(None, "narrow"),
        P(None, "narrow"),
    )
    out_specs = (P("narrow", "wide"), P("narrow", "wide"))
    return jax.shard_map(shards, mesh=mesh, in_specs=in_specs, out_specs=out_specs, check_vma=False)
```

```python
import functools

import jax
import jax.numpy as jnp
from jax import lax
from jax.experimental import pallas as pl
from jax.experimental.pallas import tpu as pltpu
from jax.sharding import PartitionSpec as P

P_SIZE = 256
CAP = 16
NY, NZ, NH = 4, 8, 2
CORE = [(0, 1), (1, 0), (2, 3), (3, 2)]
CHIP = [(0, 2), (1, 3), (2, 0), (3, 1)]


def shift(dy, dz, dh):
    pairs = []
    for y in range(NY):
        for z in range(NZ):
            for h in range(NH):
                to = ((y + dy) % NY * NZ + (z + dz) % NZ) * NH + (h + dh) % NH
                pairs.append(((y * NZ + z) * NH + h, to))
    return pairs


def moved(block, offsets, step):
    got = lax.ppermute(block, "wide", shift(*step))
    return got, [
        ((y - step[0]) % NY, (z - step[1]) % NZ, (h - step[2]) % NH) for y, z, h in offsets
    ]


def gather_tiles(block, made):
    rows = block.shape[0]
    held, at = block, [(0, 0, 0)]
    got, its = moved(held, at, (0, 4, 0))
    held, at = jnp.concatenate([held, got], 0), at + its
    parts = [moved(held, at, step) for step in ((2, 1, 0), (2, -1, 0), (0, 2, 0))]
    held = jnp.concatenate([held] + [p[0] for p in parts], 0)
    at = at + parts[0][1] + parts[1][1] + parts[2][1]
    half = len(at) // 2
    cut = half * rows
    over = moved(held, at, (0, 0, 1))
    ahead = moved(held, at, (1, 0, 0))
    behind = moved(held, at, (-1, 0, 0))
    up = moved(held[:cut], at[:half], (0, 1, 0))
    down = moved(held[:cut], at[:half], (0, -1, 0))
    early = [(held, at), ahead, behind, over, up, down]
    ready = made(held)
    (middle,) = cuts([(over[0], 0, cut, 0, 0)], [cut])
    late = [
        moved(over[0], over[1], (1, 0, 0)),
        moved(over[0], over[1], (-1, 0, 0)),
        moved(middle, over[1][:half], (0, 1, 0)),
        moved(middle, over[1][:half], (0, -1, 0)),
    ]
    return early, late, ready


def in_hbm(value):
    return pltpu.with_memory_space_constraint(value, pltpu.HBM)


def cuts_kernel(*refs, parts, inputs):
    sems = refs[-1]
    outs = refs[inputs:-1]
    copies = []
    for i, (start, size, out, to) in enumerate(parts):
        copies.append(
            pltpu.make_async_copy(
                refs[i].at[pl.ds(start, size)], outs[out].at[pl.ds(to, size)], sems.at[i]
            )
        )
        copies[-1].start()
    for copy in copies:
        copy.wait()


def cuts(parts, sizes, following=None):
    args = [in_vmem(part[0]) for part in parts] + ([] if following is None else [following])
    width = parts[0][0].shape[1]
    return pl.pallas_call(
        functools.partial(cuts_kernel, parts=[part[1:] for part in parts], inputs=len(args)),
        in_specs=[pl.BlockSpec(memory_space=pl.ANY)] * len(args),
        out_specs=[pl.BlockSpec(memory_space=pltpu.VMEM)] * len(sizes),
        out_shape=[jax.ShapeDtypeStruct((size, width), jnp.float32) for size in sizes],
        scratch_shapes=[pltpu.SemaphoreType.DMA((len(parts),))],
        compiler_params=pltpu.CompilerParams(vmem_limit_bytes=20 * 2**20),
    )(*args)


def split(value):
    big = value.astype(jnp.bfloat16)
    return big, (value - big.astype(jnp.float32)).astype(jnp.bfloat16)


def dot3(left, right, dims):
    def dot(x, y):
        return lax.dot_general(x, y, (dims, ((), ())), preferred_element_type=jnp.float32)

    return dot(left[0], right[0]) + (dot(left[0], right[1]) + dot(left[1], right[0]))


def slots_kernel(low_ref, pivots_hbm, a_hbm, lt_ref, out_ref, lt_buf, pivots_ref, a_ref, sems, more):
    k_local, width = lt_ref.shape
    depth = k_local // sems.shape[0]
    copies = []
    small = [
        pltpu.make_async_copy(pivots_hbm, pivots_ref, more.at[0]),
        pltpu.make_async_copy(a_hbm, a_ref, more.at[1]),
    ]
    for copy in small:
        copy.start()
    for i in range(sems.shape[0]):
        rows = slice(i * depth, (i + 1) * depth)
        copies.append(pltpu.make_async_copy(lt_ref.at[rows], lt_buf.at[rows], sems.at[i]))
        copies[-1].start()
    small[0].wait()
    row = jnp.concatenate([pivots_ref[0:1, :], pivots_ref[1:2, :]], 1) - low_ref[0]
    count = row.shape[1]
    mine = (row >= 0) & (row < width)
    before = lax.broadcasted_iota(jnp.int32, (count, count), 0) < lax.broadcasted_iota(
        jnp.int32, (count, count), 1
    )
    ones = jnp.broadcast_to(jnp.where(mine, 1.0, 0.0), (16, count)).astype(jnp.bfloat16)
    rank = jnp.dot(
        ones, jnp.where(before, 1.0, 0.0).astype(jnp.bfloat16), preferred_element_type=jnp.float32
    )
    slot = lax.broadcasted_iota(jnp.int32, (128, count), 0).astype(jnp.float32)
    hit = (slot == rank[:1]) & mine
    offset = jnp.sum(jnp.where(hit, row + 1, 0).astype(jnp.float32), 1, keepdims=True) - 1.0
    column = lax.broadcasted_iota(jnp.int32, (128, width), 1).astype(jnp.float32)
    pick = jnp.where(column == offset, 1.0, 0.0).astype(jnp.bfloat16)
    across = (((1,), (1,)), ((), ()))

    def rows_of(value):
        total = None
        for _ in range(2):
            part = value.astype(jnp.bfloat16)
            value = value - part.astype(jnp.float32)
            got = lax.dot_general(part, pick, across, preferred_element_type=jnp.float32)
            total = got if total is None else total + got
        return total.T[:CAP]

    small[1].wait()
    extra = rows_of(a_ref[...])
    out_ref[:, k_local:] = jnp.concatenate([extra, jnp.zeros_like(extra)], 1)
    for i, copy in enumerate(copies):
        copy.wait()
        rows = slice(i * depth, (i + 1) * depth)
        out_ref[:, rows] = rows_of(lt_buf[rows, :])


def tile_slots(pivots, low, prior_lt, a_first):
    k_local, width = prior_lt.shape
    blocks = a_first.shape[0]
    vmem = pl.BlockSpec(memory_space=pltpu.VMEM)
    return pl.pallas_call(
        slots_kernel,
        in_specs=[
            pl.BlockSpec(memory_space=pltpu.SMEM),
            pl.BlockSpec(memory_space=pl.ANY),
            pl.BlockSpec(memory_space=pl.ANY),
            pl.BlockSpec(memory_space=pl.ANY),
        ],
        out_specs=vmem,
        out_shape=jax.ShapeDtypeStruct((CAP, k_local + 2 * blocks), jnp.float32),
        scratch_shapes=[
            pltpu.VMEM((k_local, width), jnp.float32),
            pltpu.VMEM(pivots.shape, jnp.int32),
            pltpu.VMEM((blocks, width), jnp.float32),
            pltpu.SemaphoreType.DMA((8,)),
            pltpu.SemaphoreType.DMA((2,)),
        ],
        compiler_params=pltpu.CompilerParams(vmem_limit_bytes=20 * 2**20),
    )(low.reshape(1), in_hbm(pivots), in_hbm(a_first), in_hbm(prior_lt))


def couple_kernel(weight_ref, lt_ref, after_ref, big_ref, small_ref):
    big_ref[...], small_ref[...] = split(couple_rows(lt_ref[...], weight_ref[...].T))


def coupled_parts(weights, prior_lt, following):
    k_local, width = prior_lt.shape
    depth = k_local // 8
    block = pl.BlockSpec((depth, width), lambda i: (i, 0))
    shape = jax.ShapeDtypeStruct((k_local, width), jnp.bfloat16)
    return pl.pallas_call(
        couple_kernel,
        grid=(8,),
        in_specs=[
            pl.BlockSpec((8, depth), lambda i: (0, i)),
            block,
            pl.BlockSpec(memory_space=pl.ANY),
        ],
        out_specs=(block, block),
        out_shape=(shape, shape),
        compiler_params=pltpu.CompilerParams(vmem_limit_bytes=20 * 2**20),
        cost_estimate=pl.CostEstimate(
            flops=8 * k_local * width, bytes_accessed=8 * k_local * width, transcendentals=0
        ),
    )(weights, in_hbm(prior_lt), following)


def fill_parts(parts_ref, pieces):
    start, total = 0, parts_ref.shape[0] // 2
    for ref in pieces:
        size = ref.shape[0]
        big, small = split(ref[...])
        parts_ref[start : start + size, :] = big
        parts_ref[total + start : total + start + size, :] = small
        start += size


def hits(index, base, total):
    slot = base + lax.broadcasted_iota(jnp.int32, (index.shape[0], total), 1)
    hit = jnp.where(index == slot, 1.0, 0.0).astype(jnp.bfloat16)
    return jnp.concatenate([hit, hit], 1)


def early_kernel(index_ref, *refs):
    *pieces, out_ref, parts_ref = refs
    fill_parts(parts_ref, pieces)
    hit = hits(index_ref[...], 0, parts_ref.shape[0] // 2)
    for low in range(0, out_ref.shape[1], 384):
        out_ref[:, low : low + 384] = jnp.dot(
            hit, parts_ref[:, low : low + 384], preferred_element_type=jnp.float32
        )


def send_kernel(index_ref, weight_ref, carry_ref, lt_big_ref, lt_small_ref, *refs, base):
    *pieces, out_ref, second_ref, entries_ref, big_ref, small_ref, keep_ref, parts_ref = refs
    fill_parts(parts_ref, pieces)
    total = parts_ref.shape[0] // 2
    rows, k_local = out_ref.shape[0], lt_big_ref.shape[0]
    tile_rows = lt_big_ref.shape[1]
    hit = hits(index_ref[...], base, total)
    taken = carry_ref[...] + jnp.dot(hit, parts_ref[...], preferred_element_type=jnp.float32)
    keep_ref[...] = taken[rows + P_SIZE :, :k_local]
    second = taken[rows : rows + P_SIZE]
    entries_ref[...] = second[:, k_local:]
    second = second[:, :k_local]
    second_ref[...] = second
    after = pltpu.roll(second, k_local - 1, 1)
    before = pltpu.roll(second, 1, 1)
    coupled = split(
        weight_ref[0:1, :] * second + weight_ref[1:2, :] * after + weight_ref[2:3, :] * before
    )
    big_ref[...] = coupled[0]
    small_ref[...] = coupled[1]
    first = split(taken[:rows, :k_local])
    out_ref[:, :tile_rows] = dot3(first, (lt_big_ref[...], lt_small_ref[...]), ((1,), (0,)))
    out_ref[:, tile_rows:] = dot3(first, coupled, ((1,), (1,)))


def keep_kernel(taken_ref, lt_big_ref, lt_small_ref, big_ref, small_ref, out_ref):
    tile_rows = lt_big_ref.shape[1]
    first = split(taken_ref[...])
    out_ref[:, :tile_rows] = dot3(first, (lt_big_ref[...], lt_small_ref[...]), ((1,), (0,)))
    out_ref[:, tile_rows:] = dot3(first, (big_ref[...], small_ref[...]), ((1,), (1,)))


def second_kernel(quarter_ref, second_ref, lt_big_ref, lt_small_ref, out_ref, whole_ref):
    blocks = out_ref.shape[0] // 4
    rows = split(second_ref[...])
    whole_ref[...] = dot3(rows, (lt_big_ref[...], lt_small_ref[...]), ((1,), (0,)))
    for i in range(4):
        start = pl.multiple_of(quarter_ref[i] * blocks, blocks)
        out_ref[i * blocks : (i + 1) * blocks, :] = whole_ref[pl.ds(start, blocks), :]


def local_call(kernel, out_shape, flops, *args, scratch=(), smem=0):
    vmem = pl.BlockSpec(memory_space=pltpu.VMEM)
    specs = [pl.BlockSpec(memory_space=pltpu.SMEM)] * smem + [vmem] * (len(args) - smem)
    return pl.pallas_call(
        kernel,
        in_specs=specs,
        out_specs=jax.tree.map(lambda _: vmem, out_shape),
        out_shape=out_shape,
        scratch_shapes=list(scratch),
        compiler_params=pltpu.CompilerParams(vmem_limit_bytes=20 * 2**20),
        cost_estimate=pl.CostEstimate(
            flops=flops, bytes_accessed=4 * sum(x.size for x in args), transcendentals=0
        ),
    )(*args)


def quarter_order(me):
    core, chip = me % 2, me // 2
    return [(1 - chip) * 2 + 1 - core, chip * 2 + 1 - core, (1 - chip) * 2 + core, me]


def in_quarters(rows, quarters, blocks):
    return jnp.concatenate([lax.dynamic_slice_in_dim(rows, q * blocks, blocks) for q in quarters], 0)


def in_vmem(value):
    return pltpu.with_memory_space_constraint(value, pltpu.VMEM)


def add_kernel(keep_ref, got_ref, away_ref, rest_ref):
    half = away_ref.shape[0]
    away_ref[...] = keep_ref[:half, :] + got_ref[:half, :]
    rest_ref[...] = keep_ref[half:, :] + got_ref[half:, :]


def hop_sum(send, keep):
    got = lax.ppermute(send, "narrow", CORE)
    part = jax.ShapeDtypeStruct((keep.shape[0] // 2, keep.shape[1]), keep.dtype)
    away, rest = local_call(add_kernel, (part, part), keep.size, in_vmem(keep), in_vmem(got))
    return rest, lax.ppermute(away, "narrow", CHIP)


def couple_rows(value, weight):
    rows = value.shape[0]
    after = pltpu.roll(value, rows - 1, 0)
    before = pltpu.roll(value, 1, 0)
    return weight[:, 0:1] * value + weight[:, 1:2] * after + weight[:, 2:3] * before


def middle_kernel(
    quarter_ref, weight_ref, a_ref, entries_ref, update_ref, rest_ref, away_ref,
    out_ref, send_ref, keep_ref, turned_ref,
):
    blocks, tile_rows = a_ref.shape
    half = send_ref.shape[0]
    summed = rest_ref[...] + away_ref[...]
    weight = weight_ref[...].T[:blocks]
    w_first = a_ref[...] - summed[:, :tile_rows]
    out_ref[...] = couple_rows(w_first, weight)
    crossed = couple_rows(entries_ref[...].T[:blocks] - summed[:, tile_rows:], weight)
    turned_ref[:, :blocks] = crossed.T
    right = split(w_first)
    for i, ref in enumerate((send_ref, keep_ref)):
        left = [
            turned_ref[pl.ds(pl.multiple_of(quarter_ref[2 * i + j] * blocks, blocks), blocks), :blocks]
            for j in range(2)
        ]
        left = split(jnp.concatenate(left, 0))
        ref[...] = update_ref[i * half : (i + 1) * half, :] + dot3(left, right, ((1,), (0,)))


def last_kernel(weight_ref, a_ref, rest_ref, away_ref, out_ref):
    weight = weight_ref[...].T[: a_ref.shape[0]]
    out_ref[...] = couple_rows(a_ref[...] - (rest_ref[...] + away_ref[...]), weight)


def operator_rows(diag, off, pairs):
    joined = off * pairs.astype(jnp.float32)
    lower = jnp.concatenate([jnp.zeros_like(joined[:1]), joined[:-1]])
    rows = jnp.stack([diag, joined, lower])
    return jnp.pad(rows, ((0, 5), (0, -diag.shape[0] % 128)))


def shards(
    prior_lt, prior_d, prior_e, prior_pairs, pivots, a_first, a_second, inv_d, inv_e, panel_pairs
):
    k_local, tile_rows = prior_lt.shape
    blocks = a_first.shape[0]
    here = lax.axis_index("wide")
    flat = pivots.reshape(-1)
    tile = flat // tile_rows
    count = flat.shape[0]
    order = jnp.arange(count)
    rank = jnp.sum((tile[:, None] == tile[None, :]) & (order[None, :] < order[:, None]), 1)
    block = tile_slots(pivots, here * tile_rows, prior_lt, a_first)
    weights = operator_rows(prior_d, prior_e, prior_pairs)
    early, late, (lt_big, lt_small) = gather_tiles(
        block, lambda held: coupled_parts(weights, prior_lt, held)
    )
    offsets = [o for piece in early + late for o in piece[1]]
    ty, tz, th = tile // (NZ * NH), tile // NH % NZ, tile % NH
    hy, hz, hh = here // (NZ * NH), here // NH % NZ, here % NH
    rel = ((ty - hy) % NY * NZ + (tz - hz) % NZ) * NH + (th - hh) % NH
    place_of = [0] * (NY * NZ * NH)
    for i, (y, z, h) in enumerate(offsets):
        place_of[(y * NZ + z) * NH + h] = i
    place = jnp.sum(
        jnp.where(rel[:, None] == jnp.arange(NY * NZ * NH)[None, :], jnp.array(place_of)[None, :], 0), 1
    )
    where = place * CAP + rank
    quarters = quarter_order(lax.axis_index("narrow"))
    ordered = in_quarters(where[:P_SIZE], quarters, blocks)
    half = P_SIZE // 2
    where = jnp.concatenate([ordered[:half], where[P_SIZE:], ordered[half:]]).reshape(-1, 1)
    early_rows = CAP * sum(len(piece[1]) for piece in early)
    late_rows = CAP * sum(len(piece[1]) for piece in late)
    width = block.shape[1]
    wide = tile_rows + P_SIZE
    f32, b16 = jnp.float32, jnp.bfloat16
    shape = jax.ShapeDtypeStruct
    carry = local_call(
        early_kernel,
        shape((2 * P_SIZE, width), f32),
        4 * 2 * P_SIZE * early_rows * width,
        where,
        *[in_vmem(piece[0]) for piece in early[:4]],
        *[in_hbm(piece[0]) for piece in early[4:]],
        scratch=[pltpu.VMEM((2 * early_rows, width), b16)],
    )
    send, second, entries, second_big, second_small, taken = local_call(
        functools.partial(send_kernel, base=early_rows),
        (
            shape((half, wide), f32),
            shape((P_SIZE, k_local), f32),
            shape((P_SIZE, width - k_local), f32),
            shape((P_SIZE, k_local), b16),
            shape((P_SIZE, k_local), b16),
            shape((half, k_local), f32),
        ),
        8 * P_SIZE * late_rows * width + 6 * half * k_local * wide,
        where,
        weights,
        carry,
        lt_big,
        lt_small,
        *[in_vmem(piece[0]) for piece in late],
        scratch=[pltpu.VMEM((2 * late_rows, width), b16)],
    )
    keep = local_call(
        keep_kernel,
        shape((half, wide), f32),
        6 * half * k_local * wide,
        taken,
        lt_big,
        lt_small,
        second_big,
        second_small,
    )
    rest, away = hop_sum(send, keep)
    update_second = local_call(
        second_kernel,
        shape((P_SIZE, tile_rows), f32),
        6 * P_SIZE * k_local * tile_rows,
        jnp.stack(quarters),
        second,
        lt_big,
        lt_small,
        scratch=[pltpu.VMEM((P_SIZE, tile_rows), f32)],
        smem=1,
    )
    l_first, send, keep = local_call(
        middle_kernel,
        (shape((blocks, tile_rows), f32), shape((half, tile_rows), f32), shape((half, tile_rows), f32)),
        6 * P_SIZE * blocks * tile_rows,
        jnp.stack(quarters),
        operator_rows(inv_d[0], inv_e[0], panel_pairs[0]),
        a_first,
        entries,
        update_second,
        in_vmem(rest),
        in_vmem(away),
        scratch=[pltpu.VMEM((P_SIZE, 128), f32)],
        smem=1,
    )
    rest, away = hop_sum(send, keep)
    l_second = local_call(
        last_kernel,
        shape((blocks, tile_rows), f32),
        8 * blocks * tile_rows,
        operator_rows(inv_d[1], inv_e[1], panel_pairs[1]),
        a_second,
        in_vmem(rest),
        in_vmem(away),
    )
    return (l_first, l_second)


def solution(mesh):
    in_specs = (
        P("narrow", "wide"),
        P("narrow"),
        P("narrow"),
        P("narrow"),
        P(),
        P("narrow", "wide"),
        P("narrow", "wide"),
        P(None, "narrow"),
        P(None, "narrow"),
        P(None, "narrow"),
    )
    out_specs = (P("narrow", "wide"), P("narrow", "wide"))
    return jax.shard_map(shards, mesh=mesh, in_specs=in_specs, out_specs=out_specs, check_vma=False)
```

```python
import functools

import jax
import jax.numpy as jnp
from jax import lax
from jax.experimental import pallas as pl
from jax.experimental.pallas import tpu as pltpu
from jax.sharding import PartitionSpec as P

P_SIZE = 256
CAP = 16
NY, NZ, NH = 4, 8, 2
CORE = [(0, 1), (1, 0), (2, 3), (3, 2)]
CHIP = [(0, 2), (1, 3), (2, 0), (3, 1)]


def shift(dy, dz, dh):
    pairs = []
    for y in range(NY):
        for z in range(NZ):
            for h in range(NH):
                to = ((y + dy) % NY * NZ + (z + dz) % NZ) * NH + (h + dh) % NH
                pairs.append(((y * NZ + z) * NH + h, to))
    return pairs


def moved(block, offsets, step):
    got = lax.ppermute(block, "wide", shift(*step))
    return got, [
        ((y - step[0]) % NY, (z - step[1]) % NZ, (h - step[2]) % NH) for y, z, h in offsets
    ]


def gather_tiles(block, made):
    rows = block.shape[0]
    held, at = block, [(0, 0, 0)]
    got, its = moved(held, at, (0, 4, 0))
    held, at = jnp.concatenate([held, got], 0), at + its
    parts = [moved(held, at, step) for step in ((2, 1, 0), (2, -1, 0), (0, 2, 0))]
    held = jnp.concatenate([held] + [p[0] for p in parts], 0)
    at = at + parts[0][1] + parts[1][1] + parts[2][1]
    half = len(at) // 2
    cut = half * rows
    over = moved(held, at, (0, 0, 1))
    ahead = moved(held, at, (1, 0, 0))
    behind = moved(held, at, (-1, 0, 0))
    up = moved(held[:cut], at[:half], (0, 1, 0))
    down = moved(held[:cut], at[:half], (0, -1, 0))
    early = [(held, at), ahead, behind, over, up, down]
    ready = made(held)
    (middle,) = cuts([(over[0], 0, cut, 0, 0)], [cut])
    late = [
        moved(over[0], over[1], (1, 0, 0)),
        moved(over[0], over[1], (-1, 0, 0)),
        moved(middle, over[1][:half], (0, 1, 0)),
        moved(middle, over[1][:half], (0, -1, 0)),
    ]
    return early, late, ready


def in_hbm(value):
    return pltpu.with_memory_space_constraint(value, pltpu.HBM)


def cuts_kernel(*refs, parts, inputs):
    sems = refs[-1]
    outs = refs[inputs:-1]
    copies = []
    for i, (start, size, out, to) in enumerate(parts):
        copies.append(
            pltpu.make_async_copy(
                refs[i].at[pl.ds(start, size)], outs[out].at[pl.ds(to, size)], sems.at[i]
            )
        )
        copies[-1].start()
    for copy in copies:
        copy.wait()


def cuts(parts, sizes, following=None):
    args = [in_vmem(part[0]) for part in parts] + ([] if following is None else [following])
    width = parts[0][0].shape[1]
    return pl.pallas_call(
        functools.partial(cuts_kernel, parts=[part[1:] for part in parts], inputs=len(args)),
        in_specs=[pl.BlockSpec(memory_space=pl.ANY)] * len(args),
        out_specs=[pl.BlockSpec(memory_space=pltpu.VMEM)] * len(sizes),
        out_shape=[jax.ShapeDtypeStruct((size, width), jnp.float32) for size in sizes],
        scratch_shapes=[pltpu.SemaphoreType.DMA((len(parts),))],
        compiler_params=pltpu.CompilerParams(vmem_limit_bytes=20 * 2**20),
    )(*args)


def split(value):
    big = value.astype(jnp.bfloat16)
    return big, (value - big.astype(jnp.float32)).astype(jnp.bfloat16)


def dot3(left, right, dims):
    def dot(x, y):
        return lax.dot_general(x, y, (dims, ((), ())), preferred_element_type=jnp.float32)

    return dot(left[0], right[0]) + (dot(left[0], right[1]) + dot(left[1], right[0]))


def slots_kernel(low_ref, pivots_hbm, a_hbm, lt_ref, out_ref, lt_buf, pivots_ref, a_ref, sems, more):
    k_local, width = lt_ref.shape
    depth = k_local // sems.shape[0]
    copies = []
    small = [
        pltpu.make_async_copy(pivots_hbm, pivots_ref, more.at[0]),
        pltpu.make_async_copy(a_hbm, a_ref, more.at[1]),
    ]
    for copy in small:
        copy.start()
    for i in range(sems.shape[0]):
        rows = slice(i * depth, (i + 1) * depth)
        copies.append(pltpu.make_async_copy(lt_ref.at[rows], lt_buf.at[rows], sems.at[i]))
        copies[-1].start()
    small[0].wait()
    row = jnp.concatenate([pivots_ref[0:1, :], pivots_ref[1:2, :]], 1) - low_ref[0]
    count = row.shape[1]
    mine = (row >= 0) & (row < width)
    before = lax.broadcasted_iota(jnp.int32, (count, count), 0) < lax.broadcasted_iota(
        jnp.int32, (count, count), 1
    )
    ones = jnp.broadcast_to(jnp.where(mine, 1.0, 0.0), (16, count)).astype(jnp.bfloat16)
    rank = jnp.dot(
        ones, jnp.where(before, 1.0, 0.0).astype(jnp.bfloat16), preferred_element_type=jnp.float32
    )
    slot = lax.broadcasted_iota(jnp.int32, (128, count), 0).astype(jnp.float32)
    hit = (slot == rank[:1]) & mine
    offset = jnp.sum(jnp.where(hit, row + 1, 0).astype(jnp.float32), 1, keepdims=True) - 1.0
    column = lax.broadcasted_iota(jnp.int32, (128, width), 1).astype(jnp.float32)
    pick = jnp.where(column == offset, 1.0, 0.0).astype(jnp.bfloat16)
    across = (((1,), (1,)), ((), ()))

    def rows_of(value):
        total = None
        for _ in range(2):
            part = value.astype(jnp.bfloat16)
            value = value - part.astype(jnp.float32)
            got = lax.dot_general(part, pick, across, preferred_element_type=jnp.float32)
            total = got if total is None else total + got
        return total.T[:CAP]

    small[1].wait()
    extra = rows_of(a_ref[...])
    out_ref[:, k_local:] = jnp.concatenate([extra, jnp.zeros_like(extra)], 1)
    for i, copy in enumerate(copies):
        copy.wait()
        rows = slice(i * depth, (i + 1) * depth)
        out_ref[:, rows] = rows_of(lt_buf[rows, :])


def tile_slots(pivots, low, prior_lt, a_first):
    k_local, width = prior_lt.shape
    blocks = a_first.shape[0]
    vmem = pl.BlockSpec(memory_space=pltpu.VMEM)
    return pl.pallas_call(
        slots_kernel,
        in_specs=[
            pl.BlockSpec(memory_space=pltpu.SMEM),
            pl.BlockSpec(memory_space=pl.ANY),
            pl.BlockSpec(memory_space=pl.ANY),
            pl.BlockSpec(memory_space=pl.ANY),
        ],
        out_specs=vmem,
        out_shape=jax.ShapeDtypeStruct((CAP, k_local + 2 * blocks), jnp.float32),
        scratch_shapes=[
            pltpu.VMEM((k_local, width), jnp.float32),
            pltpu.VMEM(pivots.shape, jnp.int32),
            pltpu.VMEM((blocks, width), jnp.float32),
            pltpu.SemaphoreType.DMA((2,)),
            pltpu.SemaphoreType.DMA((2,)),
        ],
        compiler_params=pltpu.CompilerParams(vmem_limit_bytes=20 * 2**20),
    )(low.reshape(1), in_hbm(pivots), in_hbm(a_first), in_hbm(prior_lt))


def couple_kernel(weight_ref, lt_ref, after_ref, big_ref, small_ref):
    big_ref[...], small_ref[...] = split(couple_rows(lt_ref[...], weight_ref[...].T))


def coupled_parts(weights, prior_lt, following):
    k_local, width = prior_lt.shape
    depth = k_local // 2
    block = pl.BlockSpec((depth, width), lambda i: (i, 0))
    shape = jax.ShapeDtypeStruct((k_local, width), jnp.bfloat16)
    return pl.pallas_call(
        couple_kernel,
        grid=(2,),
        in_specs=[
            pl.BlockSpec((8, depth), lambda i: (0, i)),
            block,
            pl.BlockSpec(memory_space=pl.ANY),
        ],
        out_specs=(block, block),
        out_shape=(shape, shape),
        compiler_params=pltpu.CompilerParams(vmem_limit_bytes=20 * 2**20),
        cost_estimate=pl.CostEstimate(
            flops=8 * k_local * width, bytes_accessed=8 * k_local * width, transcendentals=0
        ),
    )(weights, in_hbm(prior_lt), following)


def fill_parts(parts_ref, pieces):
    start, total = 0, parts_ref.shape[0] // 2
    for ref in pieces:
        size = ref.shape[0]
        big, small = split(ref[...])
        parts_ref[start : start + size, :] = big
        parts_ref[total + start : total + start + size, :] = small
        start += size


def hits(index, base, total):
    slot = base + lax.broadcasted_iota(jnp.int32, (index.shape[0], total), 1)
    hit = jnp.where(index == slot, 1.0, 0.0).astype(jnp.bfloat16)
    return jnp.concatenate([hit, hit], 1)


def early_kernel(index_ref, *refs):
    *pieces, out_ref, parts_ref = refs
    fill_parts(parts_ref, pieces)
    hit = hits(index_ref[...], 0, parts_ref.shape[0] // 2)
    for low in range(0, out_ref.shape[1], 384):
        out_ref[:, low : low + 384] = jnp.dot(
            hit, parts_ref[:, low : low + 384], preferred_element_type=jnp.float32
        )


def send_kernel(index_ref, weight_ref, carry_ref, lt_big_ref, lt_small_ref, *refs, base):
    *pieces, out_ref, second_ref, entries_ref, big_ref, small_ref, keep_ref, parts_ref = refs
    fill_parts(parts_ref, pieces)
    total = parts_ref.shape[0] // 2
    rows, k_local = out_ref.shape[0], lt_big_ref.shape[0]
    tile_rows = lt_big_ref.shape[1]
    hit = hits(index_ref[...], base, total)
    taken = carry_ref[...] + jnp.dot(hit, parts_ref[...], preferred_element_type=jnp.float32)
    keep_ref[...] = taken[rows + P_SIZE :, :k_local]
    second = taken[rows : rows + P_SIZE]
    entries_ref[...] = second[:, k_local:]
    second = second[:, :k_local]
    second_ref[...] = second
    after = pltpu.roll(second, k_local - 1, 1)
    before = pltpu.roll(second, 1, 1)
    coupled = split(
        weight_ref[0:1, :] * second + weight_ref[1:2, :] * after + weight_ref[2:3, :] * before
    )
    big_ref[...] = coupled[0]
    small_ref[...] = coupled[1]
    first = split(taken[:rows, :k_local])
    out_ref[:, :tile_rows] = dot3(first, (lt_big_ref[...], lt_small_ref[...]), ((1,), (0,)))
    out_ref[:, tile_rows:] = dot3(first, coupled, ((1,), (1,)))


def keep_kernel(taken_ref, lt_big_ref, lt_small_ref, big_ref, small_ref, out_ref):
    tile_rows = lt_big_ref.shape[1]
    first = split(taken_ref[...])
    out_ref[:, :tile_rows] = dot3(first, (lt_big_ref[...], lt_small_ref[...]), ((1,), (0,)))
    out_ref[:, tile_rows:] = dot3(first, (big_ref[...], small_ref[...]), ((1,), (1,)))


def second_kernel(quarter_ref, second_ref, lt_big_ref, lt_small_ref, out_ref, whole_ref):
    blocks = out_ref.shape[0] // 4
    rows = split(second_ref[...])
    whole_ref[...] = dot3(rows, (lt_big_ref[...], lt_small_ref[...]), ((1,), (0,)))
    for i in range(4):
        start = pl.multiple_of(quarter_ref[i] * blocks, blocks)
        out_ref[i * blocks : (i + 1) * blocks, :] = whole_ref[pl.ds(start, blocks), :]


def local_call(kernel, out_shape, flops, *args, scratch=(), smem=0):
    vmem = pl.BlockSpec(memory_space=pltpu.VMEM)
    specs = [pl.BlockSpec(memory_space=pltpu.SMEM)] * smem + [vmem] * (len(args) - smem)
    return pl.pallas_call(
        kernel,
        in_specs=specs,
        out_specs=jax.tree.map(lambda _: vmem, out_shape),
        out_shape=out_shape,
        scratch_shapes=list(scratch),
        compiler_params=pltpu.CompilerParams(vmem_limit_bytes=20 * 2**20),
        cost_estimate=pl.CostEstimate(
            flops=flops, bytes_accessed=4 * sum(x.size for x in args), transcendentals=0
        ),
    )(*args)


def quarter_order(me):
    core, chip = me % 2, me // 2
    return [(1 - chip) * 2 + 1 - core, chip * 2 + 1 - core, (1 - chip) * 2 + core, me]


def in_quarters(rows, quarters, blocks):
    return jnp.concatenate([lax.dynamic_slice_in_dim(rows, q * blocks, blocks) for q in quarters], 0)


def in_vmem(value):
    return pltpu.with_memory_space_constraint(value, pltpu.VMEM)


def add_kernel(keep_ref, got_ref, away_ref, rest_ref):
    half = away_ref.shape[0]
    away_ref[...] = keep_ref[:half, :] + got_ref[:half, :]
    rest_ref[...] = keep_ref[half:, :] + got_ref[half:, :]


def hop_sum(send, keep):
    got = lax.ppermute(send, "narrow", CORE)
    part = jax.ShapeDtypeStruct((keep.shape[0] // 2, keep.shape[1]), keep.dtype)
    away, rest = local_call(add_kernel, (part, part), keep.size, in_vmem(keep), in_vmem(got))
    return rest, lax.ppermute(away, "narrow", CHIP)


def couple_rows(value, weight):
    rows = value.shape[0]
    after = pltpu.roll(value, rows - 1, 0)
    before = pltpu.roll(value, 1, 0)
    return weight[:, 0:1] * value + weight[:, 1:2] * after + weight[:, 2:3] * before


def middle_kernel(
    quarter_ref, weight_ref, a_ref, entries_ref, update_ref, rest_ref, away_ref,
    out_ref, send_ref, keep_ref, turned_ref,
):
    blocks, tile_rows = a_ref.shape
    half = send_ref.shape[0]
    summed = rest_ref[...] + away_ref[...]
    weight = weight_ref[...].T[:blocks]
    w_first = a_ref[...] - summed[:, :tile_rows]
    out_ref[...] = couple_rows(w_first, weight)
    crossed = couple_rows(entries_ref[...].T[:blocks] - summed[:, tile_rows:], weight)
    turned_ref[:, :blocks] = crossed.T
    right = split(w_first)
    for i, ref in enumerate((send_ref, keep_ref)):
        left = [
            turned_ref[pl.ds(pl.multiple_of(quarter_ref[2 * i + j] * blocks, blocks), blocks), :blocks]
            for j in range(2)
        ]
        left = split(jnp.concatenate(left, 0))
        ref[...] = update_ref[i * half : (i + 1) * half, :] + dot3(left, right, ((1,), (0,)))


def last_kernel(weight_ref, a_ref, rest_ref, away_ref, out_ref):
    weight = weight_ref[...].T[: a_ref.shape[0]]
    out_ref[...] = couple_rows(a_ref[...] - (rest_ref[...] + away_ref[...]), weight)


def operator_rows(diag, off, pairs):
    joined = off * pairs.astype(jnp.float32)
    lower = jnp.concatenate([jnp.zeros_like(joined[:1]), joined[:-1]])
    rows = jnp.stack([diag, joined, lower])
    return jnp.pad(rows, ((0, 5), (0, -diag.shape[0] % 128)))


def shards(
    prior_lt, prior_d, prior_e, prior_pairs, pivots, a_first, a_second, inv_d, inv_e, panel_pairs
):
    k_local, tile_rows = prior_lt.shape
    blocks = a_first.shape[0]
    here = lax.axis_index("wide")
    flat = pivots.reshape(-1)
    tile = flat // tile_rows
    count = flat.shape[0]
    order = jnp.arange(count)
    rank = jnp.sum((tile[:, None] == tile[None, :]) & (order[None, :] < order[:, None]), 1)
    block = tile_slots(pivots, here * tile_rows, prior_lt, a_first)
    weights = operator_rows(prior_d, prior_e, prior_pairs)
    early, late, (lt_big, lt_small) = gather_tiles(
        block, lambda held: coupled_parts(weights, prior_lt, held)
    )
    offsets = [o for piece in early + late for o in piece[1]]
    ty, tz, th = tile // (NZ * NH), tile // NH % NZ, tile % NH
    hy, hz, hh = here // (NZ * NH), here // NH % NZ, here % NH
    rel = ((ty - hy) % NY * NZ + (tz - hz) % NZ) * NH + (th - hh) % NH
    place_of = [0] * (NY * NZ * NH)
    for i, (y, z, h) in enumerate(offsets):
        place_of[(y * NZ + z) * NH + h] = i
    place = jnp.sum(
        jnp.where(rel[:, None] == jnp.arange(NY * NZ * NH)[None, :], jnp.array(place_of)[None, :], 0), 1
    )
    where = place * CAP + rank
    quarters = quarter_order(lax.axis_index("narrow"))
    ordered = in_quarters(where[:P_SIZE], quarters, blocks)
    half = P_SIZE // 2
    where = jnp.concatenate([ordered[:half], where[P_SIZE:], ordered[half:]]).reshape(-1, 1)
    early_rows = CAP * sum(len(piece[1]) for piece in early)
    late_rows = CAP * sum(len(piece[1]) for piece in late)
    width = block.shape[1]
    wide = tile_rows + P_SIZE
    f32, b16 = jnp.float32, jnp.bfloat16
    shape = jax.ShapeDtypeStruct
    carry = local_call(
        early_kernel,
        shape((2 * P_SIZE, width), f32),
        4 * 2 * P_SIZE * early_rows * width,
        where,
        *[in_vmem(piece[0]) for piece in early[:4]],
        *[in_hbm(piece[0]) for piece in early[4:]],
        scratch=[pltpu.VMEM((2 * early_rows, width), b16)],
    )
    send, second, entries, second_big, second_small, taken = local_call(
        functools.partial(send_kernel, base=early_rows),
        (
            shape((half, wide), f32),
            shape((P_SIZE, k_local), f32),
            shape((P_SIZE, width - k_local), f32),
            shape((P_SIZE, k_local), b16),
            shape((P_SIZE, k_local), b16),
            shape((half, k_local), f32),
        ),
        8 * P_SIZE * late_rows * width + 6 * half * k_local * wide,
        where,
        weights,
        carry,
        lt_big,
        lt_small,
        *[in_vmem(piece[0]) for piece in late],
        scratch=[pltpu.VMEM((2 * late_rows, width), b16)],
    )
    keep = local_call(
        keep_kernel,
        shape((half, wide), f32),
        6 * half * k_local * wide,
        taken,
        lt_big,
        lt_small,
        second_big,
        second_small,
    )
    rest, away = hop_sum(send, keep)
    update_second = local_call(
        second_kernel,
        shape((P_SIZE, tile_rows), f32),
        6 * P_SIZE * k_local * tile_rows,
        jnp.stack(quarters),
        second,
        lt_big,
        lt_small,
        scratch=[pltpu.VMEM((P_SIZE, tile_rows), f32)],
        smem=1,
    )
    l_first, send, keep = local_call(
        middle_kernel,
        (shape((blocks, tile_rows), f32), shape((half, tile_rows), f32), shape((half, tile_rows), f32)),
        6 * P_SIZE * blocks * tile_rows,
        jnp.stack(quarters),
        operator_rows(inv_d[0], inv_e[0], panel_pairs[0]),
        a_first,
        entries,
        update_second,
        in_vmem(rest),
        in_vmem(away),
        scratch=[pltpu.VMEM((P_SIZE, 128), f32)],
        smem=1,
    )
    rest, away = hop_sum(send, keep)
    l_second = local_call(
        last_kernel,
        shape((blocks, tile_rows), f32),
        8 * blocks * tile_rows,
        operator_rows(inv_d[1], inv_e[1], panel_pairs[1]),
        a_second,
        in_vmem(rest),
        in_vmem(away),
    )
    return (l_first, l_second)


def solution(mesh):
    in_specs = (
        P("narrow", "wide"),
        P("narrow"),
        P("narrow"),
        P("narrow"),
        P(),
        P("narrow", "wide"),
        P("narrow", "wide"),
        P(None, "narrow"),
        P(None, "narrow"),
        P(None, "narrow"),
    )
    out_specs = (P("narrow", "wide"), P("narrow", "wide"))
    return jax.shard_map(shards, mesh=mesh, in_specs=in_specs, out_specs=out_specs, check_vma=False)
```
